256 devices in a mesh: dp: 32 (over x, z), mp: 8 (over y, core).
Axes of the slice: x: 4, y: 4, z: 8, core: 2. Of those that a mesh axis runs over, the one named last changes fastest.
Arguments:
- activations: bfloat16 [4096, 4096], P('dp', 'mp'), may hold values from -6 to 6
- cotangents: bfloat16 [4096, 16384], P('dp', 'mp'), may hold values from -0.21875 to 0.21875
- owners: int32 [256, 1], P('mp'), may hold values from 0 to 31; in each aligned block of 32 rows (0 to 31, 32 to 63, ...) at most 2 rows name the same one
- stats_left: float32 [8, 32, 2, 512, 512], P('mp', 'dp'), as said below
- stats_right: float32 [8, 32, 2, 512, 512], P('mp', 'dp'), as said below
- variance: float32 [8, 512, 32, 512], P('mp', 'dp'), may hold values from 0.3 to 90, as said below
Outputs:
- direction: bfloat16 [8, 512, 32, 512], P('mp', 'dp')
- new_left: float32 [8, 32, 2, 512, 512], P('mp', 'dp')
- new_right: float32 [8, 32, 2, 512, 512], P('mp', 'dp')
- new_variance: float32 [8, 512, 32, 512], P('mp', 'dp')
The draws below stay inside these ranges and needn't reach their ends.
Inputs may be any that keep to these rules, and one draw needn't show every extreme that they name: `owners`: among the 32 blocks of one index of mp no owner has more than 2 blocks, and some owner has exactly 2. `stats_left`: every slot is a symmetric positive definite matrix. `stats_right`: every slot is a symmetric positive definite matrix. `variance`: every entry is positive.
All inputs are finite; a program needn't handle non-finite values. Where the reference program divides by a largest or mean magnitude, that divisor is 1e-20 or more.
Results may differ from the reference program's by a relative error of at most 0.001.
Values may be sent and summed in bfloat16 or wider, within the bound.
A program may use at most 192 MiB of HBM per device.

```python
import math
import jax
import jax.numpy as jnp
import numpy as np
from jax import lax

BLOCK = 512
ROW_BLOCKS = 8
COL_BLOCKS = 4
TOK_DEV = 128
ITERS = 2
TOKENS = 4096
NB = 32
MOST = 2
N_DP = 32
N_MP = 8


def build_slots(entries, exponent):
    symmetric = (entries + jnp.swapaxes(entries, -1, -2)) * 0.5
    identity = jnp.eye(BLOCK, dtype=jnp.float32)
    scales = jnp.exp(exponent)
    return (identity + symmetric) * scales[..., :, None] * scales[..., None, :]


def draw_stats_left(key, part):
    key = jax.random.fold_in(key, 11)
    noise_key, scale_key = jax.random.split(key)
    array_shape = (N_MP, N_DP, MOST, BLOCK, BLOCK)
    entries = jax.random.uniform(noise_key, array_shape, jnp.float32, -1.0, 1.0) * (0.955 / math.sqrt(BLOCK))
    exponent = jax.random.uniform(scale_key, array_shape[:-1], jnp.float32) * (0.5 * math.log(10.0))
    return build_slots(entries, exponent)


def draw_stats_right(key, part):
    key = jax.random.fold_in(key, 23)
    noise_key, scale_key = jax.random.split(key)
    array_shape = (N_MP, N_DP, MOST, BLOCK, BLOCK)
    entries = jax.random.uniform(noise_key, array_shape, jnp.float32, -1.0, 1.0) * (0.955 / math.sqrt(BLOCK))
    exponent = jax.random.uniform(scale_key, array_shape[:-1], jnp.float32) * (0.5 * math.log(10.0))
    return build_slots(entries, exponent)


def rising_rows(rise):
    position = jnp.arange(BLOCK, dtype=jnp.float32) / (BLOCK - 1.0)
    return jnp.exp(position * math.log(rise))[None, :, None, None]


def draw_variance(key, part):
    key = jax.random.fold_in(key, 37)
    array_shape = (N_MP, BLOCK, NB, BLOCK)
    spread = jax.random.uniform(key, array_shape, jnp.float32, -1.0, 1.0)
    base = jnp.exp(spread * math.log(10.0) * 0.5)
    return base * rising_rows(10.0)


def block_levels(own_key, dims, cuts, smallest, top_value):
    gain = 1.0
    for axis_at, blocks in cuts:
        steps = jax.random.uniform(jax.random.fold_in(jax.random.fold_in(own_key, 6), axis_at), (blocks,), jnp.float32, smallest / len(cuts), top_value / len(cuts))
        gain = gain * jnp.repeat(jnp.exp(steps), dims[axis_at] // blocks).reshape((-1,) + (1,) * (len(dims) - 1 - axis_at))
    return gain


def shared_out(own_key, own, number, rows, number_of, top, most, skew):
    ranking = jax.random.permutation(own_key, number_of)
    heavy_load, common = shares(number_of, rows * top, most, skew, True), shares(number_of, rows * top, most, skew, False)
    places = jnp.arange(number_of)

    def named(tallies, offset_by):
        used = int((tallies > 0).sum())
        fixed = max(1, used // 4)
        passed = fixed + (places - fixed + offset_by * (used - fixed)) % max(1, number_of - fixed)
        return jnp.zeros((number_of,), jnp.int32).at[ranking[jnp.where(places < fixed, places, passed)]].set(jnp.asarray(tallies, jnp.int32))

    tallies = jnp.where(number % 4 == 0, named(heavy_load, number // 4), named(common, number - number // 4 - 1))
    mixed = jax.random.permutation(jax.random.fold_in(own, 3), number_of)
    donor, sink = mixed[0:number_of // 2 * 2:2], mixed[1:number_of // 2 * 2:2]
    margin = jnp.minimum(tallies[donor] - 1, most - tallies[sink]) // 2
    margin = jnp.where((donor == ranking[0]) | (sink == ranking[0]) | (tallies[sink] == 0), 0, jnp.maximum(margin, 0))
    passed = jax.random.randint(jax.random.fold_in(own, 4), (number_of // 2,), 0, 1 << 20) % (margin + 1)
    tallies = tallies.at[donor].add(-passed).at[sink].add(passed)
    members = jnp.searchsorted(jnp.cumsum(tallies), jnp.arange(rows * top), side="right").astype(jnp.int32)
    table = members.reshape(top, rows).T
    table = table[jax.random.permutation(jax.random.fold_in(own, 1), rows)]
    offset_by = jax.random.randint(jax.random.fold_in(own, 2), (rows, 1), 0, top)
    return jnp.take_along_axis(table, (jnp.arange(top)[None, :] + offset_by) % top, axis=1)


def shares(number_of, total, most, skew, full):
    weights = [(1 << 20) // math.isqrt(standing ** skew) + 1 for standing in range(1, number_of + 1)]
    largest = most if full else min(most, max(-(-total // number_of), total * weights[0] // sum(weights)))
    least = 1 if total - largest >= number_of - 1 else 0
    counts, surplus = [largest] + [least] * (number_of - 1), total - largest - least * (number_of - 1)
    while surplus > 0:
        candidates = [i for i in range(1, number_of) if counts[i] < largest] or [i for i in range(1, number_of) if counts[i] < most]
        whole, remaining = sum([weights[i] for i in candidates]), surplus
        for i in candidates:
            more = min(most - counts[i], max(1, remaining * weights[i] // whole), surplus)
            counts[i] = counts[i] + more
            surplus = surplus - more
    return np.array(counts)


def scatter_about(rng, dims, scale, reach, cuts=(), held_as=jnp.bfloat16):
    array = jax.random.normal(rng, dims, jnp.float32) * scale
    if len(cuts) > 0:
        array = block_levels(rng, dims, cuts, -0.22, 0.18) * array
    return jnp.clip(array, min=-reach, max=reach).astype(held_as)


def setup_inputs(seed: int = 0) -> dict:
    arg_keys = jax.random.split(jax.random.key(seed), 7)
    activations = scatter_about(arg_keys[0], (TOKENS, ROW_BLOCKS * BLOCK), 1.0, 6.0, ((0, 32), (1, 8)))
    cotangents = scatter_about(arg_keys[1], (TOKENS, N_MP * COL_BLOCKS * BLOCK), 0.015, 0.21875, ((0, 32), (1, 8)))
    owners_keys = jax.random.split(jax.random.fold_in(arg_keys[2], 1), (N_MP * NB) // NB)
    owners_turns = jax.random.permutation(jax.random.fold_in(arg_keys[2], 3), (N_MP * NB) // NB)
    owners = jax.vmap(lambda own, number: shared_out(jax.random.fold_in(arg_keys[2], 2), own, number, NB, N_DP, 1, MOST, 2))(owners_keys, owners_turns).reshape((N_MP * NB, 1))
    stats_left = draw_stats_left(jax.random.fold_in(arg_keys[6], 71), 0)
    stats_right = draw_stats_right(jax.random.fold_in(arg_keys[6], 71), 0)
    variance = draw_variance(jax.random.fold_in(arg_keys[6], 71), 0)
    return {"activations": activations, "cotangents": cotangents, "owners": owners, "stats_left": stats_left, "stats_right": stats_right, "variance": variance}


def batch_product(left_matrix, right_matrix):
    return jnp.einsum('...ij,...jk->...ik', left_matrix, right_matrix, precision=lax.Precision.HIGHEST)

def slot_numbers(owner_ids):
    count = owner_ids.shape[-1]
    matching = owner_ids[..., :, None] == owner_ids[..., None, :]
    earlier = jnp.arange(count)[None, :] < jnp.arange(count)[:, None]
    return lax.optimization_barrier(jnp.sum(jnp.logical_and(matching, earlier), axis=-1)).astype(jnp.int32)

def inverse_root(statistic):
    order = statistic.shape[-1]
    identity = jnp.eye(order, dtype=jnp.float32)
    bound = lax.optimization_barrier(jnp.max(lax.optimization_barrier(jnp.sum(jnp.abs(statistic), axis=-1)), axis=-1))
    matrix = statistic / bound[..., None, None]
    result = identity
    for iteration in range(ITERS):
        factor = (5.0 * identity - matrix) * 0.25
        result = factor if iteration == 0 else batch_product(result, factor)
        if iteration + 1 < ITERS:
            square = batch_product(factor, factor)
            fourth = batch_product(square, square)
            matrix = batch_product(fourth, matrix)
    return result

def reference(activations, cotangents, owners, stats_left, stats_right, variance):
    owner_table = owners[:, 0].reshape(N_MP, NB)
    slot_table = slot_numbers(owner_table)
    token_groups = activations.reshape(N_DP, TOK_DEV, ROW_BLOCKS * BLOCK)
    cot_groups = cotangents.reshape(N_DP, TOK_DEV, N_MP, COL_BLOCKS * BLOCK).transpose(2, 0, 1, 3)

    def one_group(inputs):
        cot_part, owner_row, slot_row, left_slots, right_slots, var_part = inputs

        def accumulate(total, pair):
            rows_part, cols_part = pair
            partial_term = jnp.dot(rows_part.T, cols_part, preferred_element_type=jnp.float32)
            return (total + partial_term, None)
        start_total = jnp.zeros((ROW_BLOCKS * BLOCK, COL_BLOCKS * BLOCK), jnp.float32)
        gradient, _ = lax.scan(accumulate, start_total, (token_groups, cot_part))
        blocks = gradient.reshape(ROW_BLOCKS, BLOCK, COL_BLOCKS, BLOCK).transpose(0, 2, 1, 3).reshape(NB, BLOCK, BLOCK)
        left_blocks = left_slots[owner_row, slot_row]
        right_blocks = right_slots[owner_row, slot_row]

        def per_block(triple):
            grad_block, left_block, right_block = triple
            left_root = inverse_root(left_block)
            right_root = inverse_root(right_block)
            precond = batch_product(batch_product(left_root, grad_block), right_root)
            outer_left = batch_product(grad_block, grad_block.T)
            outer_right = batch_product(grad_block.T, grad_block)
            return (precond, outer_left, outer_right)
        precond, outer_left, outer_right = lax.map(per_block, (blocks, left_blocks, right_blocks))
        added_left = jnp.zeros_like(left_slots).at[owner_row, slot_row].set(outer_left)
        added_right = jnp.zeros_like(right_slots).at[owner_row, slot_row].set(outer_right)
        left_new = 0.9 * left_slots + 0.1 * added_left
        right_new = 0.9 * right_slots + 0.1 * added_right
        grad_rows = blocks.transpose(1, 0, 2)
        var_new = 0.9 * var_part + 0.1 * grad_rows * grad_rows
        adam_rows = grad_rows / jnp.sqrt(var_new)
        pre_rows = precond.transpose(1, 0, 2)
        mean_adam = lax.optimization_barrier(jnp.mean(adam_rows * adam_rows, axis=(0, 2)))
        mean_pre = lax.optimization_barrier(jnp.mean(pre_rows * pre_rows, axis=(0, 2)))
        ratio = jnp.sqrt(mean_adam / (mean_pre + 1e-06))
        direction = (pre_rows * ratio[None, :, None]).astype(jnp.bfloat16)
        return (direction, left_new, right_new, var_new)
    results = lax.map(one_group, (cot_groups, owner_table, slot_table, stats_left, stats_right, variance))
    return (results[0], results[1], results[2], results[3])
```

```python
import jax
import jax.numpy as jnp
from jax import lax
from jax.sharding import Mesh, PartitionSpec as P

X, Z, Y = 4, 8, 4
HIGH = lax.Precision.HIGH


def product(left, right):
    return jnp.einsum("...ij,...jk->...ik", left, right, precision=HIGH)


def root_of(statistic):
    order = statistic.shape[-1]
    identity = jnp.eye(order, dtype=jnp.float32)
    bound = jnp.max(jnp.sum(jnp.abs(statistic), axis=-1), axis=-1)
    factor = 1.25 * identity - statistic * (0.25 / bound)[..., None, None]
    square = product(factor, factor)
    cubic = product(square, 4.0 * square - 5.0 * factor)
    return 1.25 * factor + 0.25 * product(square, cubic)


def slot_targets(owner_ids, capacity):
    count = owner_ids.shape[-1]
    matching = owner_ids[:, None] == owner_ids[None, :]
    earlier = jnp.arange(count)[None, :] < jnp.arange(count)[:, None]
    slots = jnp.sum(jnp.logical_and(matching, earlier), axis=-1)
    return owner_ids * capacity + slots


def per_device(activations, cotangents, owners, stats_left, stats_right, variance):
    tokens, block = activations.shape
    columns = cotangents.shape[1] // block
    count = owners.shape[0]
    rows = count // columns
    capacity = stats_left.shape[2]
    devices = X * Z
    strip = block // devices

    targets = slot_targets(owners[:, 0], capacity)
    slot_ids = jnp.arange(devices * capacity, dtype=jnp.int32)
    select = targets[:, None] == slot_ids[None, :]

    left_root = root_of(stats_left[0, 0])
    right_root = root_of(stats_right[0, 0])

    cot = cotangents.reshape(tokens, columns, block).transpose(1, 0, 2)
    cot = lax.all_to_all(cot, "x", 0, 0, tiled=True)
    cot = lax.all_gather(cot.reshape(X * tokens, block), "z", axis=0, tiled=True)

    act = activations.T.reshape(X, Z, strip, tokens).transpose(1, 0, 2, 3)
    act = lax.all_to_all(act, "z", 0, 0, tiled=True)
    act = act.reshape(Z, X * strip, tokens)
    act = lax.all_gather(act, ("x", "y", "c"), axis=0, tiled=False)
    act = act.reshape(X, rows, Z, X * strip, tokens)
    cot = cot.reshape(Z, X, tokens, block)
    grad = jnp.einsum("xizrt,zxtc->irc", act, cot, preferred_element_type=jnp.float32)

    grad = grad.reshape(rows, X, strip, block).transpose(1, 0, 2, 3)
    grad = lax.all_to_all(grad, "x", 0, 0, tiled=True)
    grad = grad.transpose(2, 1, 0, 3).reshape(strip, count, block)

    var_new = 0.9 * variance[0] + 0.1 * grad * grad
    sums_adam = jnp.sum(grad * grad / var_new, axis=(0, 2))

    outgoing = jnp.einsum(
        "rbc,bq->qrc", grad, select.astype(jnp.float32), precision=lax.Precision.HIGHEST
    )
    scale = jnp.maximum(jnp.max(jnp.abs(outgoing), axis=-1, keepdims=True), 1e-30)
    coded = outgoing * (32767.0 / scale)
    coded = jnp.round(coded).astype(jnp.int16)
    sums_slot = jnp.sum(jnp.where(select, sums_adam[:, None], 0.0), axis=0)
    extra = jnp.concatenate([scale[:, :, 0], sums_slot[:, None]], axis=1)
    coded = lax.all_to_all(coded, ("x", "z"), 0, 0, tiled=True)
    extra = lax.all_to_all(extra, ("x", "z"), 0, 0, tiled=True)
    coded = coded.reshape(devices, capacity, strip, block).transpose(1, 0, 2, 3)
    extra = extra.reshape(devices, capacity, strip + 1).transpose(1, 0, 2)
    scale = extra[:, :, :strip] * (1.0 / 32767.0)
    owned = coded.astype(jnp.float32) * scale[..., None]
    owned = owned.reshape(capacity, block, block)

    precond = product(product(left_root, owned), right_root)
    mean_adam = jnp.sum(extra[:, :, strip], axis=1) / (block * block)
    mean_pre = jnp.mean(precond * precond, axis=(1, 2))
    ratio = jnp.sqrt(mean_adam / (mean_pre + 1e-6))
    finished = (precond * ratio[:, None, None]).astype(jnp.bfloat16)
    finished = finished.reshape(capacity, devices, strip, block).transpose(1, 0, 2, 3)
    finished = lax.all_to_all(finished, ("x", "z"), 0, 0, tiled=True)
    finished = finished.reshape(devices * capacity, strip, block)
    direction = jnp.einsum("qrc,bq->rbc", finished, select.astype(jnp.bfloat16))

    flipped = jnp.swapaxes(owned, -1, -2)
    left_new = 0.9 * stats_left + 0.1 * product(owned, flipped)[None, None]
    right_new = 0.9 * stats_right + 0.1 * product(flipped, owned)[None, None]
    return (direction[None], left_new, right_new, var_new[None])


def solution(mesh):
    fine = Mesh(mesh.devices.reshape(X, Z, Y, 2), ("x", "z", "y", "c"))
    dp, mp = ("x", "z"), ("y", "c")

    def whole(activations, cotangents, owners, stats_left, stats_right, variance):
        return per_device(activations, cotangents, owners, stats_left, stats_right, variance)

    return jax.shard_map(
        whole,
        mesh=fine,
        in_specs=(
            P(dp, mp),
            P(dp, mp),
            P(mp, None),
            P(mp, dp, None, None, None),
            P(mp, dp, None, None, None),
            P(mp, dp, None, None),
        ),
        out_specs=(
            P(mp, dp, None, None),
            P(mp, dp, None, None, None),
            P(mp, dp, None, None, None),
            P(mp, dp, None, None),
        ),
        check_vma=False,
    )
```

```python
import functools

import jax
import jax.numpy as jnp
from jax import lax
from jax.experimental import pallas as pl
from jax.experimental.pallas import tpu as pltpu
from jax.sharding import Mesh, PartitionSpec as P

X, Z, Y = 4, 8, 4
HIGH = lax.Precision.HIGH
MESH = pl.DeviceIdType.MESH
COEFFICIENTS = (
    25 / 16, -5 / 16 - 3125 / 4096, 3125 / 4096, -1250 / 4096, 250 / 4096, -25 / 4096, 1 / 4096,
)


def halves(value):
    high = value.astype(jnp.bfloat16)
    return high, (value - high.astype(jnp.float32)).astype(jnp.bfloat16)


def dot(left, right):
    return jnp.dot(left, right, preferred_element_type=jnp.float32)


def tiled_product(left_high, left_low, right_high, right_low, order, finish):
    tile = order // 2

    def one(step, carry):
        rows = pl.ds(pl.multiple_of(step * tile, tile), tile)
        high, low = left_high[rows, :], left_low[rows, :]
        total = dot(high, right_low[...]) + dot(low, right_high[...])
        finish(rows, dot(high, right_high[...]) + total)
        return carry

    lax.fori_loop(0, 2, one, 0)


def gather_kernel(
    sizes, act, cot, stats_left, stats_right, strips, roots,
    cbuf, abuf, grad, sbuf, m2, m_h, m_l, m2_h, m2_l, w_h, w_l,
    own_sem, stat_sem, c1_s, c1_r, a1_s, a1_r, zr_s, zr_r, a2_s, a2_r,
    y_s, y_r, sib_s, sib_r, ex_s, ex_r,
):
    nx, nz, ny, block, strip, tokens, rows_i = sizes
    half = nz // 2
    x, z = lax.axis_index("x"), lax.axis_index("z")
    y, c = lax.axis_index("y"), lax.axis_index("c")
    mine = 2 * y + c

    def remote(src, dst, send, recv, **where):
        return pltpu.make_async_remote_copy(
            src_ref=src, dst_ref=dst, send_sem=send, recv_sem=recv,
            device_id=where, device_id_type=MESH,
        )

    loads = [
        pltpu.make_async_copy(ref.at[slot], sbuf.at[2 * side + slot], stat_sem.at[2 * side + slot])
        for side, ref in enumerate((stats_left, stats_right))
        for slot in range(2)
    ]
    own_c = pltpu.make_async_copy(
        cot.at[:, pl.ds(pl.multiple_of(x * block, block), block)], cbuf.at[z, x], own_sem.at[0]
    )
    own_a = pltpu.make_async_copy(act.at[z], abuf.at[z, x, mine], own_sem.at[1])
    own_c.start()
    own_a.start()
    for load in loads:
        load.start()

    barrier = pltpu.get_barrier_semaphore()
    partners = [{"x": lax.rem(x + d, nx)} for d in range(1, nx)]
    partners += [{"z": lax.rem(z + d, nz)} for d in range(1, nz)]
    partners += [{"y": lax.rem(y + d, ny)} for d in range(1, ny)]
    partners += [{"c": 1 - c}]
    for partner in partners:
        pl.semaphore_signal(barrier, inc=1, device_id=partner, device_id_type=MESH)
    pl.semaphore_wait(barrier, len(partners))

    sends = []

    def launch(copy):
        copy.start()
        sends.append(copy)

    def c1(d):
        j = lax.rem(x + d, nx)
        return remote(
            cot.at[:, pl.ds(pl.multiple_of(j * block, block), block)],
            cbuf.at[z, x], c1_s.at[d - 1], c1_r.at[d - 1], x=j,
        )

    def a1(d):
        z2 = lax.rem(z + d, nz)
        return remote(act.at[z2], abuf.at[z, x, mine], a1_s.at[d - 1], a1_r.at[d - 1], z=z2)

    def ring(way, hop, k):
        x2 = lax.rem(x - k + nx, nx)
        step = 1 if way == 0 else nz - 1
        origin = lax.rem(z - hop + nz, nz) if way == 0 else lax.rem(z + hop, nz)
        part = cbuf.at[origin, x2]
        return remote(
            part, part, zr_s.at[way, hop, k], zr_r.at[way, hop, k], z=lax.rem(z + step, nz)
        )

    def a2(d):
        part = abuf.at[:, x, mine]
        return remote(part, part, a2_s.at[d - 1], a2_r.at[d - 1], x=lax.rem(x + d, nx))

    def over_y(k, d):
        part = abuf.at[:, lax.rem(x - k + nx, nx), mine]
        return remote(
            part, part, y_s.at[k, d - 1], y_r.at[k, d - 1], y=lax.rem(y + d, ny)
        )

    def sibling(k, d):
        part = abuf.at[:, lax.rem(x - k + nx, nx), 2 * lax.rem(y - d + ny, ny) + c]
        return remote(part, part, sib_s.at[k, d], sib_r.at[k, d], c=1 - c)

    for d in range(1, nx):
        launch(c1(d))
    own_c.wait()
    for way in range(2):
        launch(ring(way, 0, 0))
    for d in range(1, nz):
        launch(a1(d))
    for k in range(1, nx):
        c1(k).wait_recv()
        for way in range(2):
            launch(ring(way, 0, k))
    own_a.wait()
    for d in range(1, nz):
        a1(d).wait_recv()
    for d in range(1, nx):
        launch(a2(d))
    for d in range(1, ny):
        launch(over_y(0, d))
    launch(sibling(0, 0))
    for load in loads:
        load.wait()

    items = nx * (ny - 1)
    per_step = -(-items // 6)

    def one_matrix(q, carry):
        for t in range(3):
            n = 3 * q + t
            hop, k = n // nx + 1, lax.rem(n, nx)
            ring(0, hop - 1, k).wait_recv()
            ring(1, hop - 1, k).wait_recv()
            inner = hop < half - 1

            @pl.when(jnp.logical_or(inner, k < nx // 2))
            def _():
                ring(0, hop, k).start()

            @pl.when(jnp.logical_or(inner, k >= nx // 2))
            def _():
                ring(1, hop, k).start()

            if t + 1 < nx:

                @pl.when(q == 0)
                def _():
                    a2(t + 1).wait_recv()
                    for d in range(1, ny):
                        over_y(t + 1, d).start()
                    sibling(t + 1, 0).start()

            for extra in range(per_step):
                item = (n - 3) * per_step + extra

                @pl.when(jnp.logical_and(n >= 3, item < items))
                def _():
                    k2, d2 = item // (ny - 1), lax.rem(item, ny - 1) + 1
                    over_y(k2, d2).wait_recv()
                    sibling(k2, d2).start()

            if t == 0:
                stat = sbuf[q]
                bound = jnp.max(jnp.sum(jnp.abs(stat), axis=1, keepdims=True), axis=0, keepdims=True)
                matrix = stat * (1.0 / bound)
                sbuf[q] = matrix
                m_h[...], m_l[...] = halves(matrix)

                def finish(rows, value):
                    m2[rows, :] = value
                    m2_h[rows, :], m2_l[rows, :] = halves(value)
                    w_h[rows, :], w_l[rows, :] = halves(
                        COEFFICIENTS[5] * sbuf[q, rows, :] + COEFFICIENTS[6] * value
                    )

                tiled_product(m_h, m_l, m_h, m_l, block, finish)
            elif t == 1:

                def finish(rows, value):
                    value += COEFFICIENTS[3] * sbuf[q, rows, :] + COEFFICIENTS[4] * m2[rows, :]
                    m_h[rows, :], m_l[rows, :] = halves(value)

                tiled_product(m2_h, m2_l, w_h, w_l, block, finish)
            else:

                def finish(rows, value):
                    value += COEFFICIENTS[1] * sbuf[q, rows, :] + COEFFICIENTS[2] * m2[rows, :]
                    ids = lax.broadcasted_iota(jnp.int32, value.shape, 0) + rows.start
                    columns = lax.broadcasted_iota(jnp.int32, value.shape, 1)
                    roots[q, rows, :] = value + jnp.where(ids == columns, COEFFICIENTS[0], 0.0)

                tiled_product(m2_h, m2_l, m_h, m_l, block, finish)
        return carry

    lax.fori_loop(0, 4, one_matrix, 0)

    for k in range(nx):
        for d in range(ny):
            sibling(k, d).wait_recv()

    def shard(origin, rows=None):
        parts = []
        for x2 in range(nx):
            if rows is None:
                piece = abuf[origin, x2]
            else:
                piece = abuf[origin, x2, :, rows, :]
            parts.append(piece.reshape(-1, tokens))
        left = jnp.concatenate(parts, axis=1)
        return dot(left, cbuf[origin].reshape(nx * tokens, block))

    grad[...] = shard(z).reshape(grad.shape)

    def add(d, carry):
        grad[...] += shard(lax.rem(z + d + (d >= half).astype(jnp.int32), nz)).reshape(grad.shape)
        return carry

    lax.fori_loop(1, nz - 1, add, 0)

    for k in range(nx):
        ring(0 if k < nx // 2 else 1, half - 1, k).wait_recv()
    far = lax.rem(z + half, nz)

    def exchange(d):
        j = lax.rem(x + d, nx)
        rows = pl.ds(pl.multiple_of(j * strip, strip), strip)
        return rows, remote(
            grad.at[:, rows, :], strips.at[x], ex_s.at[d - 1], ex_r.at[d - 1], x=j
        )

    for d in range(1, nx):
        rows, copy = exchange(d)
        grad[:, rows, :] += shard(far, rows).reshape(rows_i, strip, block)
        launch(copy)
    rows = pl.ds(pl.multiple_of(x * strip, strip), strip)
    strips[x] = grad[:, rows, :] + shard(far, rows).reshape(rows_i, strip, block)
    for d in range(1, nx):
        exchange(d)[1].wait_recv()

    for copy in sends:
        copy.wait_send()
    for hop in range(1, half):
        for k in range(nx):
            for way in range(2):
                if hop < half - 1 or (k < nx // 2) == (way == 0):
                    ring(way, hop, k).wait_send()
    for k in range(1, nx):
        for d in range(1, ny):
            over_y(k, d).wait_send()
    for k in range(nx):
        for d in range(ny):
            if (k, d) != (0, 0):
                sibling(k, d).wait_send()


def gather_and_roots(act, cot, stats_left, stats_right):
    nz, rows_z, tokens = act.shape
    nx, ny = lax.axis_size("x"), lax.axis_size("y")
    block = stats_left.shape[-1]
    strip = rows_z // nx
    rows_i = 2 * ny
    sizes = (nx, nz, ny, block, strip, tokens, rows_i)
    half = nz // 2
    bf16, f32 = jnp.bfloat16, jnp.float32
    sem = pltpu.SemaphoreType.DMA
    square = (block, block)
    return pl.pallas_call(
        functools.partial(gather_kernel, sizes),
        out_shape=(
            jax.ShapeDtypeStruct((nx, rows_i, strip, block), f32),
            jax.ShapeDtypeStruct((4, block, block), f32),
        ),
        in_specs=[pl.BlockSpec(memory_space=pl.ANY)] * 4,
        out_specs=(pl.BlockSpec(memory_space=pltpu.VMEM),) * 2,
        scratch_shapes=[
            pltpu.VMEM((nz, nx, tokens, block), bf16),
            pltpu.VMEM((nz, nx, rows_i, rows_z, tokens), bf16),
            pltpu.VMEM((rows_i, rows_z, block), f32),
            pltpu.VMEM((4, block, block), f32),
            pltpu.VMEM(square, f32),
        ]
        + [pltpu.VMEM(square, bf16)] * 6
        + [
            sem((2,)), sem((4,)),
            sem((nx - 1,)), sem((nx - 1,)),
            sem((nz - 1,)), sem((nz - 1,)),
            sem((2, half, nx)), sem((2, half, nx)),
            sem((nx - 1,)), sem((nx - 1,)),
            sem((nx, ny - 1)), sem((nx, ny - 1)),
            sem((nx, ny)), sem((nx, ny)),
            sem((nx - 1,)), sem((nx - 1,)),
        ],
        compiler_params=pltpu.CompilerParams(
            collective_id=0, has_side_effects=True, vmem_limit_bytes=48 * 1024 * 1024
        ),
    )(act, cot, stats_left, stats_right)


def product(left, right):
    return jnp.einsum("...ij,...jk->...ik", left, right, precision=HIGH)


def slot_targets(owner_ids, capacity):
    count = owner_ids.shape[-1]
    matching = owner_ids[:, None] == owner_ids[None, :]
    earlier = jnp.arange(count)[None, :] < jnp.arange(count)[:, None]
    slots = jnp.sum(jnp.logical_and(matching, earlier), axis=-1)
    return owner_ids * capacity + slots


def per_device(activations, cotangents, owners, stats_left, stats_right, variance):
    tokens, block = activations.shape
    count = owners.shape[0]
    capacity = stats_left.shape[2]
    devices = X * Z
    strip = block // devices

    targets = slot_targets(owners[:, 0], capacity)
    slot_ids = jnp.arange(devices * capacity, dtype=jnp.int32)
    select = targets[:, None] == slot_ids[None, :]

    act = activations.T.reshape(X, Z, strip, tokens).transpose(1, 0, 2, 3)
    act = act.reshape(Z, X * strip, tokens)
    grad, roots = gather_and_roots(act, cotangents, stats_left[0, 0], stats_right[0, 0])
    left_root, right_root = roots[:2], roots[2:]
    grad = grad.transpose(2, 1, 0, 3).reshape(strip, count, block)

    var_new = 0.9 * variance[0] + 0.1 * grad * grad
    sums_adam = jnp.sum(grad * grad / var_new, axis=(0, 2))

    outgoing = jnp.einsum(
        "rbc,bq->qrc", grad, select.astype(jnp.float32), precision=lax.Precision.HIGHEST
    )
    scale = jnp.maximum(jnp.max(jnp.abs(outgoing), axis=-1, keepdims=True), 1e-30)
    coded = outgoing * (32767.0 / scale)
    coded = jnp.round(coded).astype(jnp.int16)
    sums_slot = jnp.sum(jnp.where(select, sums_adam[:, None], 0.0), axis=0)
    extra = jnp.concatenate([scale[:, :, 0], sums_slot[:, None]], axis=1)
    coded = lax.all_to_all(coded, ("x", "z"), 0, 0, tiled=True)
    extra = lax.all_to_all(extra, ("x", "z"), 0, 0, tiled=True)
    coded = coded.reshape(devices, capacity, strip, block).transpose(1, 0, 2, 3)
    extra = extra.reshape(devices, capacity, strip + 1).transpose(1, 0, 2)
    scale = extra[:, :, :strip] * (1.0 / 32767.0)
    owned = coded.astype(jnp.float32) * scale[..., None]
    owned = owned.reshape(capacity, block, block)

    precond = product(product(left_root, owned), right_root)
    mean_adam = jnp.sum(extra[:, :, strip], axis=1) / (block * block)
    mean_pre = jnp.mean(precond * precond, axis=(1, 2))
    ratio = jnp.sqrt(mean_adam / (mean_pre + 1e-6))
    finished = (precond * ratio[:, None, None]).astype(jnp.bfloat16)
    finished = finished.reshape(capacity, devices, strip, block).transpose(1, 0, 2, 3)
    finished = lax.all_to_all(finished, ("x", "z"), 0, 0, tiled=True)
    finished = finished.reshape(devices * capacity, strip, block)
    direction = jnp.einsum("qrc,bq->rbc", finished, select.astype(jnp.bfloat16))

    flipped = jnp.swapaxes(owned, -1, -2)
    left_new = 0.9 * stats_left + 0.1 * product(owned, flipped)[None, None]
    right_new = 0.9 * stats_right + 0.1 * product(flipped, owned)[None, None]
    return (direction[None], left_new, right_new, var_new[None])


def solution(mesh):
    fine = Mesh(mesh.devices.reshape(X, Z, Y, 2), ("x", "z", "y", "c"))
    dp, mp = ("x", "z"), ("y", "c")

    def whole(activations, cotangents, owners, stats_left, stats_right, variance):
        return per_device(activations, cotangents, owners, stats_left, stats_right, variance)

    return jax.shard_map(
        whole,
        mesh=fine,
        in_specs=(
            P(dp, mp),
            P(dp, mp),
            P(mp, None),
            P(mp, dp, None, None, None),
            P(mp, dp, None, None, None),
            P(mp, dp, None, None),
        ),
        out_specs=(
            P(mp, dp, None, None),
            P(mp, dp, None, None, None),
            P(mp, dp, None, None, None),
            P(mp, dp, None, None),
        ),
        check_vma=False,
    )
```

```python
import functools

import jax
import jax.numpy as jnp
from jax import lax
from jax.experimental import pallas as pl
from jax.experimental.pallas import tpu as pltpu
from jax.sharding import Mesh, PartitionSpec as P

X, Z, Y = 4, 8, 4
MESH = pl.DeviceIdType.MESH
COEFFICIENTS = (
    25 / 16, -5 / 16 - 3125 / 4096, 3125 / 4096, -1250 / 4096, 250 / 4096, -25 / 4096, 1 / 4096,
)


def halves(value):
    high = value.astype(jnp.bfloat16)
    return high, (value - high.astype(jnp.float32)).astype(jnp.bfloat16)


def dot(left, right):
    return jnp.dot(left, right, preferred_element_type=jnp.float32)


def tiled_product(left_high, left_low, right_high, right_low, order, finish):
    tile = order // 2

    def one(step, carry):
        rows = pl.ds(pl.multiple_of(step * tile, tile), tile)
        high, low = left_high[rows, :], left_low[rows, :]
        total = dot(high, right_low[...]) + dot(low, right_high[...])
        finish(rows, dot(high, right_high[...]) + total)
        return carry

    lax.fori_loop(0, 2, one, 0)


def step_kernel(
    sizes, act, cot, stats_left, stats_right, variance, source, targets, used,
    direction, left_new, right_new, var_new,
    cbuf, abuf, grad, sbuf, vbuf, vt, matrix, m2, m_h, m_l, m2_h, m2_l, w_h, w_l, root_h, root_l,
    gsend, gsend_row, gq, gq_row, scale_rows, adam_rows, send_q, send_row, rq, rq_row,
    owned_h, owned_l, pre, finished, ret,
    own_sem, stat_sem, out_sem, var_sem, c1_s, c1_r, a1_s, a1_r, zr_s, zr_r, a2_s, a2_r,
    y_s, y_r, sib_s, sib_r, ex_s, ex_r, exr_s, exr_r, go_s, go_r, gor_s, gor_r, back_s, back_r,
):
    nx, nz, ny, block, strip, tokens, rows_i = sizes
    count, devices, width = rows_i * nx, nx * nz, rows_i * strip
    lane = vbuf.shape[2]
    half = nz // 2
    x, z = lax.axis_index("x"), lax.axis_index("z")
    y, c = lax.axis_index("y"), lax.axis_index("c")
    mine = 2 * y + c
    me = x * nz + z

    def remote(src, dst, send, recv, **where):
        return pltpu.make_async_remote_copy(
            src_ref=src, dst_ref=dst, send_sem=send, recv_sem=recv,
            device_id=where, device_id_type=MESH,
        )

    loads = [
        pltpu.make_async_copy(ref.at[slot], sbuf.at[2 * side + slot], stat_sem.at[2 * side + slot])
        for side, ref in enumerate((stats_left, stats_right))
        for slot in range(2)
    ]
    own_c = pltpu.make_async_copy(
        cot.at[:, pl.ds(pl.multiple_of(x * block, block), block)], cbuf.at[z, x], own_sem.at[0]
    )
    own_a = pltpu.make_async_copy(act.at[z], abuf.at[z, x, mine], own_sem.at[1])
    loads += [
        pltpu.make_async_copy(
            variance.at[:, k * lane : (k + 1) * lane], vbuf.at[k], var_sem.at[0, k]
        )
        for k in range(block // lane)
    ]
    own_c.start()
    own_a.start()
    for load in loads:
        load.start()

    barrier = pltpu.get_barrier_semaphore()

    def plane(d):
        return lax.rem(x + d // nz, nx), lax.rem(z + lax.rem(d, nz), nz)

    def greet(d, carry):
        x2, z2 = plane(d)
        pl.semaphore_signal(barrier, inc=1, device_id={"x": x2, "z": z2}, device_id_type=MESH)
        return carry

    lax.fori_loop(1, devices, greet, 0)
    partners = [{"y": lax.rem(y + d, ny)} for d in range(1, ny)]
    partners += [{"c": 1 - c}]
    for partner in partners:
        pl.semaphore_signal(barrier, inc=1, device_id=partner, device_id_type=MESH)
    pl.semaphore_wait(barrier, len(partners) + devices - 1)

    sends = []

    def launch(copy):
        copy.start()
        sends.append(copy)

    def c1(d):
        j = lax.rem(x + d, nx)
        return remote(
            cot.at[:, pl.ds(pl.multiple_of(j * block, block), block)],
            cbuf.at[z, x], c1_s.at[d - 1], c1_r.at[d - 1], x=j,
        )

    def a1(d):
        z2 = lax.rem(z + d, nz)
        return remote(act.at[z2], abuf.at[z, x, mine], a1_s.at[d - 1], a1_r.at[d - 1], z=z2)

    def ring(way, hop, k):
        x2 = lax.rem(x - k + nx, nx)
        step = 1 if way == 0 else nz - 1
        origin = lax.rem(z - hop + nz, nz) if way == 0 else lax.rem(z + hop, nz)
        part = cbuf.at[origin, x2]
        return remote(
            part, part, zr_s.at[way, hop, k], zr_r.at[way, hop, k], z=lax.rem(z + step, nz)
        )

    def a2(d):
        part = abuf.at[:, x, mine]
        return remote(part, part, a2_s.at[d - 1], a2_r.at[d - 1], x=lax.rem(x + d, nx))

    def over_y(k, d):
        part = abuf.at[:, lax.rem(x - k + nx, nx), mine]
        return remote(
            part, part, y_s.at[k, d - 1], y_r.at[k, d - 1], y=lax.rem(y + d, ny)
        )

    def sibling(k, d):
        part = abuf.at[:, lax.rem(x - k + nx, nx), 2 * lax.rem(y - d + ny, ny) + c]
        return remote(part, part, sib_s.at[k, d], sib_r.at[k, d], c=1 - c)

    for d in range(1, nx):
        launch(c1(d))
    own_c.wait()
    for way in range(2):
        launch(ring(way, 0, 0))
    for d in range(1, nz):
        launch(a1(d))
    for k in range(1, nx):
        c1(k).wait_recv()
        for way in range(2):
            launch(ring(way, 0, k))
    own_a.wait()
    for d in range(1, nz):
        a1(d).wait_recv()
    for d in range(1, nx):
        launch(a2(d))
    for d in range(1, ny):
        launch(over_y(0, d))
    launch(sibling(0, 0))
    for load in loads:
        load.wait()

    items = nx * (ny - 1)
    per_step = -(-items // 6)

    def one_matrix(q, carry):
        for t in range(3):
            n = 3 * q + t
            hop, k = n // nx + 1, lax.rem(n, nx)
            ring(0, hop - 1, k).wait_recv()
            ring(1, hop - 1, k).wait_recv()
            inner = hop < half - 1

            @pl.when(jnp.logical_or(inner, k < nx // 2))
            def _():
                ring(0, hop, k).start()

            @pl.when(jnp.logical_or(inner, k >= nx // 2))
            def _():
                ring(1, hop, k).start()

            if t + 1 < nx:

                @pl.when(q == 0)
                def _():
                    a2(t + 1).wait_recv()
                    for d in range(1, ny):
                        over_y(t + 1, d).start()
                    sibling(t + 1, 0).start()

            for extra in range(per_step):
                item = (n - 3) * per_step + extra

                @pl.when(jnp.logical_and(n >= 3, item < items))
                def _():
                    k2, d2 = item // (ny - 1), lax.rem(item, ny - 1) + 1
                    over_y(k2, d2).wait_recv()
                    sibling(k2, d2).start()

            if t == 0:
                stat = sbuf[q]
                bound = jnp.max(jnp.sum(jnp.abs(stat), axis=1, keepdims=True), axis=0, keepdims=True)
                value = stat * (1.0 / bound)
                matrix[...] = value
                m_h[...], m_l[...] = halves(value)

                def finish(rows, value):
                    m2[rows, :] = value
                    m2_h[rows, :], m2_l[rows, :] = halves(value)
                    w_h[rows, :], w_l[rows, :] = halves(
                        COEFFICIENTS[5] * matrix[rows, :] + COEFFICIENTS[6] * value
                    )

                tiled_product(m_h, m_l, m_h, m_l, block, finish)
            elif t == 1:

                def finish(rows, value):
                    value += COEFFICIENTS[3] * matrix[rows, :] + COEFFICIENTS[4] * m2[rows, :]
                    m_h[rows, :], m_l[rows, :] = halves(value)

                tiled_product(m2_h, m2_l, w_h, w_l, block, finish)
            else:

                def finish(rows, value):
                    value += COEFFICIENTS[1] * matrix[rows, :] + COEFFICIENTS[2] * m2[rows, :]
                    ids = lax.broadcasted_iota(jnp.int32, value.shape, 0) + rows.start
                    columns = lax.broadcasted_iota(jnp.int32, value.shape, 1)
                    value += jnp.where(ids == columns, COEFFICIENTS[0], 0.0)
                    root_h[q, rows, :], root_l[q, rows, :] = halves(value)

                tiled_product(m2_h, m2_l, m_h, m_l, block, finish)

            each = -(-count // 12)
            for extra in range(each):
                b = n * each + extra

                @pl.when(b < count)
                def _():
                    rows = pl.ds(pl.multiple_of(b * strip, strip), strip)
                    for k in range(block // lane):
                        vt[k, rows, :] = vbuf[k, pl.ds(b, strip, stride=count), :]
        return carry

    lax.fori_loop(0, 4, one_matrix, 0)

    for k in range(nx):
        for d in range(ny):
            sibling(k, d).wait_recv()

    def shard(origin, rows=None):
        parts = []
        for x2 in range(nx):
            if rows is None:
                piece = abuf[origin, x2]
            else:
                piece = abuf[origin, x2, :, rows, :]
            parts.append(piece.reshape(-1, tokens))
        left = jnp.concatenate(parts, axis=1)
        return dot(left, cbuf[origin].reshape(nx * tokens, block))

    grad[...] = shard(z).reshape(grad.shape)

    def add(d, carry):
        grad[...] += shard(lax.rem(z + d + (d >= half).astype(jnp.int32), nz)).reshape(grad.shape)
        return carry

    lax.fori_loop(1, nz - 1, add, 0)

    for k in range(nx):
        ring(0 if k < nx // 2 else 1, half - 1, k).wait_recv()
    far = lax.rem(z + half, nz)

    def exchange(d):
        j = lax.rem(x + d, nx)
        return (
            remote(gsend.at[j], gq.at[x], ex_s.at[d - 1], ex_r.at[d - 1], x=j),
            remote(gsend_row.at[j], gq_row.at[x], exr_s.at[d - 1], exr_r.at[d - 1], x=j),
        )

    diagonal = lax.broadcasted_iota(jnp.int32, (width, width), 0) == lax.broadcasted_iota(
        jnp.int32, (width, width), 1
    )
    for d in list(range(1, nx)) + [0]:
        j = lax.rem(x + d, nx)
        rows = pl.ds(pl.multiple_of(j * strip, strip), strip)
        value = grad[:, rows, :].reshape(width, block) + shard(far, rows)
        top = jnp.maximum(jnp.max(jnp.abs(value), axis=1, keepdims=True), 1e-30)
        coded = jnp.round(value * (32767.0 / top)).astype(jnp.int32).astype(jnp.int16)
        row = jnp.sum(jnp.where(diagonal, top * (1.0 / 32767.0), 0.0), axis=0, keepdims=True)
        if d:
            gsend[j] = coded.reshape(rows_i, strip, block)
            gsend_row[j] = row
            for copy in exchange(d):
                launch(copy)
        else:
            gq[x] = coded.reshape(rows_i, strip, block)
            gq_row[x] = row

    lanes = lax.broadcasted_iota(jnp.int32, (1, width), 1)

    def strips_of(j):
        row = gq_row[j]
        column = jnp.sum(jnp.where(diagonal, row, 0.0), axis=1, keepdims=True)
        for i in range(rows_i):
            b = i * nx + j
            value = gq[j, i].astype(jnp.float32) * column[i * strip : (i + 1) * strip]
            square = value * value
            rows = pl.ds(pl.multiple_of(b * strip, strip), strip)
            old = jnp.concatenate([vt[k, rows, :] for k in range(block // lane)], axis=1)
            fresh = 0.9 * old + 0.1 * square
            for k in range(block // lane):
                vt[k, rows, :] = fresh[:, k * lane : (k + 1) * lane]
            total = jnp.sum(square / fresh, axis=0, keepdims=True)
            adam_rows[pl.ds(b, 1), :] = sum(
                total[:, k * width : (k + 1) * width] for k in range(block // width)
            )
            inside = jnp.logical_and(lanes >= i * strip, lanes < (i + 1) * strip)
            scale_rows[pl.ds(b, 1), :] = jnp.where(inside, row, 0.0)

    strips_of(x)
    for d in range(1, nx):
        for copy in exchange(d):
            copy.wait_recv()
        strips_of(lax.rem(x - d + nx, nx))

    def go(slot, d):
        x2, z2 = plane(d)
        other = x2 * nz + z2
        return (
            remote(send_q.at[slot, other], rq.at[slot, me],
                   go_s.at[slot, d - 1], go_r.at[slot, d - 1], x=x2, z=z2),
            remote(send_row.at[slot, other], rq_row.at[slot, me],
                   gor_s.at[slot, d - 1], gor_r.at[slot, d - 1], x=x2, z=z2),
        )

    def picked(slot, other):
        b = source[2 * other + slot]
        rows = jnp.concatenate([scale_rows[pl.ds(b, 1), :], adam_rows[pl.ds(b, 1), :]], axis=0)
        return gq[lax.rem(b, nx), b // nx], rows

    for slot in range(2):

        def send(d, carry):
            x2, z2 = plane(d)
            other = x2 * nz + z2
            send_q[slot, other], send_row[slot, other] = picked(slot, other)
            for copy in go(slot, d):
                copy.start()
            return carry

        lax.fori_loop(1, devices, send, 0)
        rq[slot, me], rq_row[slot, me] = picked(slot, me)

    def reorder(r, carry):
        rows = pl.ds(pl.multiple_of(r * count, count), count)
        for k in range(block // lane):
            vbuf[k, rows, :] = vt[k, pl.ds(r, count, stride=strip), :]
        return carry

    lax.fori_loop(0, strip, reorder, 0)
    outs = [
        pltpu.make_async_copy(
            vbuf.at[k], var_new.at[:, k * lane : (k + 1) * lane], var_sem.at[1, k]
        )
        for k in range(block // lane)
    ]
    for copy in outs:
        copy.start()

    def arrival(d):
        return lax.rem(x - d // nz + nx, nx) * nz + lax.rem(z - lax.rem(d, nz) + nz, nz)

    def back(slot, d):
        x2, z2 = plane(d)
        other = x2 * nz + z2
        rows = pl.ds(pl.multiple_of(other * strip, strip), strip)
        return remote(
            finished.at[slot, rows, :], ret.at[2 * me + slot],
            back_s.at[slot, d - 1], back_r.at[slot, d - 1], x=x2, z=z2,
        )

    fits = lax.rem(lax.broadcasted_iota(jnp.int32, (strip, width), 1), strip) == (
        lax.broadcasted_iota(jnp.int32, (strip, width), 0)
    )
    for slot in range(2):
        keep = used[slot]

        def decode(p, total):
            extra = rq_row[slot, p]
            column = jnp.sum(jnp.where(fits, extra[0:1], 0.0), axis=1, keepdims=True) * keep
            value = rq[slot, p].astype(jnp.float32) * column
            rows = pl.ds(pl.multiple_of(p * strip, strip), strip)
            owned_h[slot, rows, :], owned_l[slot, rows, :] = halves(value)
            return total + extra[1:2]

        def receive(d, total):
            for copy in go(slot, d):
                copy.wait_recv()
            return decode(arrival(d), total)

        total = decode(me, jnp.zeros((1, width), jnp.float32))
        total = lax.fori_loop(1, devices, receive, total)

        def finish(rows, value):
            m_h[rows, :], m_l[rows, :] = halves(value)

        tiled_product(
            root_h.at[slot], root_l.at[slot], owned_h.at[slot], owned_l.at[slot], block, finish
        )

        def finish(rows, value):
            pre[rows, :] = value

        tiled_product(m_h, m_l, root_h.at[2 + slot], root_l.at[2 + slot], block, finish)
        value = pre[...]
        squares = jnp.sum(jnp.sum(value * value, axis=0, keepdims=True), axis=1, keepdims=True)
        mean_adam = jnp.sum(total, axis=1, keepdims=True) * (1.0 / (block * block))
        ratio = jnp.sqrt(mean_adam / (squares * (1.0 / (block * block)) + 1e-6))
        finished[slot] = (value * ratio).astype(jnp.bfloat16)

        def send_back(d, carry):
            back(slot, d).start()
            return carry

        lax.fori_loop(1, devices, send_back, 0)
        rows = pl.ds(pl.multiple_of(me * strip, strip), strip)
        ret[2 * me + slot] = finished[slot, rows, :]

    tile = block // 2
    for slot in range(2):

        def outer(step, carry):
            rows = pl.ds(pl.multiple_of(step * tile, tile), tile)

            def pair(dims, left_high, left_low):
                def one(left, right):
                    return lax.dot_general(
                        left, right, (dims, ((), ())), preferred_element_type=jnp.float32
                    )

                total = one(left_high, owned_l[slot]) + one(left_low, owned_h[slot])
                return one(left_high, owned_h[slot]) + total

            left = pair(((1,), (1,)), owned_h[slot, rows, :], owned_l[slot, rows, :])
            sbuf[slot, rows, :] = 0.9 * sbuf[slot, rows, :] + 0.1 * left
            right = pair(((0,), (0,)), owned_h[slot, :, rows], owned_l[slot, :, rows])
            sbuf[2 + slot, rows, :] = 0.9 * sbuf[2 + slot, rows, :] + 0.1 * right
            return carry

        lax.fori_loop(0, 2, outer, 0)
        outs.append(pltpu.make_async_copy(sbuf.at[slot], left_new.at[slot], out_sem.at[slot]))
        outs.append(
            pltpu.make_async_copy(sbuf.at[2 + slot], right_new.at[slot], out_sem.at[2 + slot])
        )
        for copy in outs[-2:]:
            copy.start()

    for slot in range(2):

        def collect(d, carry):
            back(slot, d).wait_recv()
            return carry

        lax.fori_loop(1, devices, collect, 0)

    def choose(b, carry):
        direction[b] = ret[targets[b]]
        return carry

    lax.fori_loop(0, count, choose, 0)

    for copy in outs:
        copy.wait()
    for slot in range(2):

        def drain(d, carry):
            for copy in go(slot, d):
                copy.wait_send()
            back(slot, d).wait_send()
            return carry

        lax.fori_loop(1, devices, drain, 0)
    for copy in sends:
        copy.wait_send()
    for hop in range(1, half):
        for k in range(nx):
            for way in range(2):
                if hop < half - 1 or (k < nx // 2) == (way == 0):
                    ring(way, hop, k).wait_send()
    for k in range(1, nx):
        for d in range(1, ny):
            over_y(k, d).wait_send()
    for k in range(nx):
        for d in range(ny):
            if (k, d) != (0, 0):
                sibling(k, d).wait_send()


def shampoo(act, cot, stats_left, stats_right, variance, source, targets, used):
    nz, rows_z, tokens = act.shape
    nx, ny = lax.axis_size("x"), lax.axis_size("y")
    block = stats_left.shape[-1]
    strip = rows_z // nx
    rows_i = 2 * ny
    sizes = (nx, nz, ny, block, strip, tokens, rows_i)
    half = nz // 2
    count, devices, width = rows_i * nx, nx * nz, rows_i * strip
    lane = min(block, 128)
    bf16, f32, i16 = jnp.bfloat16, jnp.float32, jnp.int16
    sem, vmem = pltpu.SemaphoreType.DMA, pltpu.VMEM
    square = (block, block)
    anywhere = pl.BlockSpec(memory_space=pl.ANY)
    scalars = pl.BlockSpec(memory_space=pltpu.SMEM)
    return pl.pallas_call(
        functools.partial(step_kernel, sizes),
        out_shape=(
            jax.ShapeDtypeStruct((count, strip, block), bf16),
            jax.ShapeDtypeStruct(stats_left.shape, f32),
            jax.ShapeDtypeStruct(stats_right.shape, f32),
            jax.ShapeDtypeStruct(variance.shape, f32),
        ),
        in_specs=[anywhere] * 5 + [scalars] * 3,
        out_specs=(pl.BlockSpec(memory_space=pltpu.VMEM),) + (anywhere,) * 3,
        scratch_shapes=[
            vmem((nz, nx, tokens, block), bf16),
            vmem((nz, nx, rows_i, rows_z, tokens), bf16),
            vmem((rows_i, rows_z, block), f32),
            vmem((4, block, block), f32),
            vmem((block // lane, strip * count, lane), f32),
            vmem((block // lane, strip * count, lane), f32),
            vmem(square, f32),
            vmem(square, f32),
        ]
        + [vmem(square, bf16)] * 6
        + [
            vmem((4, block, block), bf16),
            vmem((4, block, block), bf16),
            vmem((nx, rows_i, strip, block), i16),
            vmem((nx, 1, width), f32),
            vmem((nx, rows_i, strip, block), i16),
            vmem((nx, 1, width), f32),
            vmem((count, width), f32),
            vmem((count, width), f32),
            vmem((2, devices, strip, block), i16),
            vmem((2, devices, 2, width), f32),
            vmem((2, devices, strip, block), i16),
            vmem((2, devices, 2, width), f32),
            vmem((2, block, block), bf16),
            vmem((2, block, block), bf16),
            vmem(square, f32),
            vmem((2, block, block), bf16),
            vmem((2 * devices, strip, block), bf16),
            sem((2,)), sem((4,)), sem((4,)), sem((2, block // lane)),
            sem((nx - 1,)), sem((nx - 1,)),
            sem((nz - 1,)), sem((nz - 1,)),
            sem((2, half, nx)), sem((2, half, nx)),
            sem((nx - 1,)), sem((nx - 1,)),
            sem((nx, max(1, ny - 1))), sem((nx, max(1, ny - 1))),
            sem((nx, ny)), sem((nx, ny)),
        ]
        + [sem((nx - 1,))] * 4
        + [sem((2, devices - 1))] * 6,
        compiler_params=pltpu.CompilerParams(
            collective_id=0, has_side_effects=True, vmem_limit_bytes=60 * 1024 * 1024
        ),
    )(act, cot, stats_left, stats_right, variance, source, targets, used)


def slot_targets(owner_ids, capacity):
    count = owner_ids.shape[-1]
    matching = owner_ids[:, None] == owner_ids[None, :]
    earlier = jnp.arange(count)[None, :] < jnp.arange(count)[:, None]
    slots = jnp.sum(jnp.logical_and(matching, earlier), axis=-1)
    return owner_ids * capacity + slots


def per_device(activations, cotangents, owners, stats_left, stats_right, variance):
    tokens, block = activations.shape
    count = owners.shape[0]
    capacity = stats_left.shape[2]
    devices = lax.axis_size("x") * lax.axis_size("z")
    strip = block // devices

    targets = slot_targets(owners[:, 0], capacity)
    slot_ids = jnp.arange(devices * capacity, dtype=jnp.int32)
    select = targets[:, None] == slot_ids[None, :]
    blocks = jnp.arange(count, dtype=jnp.int32)
    source = jnp.sum(jnp.where(select, blocks[:, None], 0), axis=0)
    me = lax.axis_index("x") * lax.axis_size("z") + lax.axis_index("z")
    mine = me * capacity + jnp.arange(capacity, dtype=jnp.int32)
    used = jnp.any(targets[:, None] == mine[None, :], axis=0).astype(jnp.float32)

    act = activations.T.reshape(-1, lax.axis_size("z"), strip, tokens).transpose(1, 0, 2, 3)
    act = act.reshape(lax.axis_size("z"), -1, tokens)
    direction, left_new, right_new, var_new = shampoo(
        act, cotangents, stats_left[0, 0], stats_right[0, 0],
        variance.reshape(strip * count, block), source, targets, used,
    )
    direction = direction.transpose(1, 0, 2)[None]
    return (direction, left_new[None, None], right_new[None, None], var_new.reshape(variance.shape))


def solution(mesh):
    fine = Mesh(mesh.devices.reshape(X, Z, Y, 2), ("x", "z", "y", "c"))
    dp, mp = ("x", "z"), ("y", "c")

    def whole(activations, cotangents, owners, stats_left, stats_right, variance):
        return per_device(activations, cotangents, owners, stats_left, stats_right, variance)

    return jax.shard_map(
        whole,
        mesh=fine,
        in_specs=(
            P(dp, mp),
            P(dp, mp),
            P(mp, None),
            P(mp, dp, None, None, None),
            P(mp, dp, None, None, None),
            P(mp, dp, None, None),
        ),
        out_specs=(
            P(mp, dp, None, None),
            P(mp, dp, None, None, None),
            P(mp, dp, None, None, None),
            P(mp, dp, None, None),
        ),
        check_vma=False,
    )
```

```python
import functools

import jax
import jax.numpy as jnp
from jax import lax
from jax.experimental import pallas as pl
from jax.experimental.pallas import tpu as pltpu
from jax.sharding import Mesh, PartitionSpec as P

X, Z, Y = 4, 8, 4
MESH = pl.DeviceIdType.MESH
COEFFICIENTS = (
    25 / 16, -5 / 16 - 3125 / 4096, 3125 / 4096, -1250 / 4096, 250 / 4096, -25 / 4096, 1 / 4096,
)


def halves(value):
    high = value.astype(jnp.bfloat16)
    return high, (value - high.astype(jnp.float32)).astype(jnp.bfloat16)


def dot(left, right):
    return jnp.dot(left, right, preferred_element_type=jnp.float32)


def tiled_product(left_high, left_low, right_high, right_low, order, finish):
    tile = order // 2

    def one(step, carry):
        rows = pl.ds(pl.multiple_of(step * tile, tile), tile)
        high, low = left_high[rows, :], left_low[rows, :]
        total = dot(high, right_low[...]) + dot(low, right_high[...])
        finish(rows, dot(high, right_high[...]) + total)
        return carry

    lax.fori_loop(0, 2, one, 0)


def step_kernel(
    sizes, act, cot, stats_left, stats_right, variance, owners,
    direction, left_new, right_new, var_new,
    act_in, act_t, source, targets, used, cbuf, abuf, grad, sbuf, vbuf, vt, matrix, m2, m_h, m_l, m2_h, m2_l, w_h, w_l, root_h, root_l,
    gsend, gsend_row, gq, gq_row, scale_rows, adam_rows, send_q, send_row, rq, rq_row,
    owned_h, owned_l, pre, finished, ret,
    own_sem, stat_sem, out_sem, var_sem, c1_s, c1_r, a1_s, a1_r, zr_s, zr_r, a2_s, a2_r,
    y_s, y_r, sib_s, sib_r, ex_s, ex_r, exr_s, exr_r, go_s, go_r, gor_s, gor_r, back_s, back_r,
):
    nx, nz, ny, block, strip, tokens, rows_i = sizes
    count, devices, width = rows_i * nx, nx * nz, rows_i * strip
    lane = vbuf.shape[2]
    half = nz // 2
    x, z = lax.axis_index("x"), lax.axis_index("z")
    y, c = lax.axis_index("y"), lax.axis_index("c")
    mine = 2 * y + c
    me = x * nz + z

    def remote(src, dst, send, recv, **where):
        return pltpu.make_async_remote_copy(
            src_ref=src, dst_ref=dst, send_sem=send, recv_sem=recv,
            device_id=where, device_id_type=MESH,
        )

    barrier = pltpu.get_barrier_semaphore()

    def plane(d):
        return lax.rem(x + d // nz, nx), lax.rem(z + lax.rem(d, nz), nz)

    partners = [{"x": lax.rem(x + d, nx)} for d in range(1, nx)]
    partners += [{"z": lax.rem(z + d, nz)} for d in range(1, nz)]
    partners += [{"y": lax.rem(y + d, ny)} for d in range(1, ny)]
    partners += [{"c": 1 - c}]
    for partner in partners:
        pl.semaphore_signal(barrier, inc=1, device_id=partner, device_id_type=MESH)
    loads = [
        pltpu.make_async_copy(ref.at[slot], sbuf.at[2 * side + slot], stat_sem.at[2 * side + slot])
        for side, ref in enumerate((stats_left, stats_right))
        for slot in range(2)
    ]
    own_c = pltpu.make_async_copy(
        cot.at[:, pl.ds(pl.multiple_of(x * block, block), block)], cbuf.at[z, x], own_sem.at[0]
    )
    act_load = pltpu.make_async_copy(act, act_in, own_sem.at[1])
    loads += [
        pltpu.make_async_copy(
            variance.at[:, k * lane : (k + 1) * lane], vbuf.at[k], var_sem.at[0, k]
        )
        for k in range(block // lane)
    ]
    act_load.start()
    own_c.start()
    for load in loads:
        load.start()

    act_load.wait()
    turned = act_in[...].T
    for x2 in range(nx):
        for z2 in range(nz):
            first = (x2 * nz + z2) * strip
            act_t[z2, x2 * strip : (x2 + 1) * strip, :] = turned[first : first + strip]
    abuf[z, x, mine] = act_t[z]
    pl.semaphore_wait(barrier, len(partners))

    sends = []

    def launch(copy):
        copy.start()
        sends.append(copy)

    def c1(d):
        j = lax.rem(x + d, nx)
        return remote(
            cot.at[:, pl.ds(pl.multiple_of(j * block, block), block)],
            cbuf.at[z, x], c1_s.at[d - 1], c1_r.at[d - 1], x=j,
        )

    def a1(d):
        z2 = lax.rem(z + d, nz)
        return remote(act_t.at[z2], abuf.at[z, x, mine], a1_s.at[d - 1], a1_r.at[d - 1], z=z2)

    def ring(way, hop, k):
        x2 = lax.rem(x - k + nx, nx)
        step = 1 if way == 0 else nz - 1
        origin = lax.rem(z - hop + nz, nz) if way == 0 else lax.rem(z + hop, nz)
        part = cbuf.at[origin, x2]
        return remote(
            part, part, zr_s.at[way, hop, k], zr_r.at[way, hop, k], z=lax.rem(z + step, nz)
        )

    def a2(d):
        part = abuf.at[:, x, mine]
        return remote(part, part, a2_s.at[d - 1], a2_r.at[d - 1], x=lax.rem(x + d, nx))

    def over_y(k, d):
        part = abuf.at[:, lax.rem(x - k + nx, nx), mine]
        return remote(
            part, part, y_s.at[k, d - 1], y_r.at[k, d - 1], y=lax.rem(y + d, ny)
        )

    def sibling(k, d):
        part = abuf.at[:, lax.rem(x - k + nx, nx), 2 * lax.rem(y - d + ny, ny) + c]
        return remote(part, part, sib_s.at[k, d], sib_r.at[k, d], c=1 - c)

    near = [1, nx - 1]
    for d in near:
        c1(d).start()
    own_c.wait()
    for way in range(2):
        launch(ring(way, 0, 0))
    for d in range(1, nz):
        launch(a1(d))
    for d in near:
        c1(d).wait_send()
    for d in range(2, nx - 1):
        launch(c1(d))
    for k in near + list(range(2, nx - 1)):
        c1(k).wait_recv()
        for way in range(2):
            launch(ring(way, 0, k))
    for d in range(1, nz):
        a1(d).wait_recv()
    for d in range(1, nx):
        launch(a2(d))
    for d in range(1, ny):
        launch(over_y(0, d))
    launch(sibling(0, 0))
    for load in loads:
        load.wait()

    def find_blocks(owner, carry):
        low, high = jnp.int32(count), jnp.int32(0)
        for b in range(count):
            hit = owners[b] == owner
            low = jnp.where(hit, jnp.minimum(low, b), low)
            high = jnp.where(hit, b, high)
        source[2 * owner] = jnp.where(low == count, 0, low)
        source[2 * owner + 1] = high
        return carry

    def find_target(b, carry):
        earlier = jnp.int32(0)
        for c2 in range(count):
            hit = jnp.logical_and(owners[c2] == owners[b], c2 < b)
            earlier = jnp.where(hit, earlier + 1, earlier)
        targets[b] = 2 * owners[b] + earlier
        return carry

    held = jnp.int32(0)
    for b in range(count):
        held = jnp.where(owners[b] == me, held + 1, held)
    for slot in range(2):
        used[slot] = jnp.where(held > slot, 1.0, 0.0)

    items = nx * (ny - 1)
    per_step = -(-items // 6)

    def one_matrix(q, carry):
        for t in range(3):
            n = 3 * q + t
            hop, place = n // nx + 1, lax.rem(n, nx)
            k = jnp.where(place == 2, nx - 1, jnp.where(place == 3, 2, place))
            ring(0, hop - 1, k).wait_recv()
            ring(1, hop - 1, k).wait_recv()
            inner = hop < half - 1

            @pl.when(jnp.logical_or(inner, place < nx // 2))
            def _():
                ring(0, hop, k).start()

            @pl.when(jnp.logical_or(inner, place >= nx // 2))
            def _():
                ring(1, hop, k).start()

            if t + 1 < nx:

                @pl.when(q == 0)
                def _():
                    a2(t + 1).wait_recv()
                    for d in range(1, ny):
                        over_y(t + 1, d).start()
                    sibling(t + 1, 0).start()

            for extra in range(per_step):
                item = (n - 3) * per_step + extra

                @pl.when(jnp.logical_and(n >= 3, item < items))
                def _():
                    k2, d2 = item // (ny - 1), lax.rem(item, ny - 1) + 1
                    over_y(k2, d2).wait_recv()
                    sibling(k2, d2).start()

            each = -(-devices // 12)
            lax.fori_loop(n * each, jnp.minimum(n * each + each, devices), find_blocks, 0)
            each = -(-count // 12)
            lax.fori_loop(n * each, jnp.minimum(n * each + each, count), find_target, 0)

            if t == 0:
                stat = sbuf[q]
                bound = jnp.max(jnp.sum(jnp.abs(stat), axis=1, keepdims=True), axis=0, keepdims=True)
                value = stat * (1.0 / bound)
                matrix[...] = value
                m_h[...], m_l[...] = halves(value)

                def finish(rows, value):
                    m2[rows, :] = value
                    m2_h[rows, :], m2_l[rows, :] = halves(value)
                    w_h[rows, :], w_l[rows, :] = halves(
                        COEFFICIENTS[5] * matrix[rows, :] + COEFFICIENTS[6] * value
                    )

                tiled_product(m_h, m_l, m_h, m_l, block, finish)
            elif t == 1:

                def finish(rows, value):
                    value += COEFFICIENTS[3] * matrix[rows, :] + COEFFICIENTS[4] * m2[rows, :]
                    m_h[rows, :], m_l[rows, :] = halves(value)

                tiled_product(m2_h, m2_l, w_h, w_l, block, finish)
            else:

                def finish(rows, value):
                    value += COEFFICIENTS[1] * matrix[rows, :] + COEFFICIENTS[2] * m2[rows, :]
                    ids = lax.broadcasted_iota(jnp.int32, value.shape, 0) + rows.start
                    columns = lax.broadcasted_iota(jnp.int32, value.shape, 1)
                    value += jnp.where(ids == columns, COEFFICIENTS[0], 0.0)
                    root_h[q, rows, :], root_l[q, rows, :] = halves(value)

                tiled_product(m2_h, m2_l, m_h, m_l, block, finish)

            each = -(-count // 12)
            for extra in range(each):
                b = n * each + extra

                @pl.when(b < count)
                def _():
                    rows = pl.ds(pl.multiple_of(b * strip, strip), strip)
                    for k in range(block // lane):
                        vt[k, rows, :] = vbuf[k, pl.ds(b, strip, stride=count), :]
        return carry

    lax.fori_loop(0, 4, one_matrix, 0)

    for k in range(nx):
        for d in range(ny):
            sibling(k, d).wait_recv()

    def shard(origin, rows=None):
        parts = []
        for x2 in range(nx):
            if rows is None:
                piece = abuf[origin, x2]
            else:
                piece = abuf[origin, x2, :, rows, :]
            parts.append(piece.reshape(-1, tokens))
        left = jnp.concatenate(parts, axis=1)
        return dot(left, cbuf[origin].reshape(nx * tokens, block))

    grad[...] = shard(z).reshape(grad.shape)

    def add(d, carry):
        grad[...] += shard(lax.rem(z + d + (d >= half).astype(jnp.int32), nz)).reshape(grad.shape)
        return carry

    lax.fori_loop(1, nz - 1, add, 0)

    for k in range(nx):
        ring(0 if k < nx // 2 else 1, half - 1, k).wait_recv()
    far = lax.rem(z + half, nz)

    def exchange(d):
        j = lax.rem(x + d, nx)
        return (
            remote(gsend.at[j], gq.at[x], ex_s.at[d - 1], ex_r.at[d - 1], x=j),
            remote(gsend_row.at[j], gq_row.at[x], exr_s.at[d - 1], exr_r.at[d - 1], x=j),
        )

    diagonal = lax.broadcasted_iota(jnp.int32, (width, width), 0) == lax.broadcasted_iota(
        jnp.int32, (width, width), 1
    )
    for d in [2, 1, nx - 1, 0]:
        j = lax.rem(x + d, nx)
        rows = pl.ds(pl.multiple_of(j * strip, strip), strip)
        value = grad[:, rows, :].reshape(width, block) + shard(far, rows)
        top = jnp.maximum(jnp.max(jnp.abs(value), axis=1, keepdims=True), 1e-30)
        coded = jnp.round(value * (32767.0 / top)).astype(jnp.int32).astype(jnp.int16)
        row = jnp.sum(jnp.where(diagonal, top * (1.0 / 32767.0), 0.0), axis=0, keepdims=True)
        if d:
            gsend[j] = coded.reshape(rows_i, strip, block)
            gsend_row[j] = row
            for copy in exchange(d):
                launch(copy)
        else:
            gq[x] = coded.reshape(rows_i, strip, block)
            gq_row[x] = row

    lanes = lax.broadcasted_iota(jnp.int32, (1, width), 1)

    def strips_of(j):
        row = gq_row[j]
        column = jnp.sum(jnp.where(diagonal, row, 0.0), axis=1, keepdims=True)
        for i in range(rows_i):
            b = i * nx + j
            value = gq[j, i].astype(jnp.float32) * column[i * strip : (i + 1) * strip]
            square = value * value
            rows = pl.ds(pl.multiple_of(b * strip, strip), strip)
            old = jnp.concatenate([vt[k, rows, :] for k in range(block // lane)], axis=1)
            fresh = 0.9 * old + 0.1 * square
            for k in range(block // lane):
                vt[k, rows, :] = fresh[:, k * lane : (k + 1) * lane]
            total = jnp.sum(square / fresh, axis=0, keepdims=True)
            adam_rows[pl.ds(b, 1), :] = sum(
                total[:, k * width : (k + 1) * width] for k in range(block // width)
            )
            inside = jnp.logical_and(lanes >= i * strip, lanes < (i + 1) * strip)
            scale_rows[pl.ds(b, 1), :] = jnp.where(inside, row, 0.0)

    strips_of(x)
    for d in (1, nx - 1, 2):
        for copy in exchange(d):
            copy.wait_recv()
        strips_of(lax.rem(x - d + nx, nx))

    def go(slot, d):
        x2, z2 = plane(d)
        other = x2 * nz + z2
        return (
            remote(send_q.at[slot, other], rq.at[slot, me],
                   go_s.at[slot, d - 1], go_r.at[slot, d - 1], x=x2, z=z2),
            remote(send_row.at[slot, other], rq_row.at[slot, me],
                   gor_s.at[slot, d - 1], gor_r.at[slot, d - 1], x=x2, z=z2),
        )

    def picked(slot, other):
        b = source[2 * other + slot]
        rows = jnp.concatenate([scale_rows[pl.ds(b, 1), :], adam_rows[pl.ds(b, 1), :]], axis=0)
        return gq[lax.rem(b, nx), b // nx], rows

    for slot in range(2):

        def send(d, carry):
            x2, z2 = plane(d)
            other = x2 * nz + z2
            send_q[slot, other], send_row[slot, other] = picked(slot, other)
            for copy in go(slot, d):
                copy.start()
            return carry

        lax.fori_loop(1, devices, send, 0)
        rq[slot, me], rq_row[slot, me] = picked(slot, me)

    def reorder(r, carry):
        rows = pl.ds(pl.multiple_of(r * count, count), count)
        for k in range(block // lane):
            vbuf[k, rows, :] = vt[k, pl.ds(r, count, stride=strip), :]
        return carry

    lax.fori_loop(0, strip, reorder, 0)
    outs = [
        pltpu.make_async_copy(
            vbuf.at[k], var_new.at[:, k * lane : (k + 1) * lane], var_sem.at[1, k]
        )
        for k in range(block // lane)
    ]
    for copy in outs:
        copy.start()

    def arrival(d):
        return lax.rem(x - d // nz + nx, nx) * nz + lax.rem(z - lax.rem(d, nz) + nz, nz)

    def back(slot, d):
        x2, z2 = plane(d)
        other = x2 * nz + z2
        rows = pl.ds(pl.multiple_of(other * strip, strip), strip)
        return remote(
            finished.at[slot, rows, :], ret.at[2 * me + slot],
            back_s.at[slot, d - 1], back_r.at[slot, d - 1], x=x2, z=z2,
        )

    fits = lax.rem(lax.broadcasted_iota(jnp.int32, (strip, width), 1), strip) == (
        lax.broadcasted_iota(jnp.int32, (strip, width), 0)
    )
    for slot in range(2):
        keep = used[slot]

        def decode(p, total):
            extra = rq_row[slot, p]
            column = jnp.sum(jnp.where(fits, extra[0:1], 0.0), axis=1, keepdims=True) * keep
            value = rq[slot, p].astype(jnp.float32) * column
            rows = pl.ds(pl.multiple_of(p * strip, strip), strip)
            owned_h[slot, rows, :], owned_l[slot, rows, :] = halves(value)
            return total + extra[1:2]

        def receive(d, total):
            for copy in go(slot, d):
                copy.wait_recv()
            return decode(arrival(d), total)

        total = decode(me, jnp.zeros((1, width), jnp.float32))
        total = lax.fori_loop(1, devices, receive, total)

        def finish(rows, value):
            m_h[rows, :], m_l[rows, :] = halves(value)

        tiled_product(
            root_h.at[slot], root_l.at[slot], owned_h.at[slot], owned_l.at[slot], block, finish
        )

        def finish(rows, value):
            pre[rows, :] = value

        tiled_product(m_h, m_l, root_h.at[2 + slot], root_l.at[2 + slot], block, finish)
        value = pre[...]
        squares = jnp.sum(jnp.sum(value * value, axis=0, keepdims=True), axis=1, keepdims=True)
        mean_adam = jnp.sum(total, axis=1, keepdims=True) * (1.0 / (block * block))
        ratio = jnp.sqrt(mean_adam / (squares * (1.0 / (block * block)) + 1e-6))
        finished[slot] = (value * ratio).astype(jnp.bfloat16)

        def send_back(d, carry):
            back(slot, d).start()
            return carry

        lax.fori_loop(1, devices, send_back, 0)
        rows = pl.ds(pl.multiple_of(me * strip, strip), strip)
        ret[2 * me + slot] = finished[slot, rows, :]

    tile = block // 2
    for slot in range(2):

        def outer(step, carry):
            rows = pl.ds(pl.multiple_of(step * tile, tile), tile)

            def pair(dims, left_high, left_low):
                def one(left, right):
                    return lax.dot_general(
                        left, right, (dims, ((), ())), preferred_element_type=jnp.float32
                    )

                total = one(left_high, owned_l[slot]) + one(left_low, owned_h[slot])
                return one(left_high, owned_h[slot]) + total

            left = pair(((1,), (1,)), owned_h[slot, rows, :], owned_l[slot, rows, :])
            sbuf[slot, rows, :] = 0.9 * sbuf[slot, rows, :] + 0.1 * left
            right = pair(((0,), (0,)), owned_h[slot, :, rows], owned_l[slot, :, rows])
            sbuf[2 + slot, rows, :] = 0.9 * sbuf[2 + slot, rows, :] + 0.1 * right
            return carry

        lax.fori_loop(0, 2, outer, 0)
        outs.append(pltpu.make_async_copy(sbuf.at[slot], left_new.at[slot], out_sem.at[slot]))
        outs.append(
            pltpu.make_async_copy(sbuf.at[2 + slot], right_new.at[slot], out_sem.at[2 + slot])
        )
        for copy in outs[-2:]:
            copy.start()

    for slot in range(2):

        def collect(d, carry):
            back(slot, d).wait_recv()
            return carry

        lax.fori_loop(1, devices, collect, 0)

    def choose(b, carry):
        direction[b] = ret[targets[b]]
        return carry

    lax.fori_loop(0, count, choose, 0)

    for copy in outs:
        copy.wait()
    for slot in range(2):

        def drain(d, carry):
            for copy in go(slot, d):
                copy.wait_send()
            back(slot, d).wait_send()
            return carry

        lax.fori_loop(1, devices, drain, 0)
    for copy in sends:
        copy.wait_send()
    for hop in range(1, half):
        for k in range(nx):
            for way in range(2):
                if hop < half - 1 or (k < nx // 2) == (way == 0):
                    ring(way, hop, k).wait_send()
    for k in range(1, nx):
        for d in range(1, ny):
            over_y(k, d).wait_send()
    for k in range(nx):
        for d in range(ny):
            if (k, d) != (0, 0):
                sibling(k, d).wait_send()


def shampoo(act, cot, stats_left, stats_right, variance, owners):
    tokens = act.shape[0]
    nx, nz, ny = lax.axis_size("x"), lax.axis_size("z"), lax.axis_size("y")
    block = stats_left.shape[-1]
    strip = block // (nx * nz)
    rows_z = nx * strip
    rows_i = 2 * ny
    sizes = (nx, nz, ny, block, strip, tokens, rows_i)
    half = nz // 2
    count, devices, width = rows_i * nx, nx * nz, rows_i * strip
    lane = min(block, 128)
    bf16, f32, i16 = jnp.bfloat16, jnp.float32, jnp.int16
    sem, vmem = pltpu.SemaphoreType.DMA, pltpu.VMEM
    square = (block, block)
    anywhere = pl.BlockSpec(memory_space=pl.ANY)
    scalars = pl.BlockSpec(memory_space=pltpu.SMEM)
    return pl.pallas_call(
        functools.partial(step_kernel, sizes),
        out_shape=(
            jax.ShapeDtypeStruct((count, strip, block), bf16),
            jax.ShapeDtypeStruct(stats_left.shape, f32),
            jax.ShapeDtypeStruct(stats_right.shape, f32),
            jax.ShapeDtypeStruct(variance.shape, f32),
        ),
        in_specs=[anywhere] * 5 + [scalars],
        out_specs=(pl.BlockSpec(memory_space=pltpu.VMEM),) + (anywhere,) * 3,
        scratch_shapes=[
            vmem((tokens, block), bf16),
            vmem((nz, rows_z, tokens), bf16),
            pltpu.SMEM((2 * devices,), jnp.int32),
            pltpu.SMEM((count,), jnp.int32),
            pltpu.SMEM((2,), f32),
            vmem((nz, nx, tokens, block), bf16),
            vmem((nz, nx, rows_i, rows_z, tokens), bf16),
            vmem((rows_i, rows_z, block), f32),
            vmem((4, block, block), f32),
            vmem((block // lane, strip * count, lane), f32),
            vmem((block // lane, strip * count, lane), f32),
            vmem(square, f32),
            vmem(square, f32),
        ]
        + [vmem(square, bf16)] * 6
        + [
            vmem((4, block, block), bf16),
            vmem((4, block, block), bf16),
            vmem((nx, rows_i, strip, block), i16),
            vmem((nx, 1, width), f32),
            vmem((nx, rows_i, strip, block), i16),
            vmem((nx, 1, width), f32),
            vmem((count, width), f32),
            vmem((count, width), f32),
            vmem((2, devices, strip, block), i16),
            vmem((2, devices, 2, width), f32),
            vmem((2, devices, strip, block), i16),
            vmem((2, devices, 2, width), f32),
            vmem((2, block, block), bf16),
            vmem((2, block, block), bf16),
            vmem(square, f32),
            vmem((2, block, block), bf16),
            vmem((2 * devices, strip, block), bf16),
            sem((2,)), sem((4,)), sem((4,)), sem((2, block // lane)),
            sem((nx - 1,)), sem((nx - 1,)),
            sem((nz - 1,)), sem((nz - 1,)),
            sem((2, half, nx)), sem((2, half, nx)),
            sem((nx - 1,)), sem((nx - 1,)),
            sem((nx, max(1, ny - 1))), sem((nx, max(1, ny - 1))),
            sem((nx, ny)), sem((nx, ny)),
        ]
        + [sem((nx - 1,))] * 4
        + [sem((2, devices - 1))] * 6,
        compiler_params=pltpu.CompilerParams(
            collective_id=0, has_side_effects=True, vmem_limit_bytes=60 * 1024 * 1024
        ),
    )(act, cot, stats_left, stats_right, variance, owners)


def settle_kernel(left, right, variance, left_out, right_out, variance_out, held, in_sem, out_sem):
    pairs = [(left.at[s], left_out.at[s]) for s in range(left.shape[0])]
    pairs += [(right.at[s], right_out.at[s]) for s in range(right.shape[0])]
    pairs += [(variance, variance_out)]
    reads = [
        pltpu.make_async_copy(src, held.at[k], in_sem.at[k]) for k, (src, _) in enumerate(pairs)
    ]
    writes = [
        pltpu.make_async_copy(held.at[k], dst, out_sem.at[k]) for k, (_, dst) in enumerate(pairs)
    ]
    for copy in reads:
        copy.start()
    for read, write in zip(reads, writes):
        read.wait()
        write.start()
    for copy in writes:
        copy.wait()


def settle(left, right, variance):
    pieces = 2 * left.shape[0] + 1
    anywhere = pl.BlockSpec(memory_space=pl.ANY)
    return pl.pallas_call(
        settle_kernel,
        out_shape=tuple(jax.ShapeDtypeStruct(a.shape, a.dtype) for a in (left, right, variance)),
        in_specs=[anywhere] * 3,
        out_specs=(anywhere,) * 3,
        scratch_shapes=[
            pltpu.VMEM((pieces,) + variance.shape, variance.dtype),
            pltpu.SemaphoreType.DMA((pieces,)),
            pltpu.SemaphoreType.DMA((pieces,)),
        ],
        compiler_params=pltpu.CompilerParams(vmem_limit_bytes=60 * 1024 * 1024),
    )(left, right, variance)


def per_device(activations, cotangents, owners, stats_left, stats_right, variance):
    block = activations.shape[1]
    count = owners.shape[0]
    strip = variance.shape[1]
    direction, left_new, right_new, var_new = shampoo(
        activations, cotangents, stats_left[0, 0], stats_right[0, 0],
        variance.reshape(strip * count, block), owners[:, 0],
    )
    left_new, right_new, var_new = settle(left_new, right_new, var_new)
    direction = direction.transpose(1, 0, 2)[None]
    return (direction, left_new[None, None], right_new[None, None], var_new.reshape(variance.shape))


def solution(mesh):
    fine = Mesh(mesh.devices.reshape(X, Z, Y, 2), ("x", "z", "y", "c"))
    dp, mp = ("x", "z"), ("y", "c")

    def whole(activations, cotangents, owners, stats_left, stats_right, variance):
        return per_device(activations, cotangents, owners, stats_left, stats_right, variance)

    return jax.shard_map(
        whole,
        mesh=fine,
        in_specs=(
            P(dp, mp),
            P(dp, mp),
            P(mp, None),
            P(mp, dp, None, None, None),
            P(mp, dp, None, None, None),
            P(mp, dp, None, None),
        ),
        out_specs=(
            P(mp, dp, None, None),
            P(mp, dp, None, None, None),
            P(mp, dp, None, None, None),
            P(mp, dp, None, None),
        ),
        check_vma=False,
    )
```

```python
import functools

import jax
import jax.numpy as jnp
from jax import lax
from jax.experimental import pallas as pl
from jax.experimental.pallas import tpu as pltpu
from jax.sharding import Mesh, PartitionSpec as P

X, Z, Y = 4, 8, 4
MESH = pl.DeviceIdType.MESH
COEFFICIENTS = (
    25 / 16, -5 / 16 - 3125 / 4096, 3125 / 4096, -1250 / 4096, 250 / 4096, -25 / 4096, 1 / 4096,
)


def halves(value):
    high = value.astype(jnp.bfloat16)
    return high, (value - high.astype(jnp.float32)).astype(jnp.bfloat16)


def dot(left, right):
    return jnp.dot(left, right, preferred_element_type=jnp.float32)


def tiled_product(left_high, left_low, right_high, right_low, order, finish):
    tile = order // 2

    def one(step, carry):
        rows = pl.ds(pl.multiple_of(step * tile, tile), tile)
        high, low = left_high[rows, :], left_low[rows, :]
        total = dot(high, right_low[...]) + dot(low, right_high[...])
        finish(rows, dot(high, right_high[...]) + total)
        return carry

    lax.fori_loop(0, 2, one, 0)


def step_kernel(
    sizes, act, cot, stats_left, stats_right, variance, owners,
    direction, left_new, right_new, var_new,
    act_in, act_t, source, targets, used, cbuf, abuf, grad, sbuf, vbuf, vt, matrix, m2, m_h, m_l, m2_h, m2_l, w_h, w_l, root_h, root_l,
    gsend, gsend_row, gq, gq_row, scale_rows, adam_rows, send_q, send_row, rq, rq_row,
    owned_h, owned_l, pre, finished, ret,
    own_sem, stat_sem, out_sem, var_sem, c1_s, c1_r, a1_s, a1_r, zr_s, zr_r, a2_s, a2_r,
    y_s, y_r, sib_s, sib_r, ex_s, ex_r, exr_s, exr_r, go_s, go_r, gor_s, gor_r, back_s, back_r,
):
    nx, nz, ny, block, strip, tokens, rows_i = sizes
    count, devices, width = rows_i * nx, nx * nz, rows_i * strip
    lane = vbuf.shape[2]
    half = nz // 2
    x, z = lax.axis_index("x"), lax.axis_index("z")
    y, c = lax.axis_index("y"), lax.axis_index("c")
    mine = 2 * y + c
    me = x * nz + z

    def remote(src, dst, send, recv, **where):
        return pltpu.make_async_remote_copy(
            src_ref=src, dst_ref=dst, send_sem=send, recv_sem=recv,
            device_id=where, device_id_type=MESH,
        )

    barrier = pltpu.get_barrier_semaphore()

    partners = [{"x": lax.rem(x + d, nx)} for d in range(1, nx)]
    partners += [{"z": lax.rem(z + d, nz)} for d in range(1, nz)]
    partners += [{"y": lax.rem(y + d, ny)} for d in range(1, ny)]
    partners += [{"c": 1 - c}]
    for partner in partners:
        pl.semaphore_signal(barrier, inc=1, device_id=partner, device_id_type=MESH)
    loads = [
        pltpu.make_async_copy(ref.at[slot], sbuf.at[2 * side + slot], stat_sem.at[2 * side + slot])
        for side, ref in enumerate((stats_left, stats_right))
        for slot in range(2)
    ]
    own_c = pltpu.make_async_copy(
        cot.at[:, pl.ds(pl.multiple_of(x * block, block), block)], cbuf.at[z, x], own_sem.at[0]
    )
    act_load = pltpu.make_async_copy(act, act_in, own_sem.at[1])
    loads += [
        pltpu.make_async_copy(
            variance.at[:, k * lane : (k + 1) * lane], vbuf.at[k], var_sem.at[0, k]
        )
        for k in range(block // lane)
    ]
    act_load.start()
    own_c.start()
    for load in loads:
        load.start()

    act_load.wait()
    turned = act_in[...].T
    for x2 in range(nx):
        for z2 in range(nz):
            first = (x2 * nz + z2) * strip
            act_t[z2, x2 * strip : (x2 + 1) * strip, :] = turned[first : first + strip]
    abuf[z, x, mine] = act_t[z]
    pl.semaphore_wait(barrier, len(partners))

    sends = []

    def launch(copy):
        copy.start()
        sends.append(copy)

    def c1(d):
        j = lax.rem(x + d, nx)
        return remote(
            cot.at[:, pl.ds(pl.multiple_of(j * block, block), block)],
            cbuf.at[z, x], c1_s.at[d - 1], c1_r.at[d - 1], x=j,
        )

    def a1(d):
        z2 = lax.rem(z + d, nz)
        return remote(act_t.at[z2], abuf.at[z, x, mine], a1_s.at[d - 1], a1_r.at[d - 1], z=z2)

    def ring(way, hop, k):
        x2 = lax.rem(x - k + nx, nx)
        step = 1 if way == 0 else nz - 1
        origin = lax.rem(z - hop + nz, nz) if way == 0 else lax.rem(z + hop, nz)
        part = cbuf.at[origin, x2]
        return remote(
            part, part, zr_s.at[way, hop, k], zr_r.at[way, hop, k], z=lax.rem(z + step, nz)
        )

    def a2(d):
        part = abuf.at[:, x, mine]
        return remote(part, part, a2_s.at[d - 1], a2_r.at[d - 1], x=lax.rem(x + d, nx))

    def over_y(k, d):
        part = abuf.at[:, lax.rem(x - k + nx, nx), mine]
        return remote(
            part, part, y_s.at[k, d - 1], y_r.at[k, d - 1], y=lax.rem(y + d, ny)
        )

    def sibling(k, d):
        part = abuf.at[:, lax.rem(x - k + nx, nx), 2 * lax.rem(y - d + ny, ny) + c]
        return remote(part, part, sib_s.at[k, d], sib_r.at[k, d], c=1 - c)

    near = [1, nx - 1]
    for d in near:
        c1(d).start()
    own_c.wait()
    for way in range(2):
        launch(ring(way, 0, 0))
    for d in range(1, nz):
        launch(a1(d))
    for d in near:
        c1(d).wait_send()
    for d in range(2, nx - 1):
        launch(c1(d))
    for k in near + list(range(2, nx - 1)):
        c1(k).wait_recv()
        for way in range(2):
            launch(ring(way, 0, k))
    for d in range(1, nz):
        a1(d).wait_recv()
    for d in range(1, nx):
        launch(a2(d))
    for d in range(1, ny):
        launch(over_y(0, d))
    launch(sibling(0, 0))
    for load in loads:
        load.wait()

    def find_blocks(owner, carry):
        low, high = jnp.int32(count), jnp.int32(0)
        for b in range(count):
            hit = owners[b] == owner
            low = jnp.where(hit, jnp.minimum(low, b), low)
            high = jnp.where(hit, b, high)
        source[2 * owner] = jnp.where(low == count, 0, low)
        source[2 * owner + 1] = high
        return carry

    def find_target(b, carry):
        earlier = jnp.int32(0)
        for c2 in range(count):
            hit = jnp.logical_and(owners[c2] == owners[b], c2 < b)
            earlier = jnp.where(hit, earlier + 1, earlier)
        targets[b] = 2 * owners[b] + earlier
        return carry

    held = jnp.int32(0)
    for b in range(count):
        held = jnp.where(owners[b] == me, held + 1, held)
    for slot in range(2):
        used[slot] = jnp.where(held > slot, 1.0, 0.0)

    items = nx * (ny - 1)
    per_step = -(-items // 6)

    def one_matrix(q, carry):
        for t in range(3):
            n = 3 * q + t
            hop, place = n // nx + 1, lax.rem(n, nx)
            k = jnp.where(place == 2, nx - 1, jnp.where(place == 3, 2, place))
            ring(0, hop - 1, k).wait_recv()
            ring(1, hop - 1, k).wait_recv()
            inner = hop < half - 1

            @pl.when(jnp.logical_or(inner, place < nx // 2))
            def _():
                ring(0, hop, k).start()

            @pl.when(jnp.logical_or(inner, place >= nx // 2))
            def _():
                ring(1, hop, k).start()

            if t + 1 < nx:

                @pl.when(q == 0)
                def _():
                    a2(t + 1).wait_recv()
                    for d in range(1, ny):
                        over_y(t + 1, d).start()
                    sibling(t + 1, 0).start()

            for extra in range(per_step):
                item = (n - 3) * per_step + extra

                @pl.when(jnp.logical_and(n >= 3, item < items))
                def _():
                    k2, d2 = item // (ny - 1), lax.rem(item, ny - 1) + 1
                    over_y(k2, d2).wait_recv()
                    sibling(k2, d2).start()

            each = -(-devices // 12)
            lax.fori_loop(n * each, jnp.minimum(n * each + each, devices), find_blocks, 0)
            each = -(-count // 12)
            lax.fori_loop(n * each, jnp.minimum(n * each + each, count), find_target, 0)

            if t == 0:
                stat = sbuf[q]
                bound = jnp.max(jnp.sum(jnp.abs(stat), axis=1, keepdims=True), axis=0, keepdims=True)
                value = stat * (1.0 / bound)
                matrix[...] = value
                m_h[...], m_l[...] = halves(value)

                def finish(rows, value):
                    m2[rows, :] = value
                    m2_h[rows, :], m2_l[rows, :] = halves(value)
                    w_h[rows, :], w_l[rows, :] = halves(
                        COEFFICIENTS[5] * matrix[rows, :] + COEFFICIENTS[6] * value
                    )

                tiled_product(m_h, m_l, m_h, m_l, block, finish)
            elif t == 1:

                def finish(rows, value):
                    value += COEFFICIENTS[3] * matrix[rows, :] + COEFFICIENTS[4] * m2[rows, :]
                    m_h[rows, :], m_l[rows, :] = halves(value)

                tiled_product(m2_h, m2_l, w_h, w_l, block, finish)
            else:

                def finish(rows, value):
                    value += COEFFICIENTS[1] * matrix[rows, :] + COEFFICIENTS[2] * m2[rows, :]
                    ids = lax.broadcasted_iota(jnp.int32, value.shape, 0) + rows.start
                    columns = lax.broadcasted_iota(jnp.int32, value.shape, 1)
                    value += jnp.where(ids == columns, COEFFICIENTS[0], 0.0)
                    root_h[q, rows, :], root_l[q, rows, :] = halves(value)

                tiled_product(m2_h, m2_l, m_h, m_l, block, finish)

            each = -(-count // 12)
            for extra in range(each):
                b = n * each + extra

                @pl.when(b < count)
                def _():
                    rows = pl.ds(pl.multiple_of(b * strip, strip), strip)
                    for k in range(block // lane):
                        vt[k, rows, :] = vbuf[k, pl.ds(b, strip, stride=count), :]
        return carry

    lax.fori_loop(0, 4, one_matrix, 0)

    for k in range(nx):
        for d in range(ny):
            sibling(k, d).wait_recv()

    def shard(origin, rows=None):
        parts = []
        for x2 in range(nx):
            if rows is None:
                piece = abuf[origin, x2]
            else:
                piece = abuf[origin, x2, :, rows, :]
            parts.append(piece.reshape(-1, tokens))
        left = jnp.concatenate(parts, axis=1)
        return dot(left, cbuf[origin].reshape(nx * tokens, block))

    grad[...] = shard(z).reshape(grad.shape)

    def add(d, carry):
        grad[...] += shard(lax.rem(z + d + (d >= half).astype(jnp.int32), nz)).reshape(grad.shape)
        return carry

    lax.fori_loop(1, nz - 1, add, 0)

    for k in range(nx):
        ring(0 if k < nx // 2 else 1, half - 1, k).wait_recv()
    far = lax.rem(z + half, nz)

    def exchange(d):
        j = lax.rem(x + d, nx)
        return (
            remote(gsend.at[j], gq.at[x], ex_s.at[d - 1], ex_r.at[d - 1], x=j),
            remote(gsend_row.at[j], gq_row.at[x], exr_s.at[d - 1], exr_r.at[d - 1], x=j),
        )

    diagonal = lax.broadcasted_iota(jnp.int32, (width, width), 0) == lax.broadcasted_iota(
        jnp.int32, (width, width), 1
    )
    for d in [2, 1, nx - 1, 0]:
        j = lax.rem(x + d, nx)
        rows = pl.ds(pl.multiple_of(j * strip, strip), strip)
        value = grad[:, rows, :].reshape(width, block) + shard(far, rows)
        top = jnp.maximum(jnp.max(jnp.abs(value), axis=1, keepdims=True), 1e-30)
        coded = jnp.round(value * (32767.0 / top)).astype(jnp.int32).astype(jnp.int16)
        row = jnp.sum(jnp.where(diagonal, top * (1.0 / 32767.0), 0.0), axis=0, keepdims=True)
        if d:
            gsend[j] = coded.reshape(rows_i, strip, block)
            gsend_row[j] = row
            for copy in exchange(d):
                launch(copy)
        else:
            gq[x] = coded.reshape(rows_i, strip, block)
            gq_row[x] = row

    lanes = lax.broadcasted_iota(jnp.int32, (1, width), 1)

    def strips_of(j):
        row = gq_row[j]
        column = jnp.sum(jnp.where(diagonal, row, 0.0), axis=1, keepdims=True)
        for i in range(rows_i):
            b = i * nx + j
            value = gq[j, i].astype(jnp.float32) * column[i * strip : (i + 1) * strip]
            square = value * value
            rows = pl.ds(pl.multiple_of(b * strip, strip), strip)
            old = jnp.concatenate([vt[k, rows, :] for k in range(block // lane)], axis=1)
            fresh = 0.9 * old + 0.1 * square
            for k in range(block // lane):
                vt[k, rows, :] = fresh[:, k * lane : (k + 1) * lane]
            total = jnp.sum(square / fresh, axis=0, keepdims=True)
            adam_rows[pl.ds(b, 1), :] = sum(
                total[:, k * width : (k + 1) * width] for k in range(block // width)
            )
            inside = jnp.logical_and(lanes >= i * strip, lanes < (i + 1) * strip)
            scale_rows[pl.ds(b, 1), :] = jnp.where(inside, row, 0.0)

    strips_of(x)
    for d in (1, nx - 1, 2):
        for copy in exchange(d):
            copy.wait_recv()
        strips_of(lax.rem(x - d + nx, nx))

    def wrapped(value, size):
        return jnp.where(value >= size, value - size, value)

    turns = [half] + [dz for step in range(1, half) for dz in (step, nz - step)]

    def others(body, sign):
        ends = {dz: wrapped(z + (dz if sign > 0 else nz - dz), nz) for dz in turns}

        def one(dx, carry):
            x2 = wrapped(x + (dx if sign > 0 else nx - dx), nx)
            for dz in turns:
                body(dx * nz + dz, x2, ends[dz])

            @pl.when(dx > 0)
            def _():
                body(dx * nz, x2, z)

            return carry

        lax.fori_loop(0, nx, one, 0)

    def go(slot, d, x2, z2):
        return remote(
            send_q.at[slot, x2 * nz + z2], rq.at[slot, me],
            go_s.at[slot, d - 1], go_r.at[slot, d - 1], x=x2, z=z2,
        )

    def go_row(d, x2, z2):
        return remote(
            send_row.at[x2 * nz + z2], rq_row.at[me], gor_s.at[d - 1], gor_r.at[d - 1], x=x2, z=z2
        )

    def picked(slot, other):
        b = source[2 * other + slot]
        return gq[lax.rem(b, nx), b // nx]

    def picked_rows(other):
        return jnp.concatenate(
            [
                rows[pl.ds(source[2 * other + slot], 1), :]
                for slot in range(2)
                for rows in (scale_rows, adam_rows)
            ],
            axis=0,
        )

    for slot in range(2):

        def send(d, x2, z2):
            other = x2 * nz + z2
            send_q[slot, other] = picked(slot, other)
            go(slot, d, x2, z2).start()
            if slot == 0:
                send_row[other] = picked_rows(other)
                go_row(d, x2, z2).start()

        others(send, 1)
        rq[slot, me] = picked(slot, me)
        if slot == 0:
            rq_row[me] = picked_rows(me)

    def reorder(r, carry):
        rows = pl.ds(pl.multiple_of(r * count, count), count)
        for k in range(block // lane):
            vbuf[k, rows, :] = vt[k, pl.ds(r, count, stride=strip), :]
        return carry

    lax.fori_loop(0, strip, reorder, 0)
    outs = [
        pltpu.make_async_copy(
            vbuf.at[k], var_new.at[:, k * lane : (k + 1) * lane], var_sem.at[1, k]
        )
        for k in range(block // lane)
    ]
    for copy in outs:
        copy.start()

    def back(slot, d, x2, z2):
        rows = pl.ds(pl.multiple_of((x2 * nz + z2) * strip, strip), strip)
        return remote(
            finished.at[slot, rows, :], ret.at[2 * me + slot],
            back_s.at[slot, d - 1], back_r.at[slot, d - 1], x=x2, z=z2,
        )

    fits = lax.rem(lax.broadcasted_iota(jnp.int32, (strip, width), 1), strip) == (
        lax.broadcasted_iota(jnp.int32, (strip, width), 0)
    )
    for slot in range(2):
        keep = used[slot]

        def decode(p):
            row = rq_row[p, 2 * slot : 2 * slot + 1]
            column = jnp.sum(jnp.where(fits, row, 0.0), axis=1, keepdims=True) * keep
            value = rq[slot, p].astype(jnp.float32) * column
            rows = pl.ds(pl.multiple_of(p * strip, strip), strip)
            owned_h[slot, rows, :], owned_l[slot, rows, :] = halves(value)

        def receive(d, x2, z2):
            if slot == 0:
                go_row(d, x2, z2).wait_recv()
            go(slot, d, x2, z2).wait_recv()
            decode(x2 * nz + z2)

        decode(me)
        others(receive, -1)
        total = jnp.sum(rq_row[:, 2 * slot + 1 : 2 * slot + 2, :], axis=0)

        def finish(rows, value):
            m_h[rows, :], m_l[rows, :] = halves(value)

        tiled_product(
            root_h.at[slot], root_l.at[slot], owned_h.at[slot], owned_l.at[slot], block, finish
        )

        def finish(rows, value):
            pre[rows, :] = value

        tiled_product(m_h, m_l, root_h.at[2 + slot], root_l.at[2 + slot], block, finish)
        value = pre[...]
        squares = jnp.sum(jnp.sum(value * value, axis=0, keepdims=True), axis=1, keepdims=True)
        mean_adam = jnp.sum(total, axis=1, keepdims=True) * (1.0 / (block * block))
        ratio = jnp.sqrt(mean_adam / (squares * (1.0 / (block * block)) + 1e-6))
        finished[slot] = (value * ratio).astype(jnp.bfloat16)

        others(lambda d, x2, z2: back(slot, d, x2, z2).start(), 1)
        rows = pl.ds(pl.multiple_of(me * strip, strip), strip)
        ret[2 * me + slot] = finished[slot, rows, :]

    tile = block // 2
    for slot in range(2):

        def outer(step, carry):
            rows = pl.ds(pl.multiple_of(step * tile, tile), tile)

            def pair(dims, left_high, left_low):
                def one(left, right):
                    return lax.dot_general(
                        left, right, (dims, ((), ())), preferred_element_type=jnp.float32
                    )

                total = one(left_high, owned_l[slot]) + one(left_low, owned_h[slot])
                return one(left_high, owned_h[slot]) + total

            left = pair(((1,), (1,)), owned_h[slot, rows, :], owned_l[slot, rows, :])
            sbuf[slot, rows, :] = 0.9 * sbuf[slot, rows, :] + 0.1 * left
            right = pair(((0,), (0,)), owned_h[slot, :, rows], owned_l[slot, :, rows])
            sbuf[2 + slot, rows, :] = 0.9 * sbuf[2 + slot, rows, :] + 0.1 * right
            return carry

        lax.fori_loop(0, 2, outer, 0)
        outs.append(pltpu.make_async_copy(sbuf.at[slot], left_new.at[slot], out_sem.at[slot]))
        outs.append(
            pltpu.make_async_copy(sbuf.at[2 + slot], right_new.at[slot], out_sem.at[2 + slot])
        )
        for copy in outs[-2:]:
            copy.start()

    for slot in range(2):
        others(lambda d, x2, z2: back(slot, d, x2, z2).wait_recv(), -1)

    def choose(b, carry):
        direction[b] = ret[targets[b]]
        return carry

    lax.fori_loop(0, count, choose, 0)

    for copy in outs:
        copy.wait()
    for slot in range(2):
        others(lambda d, x2, z2: go(slot, d, x2, z2).wait_send(), 1)
        others(lambda d, x2, z2: back(slot, d, x2, z2).wait_send(), 1)
    others(lambda d, x2, z2: go_row(d, x2, z2).wait_send(), 1)
    for copy in sends:
        copy.wait_send()
    for hop in range(1, half):
        for k in range(nx):
            for way in range(2):
                if hop < half - 1 or (k < nx // 2) == (way == 0):
                    ring(way, hop, k).wait_send()
    for k in range(1, nx):
        for d in range(1, ny):
            over_y(k, d).wait_send()
    for k in range(nx):
        for d in range(ny):
            if (k, d) != (0, 0):
                sibling(k, d).wait_send()


def shampoo(act, cot, stats_left, stats_right, variance, owners):
    tokens = act.shape[0]
    nx, nz, ny = lax.axis_size("x"), lax.axis_size("z"), lax.axis_size("y")
    block = stats_left.shape[-1]
    strip = block // (nx * nz)
    rows_z = nx * strip
    rows_i = 2 * ny
    sizes = (nx, nz, ny, block, strip, tokens, rows_i)
    half = nz // 2
    count, devices, width = rows_i * nx, nx * nz, rows_i * strip
    lane = min(block, 128)
    bf16, f32, i16 = jnp.bfloat16, jnp.float32, jnp.int16
    sem, vmem = pltpu.SemaphoreType.DMA, pltpu.VMEM
    square = (block, block)
    anywhere = pl.BlockSpec(memory_space=pl.ANY)
    scalars = pl.BlockSpec(memory_space=pltpu.SMEM)
    return pl.pallas_call(
        functools.partial(step_kernel, sizes),
        out_shape=(
            jax.ShapeDtypeStruct((count, strip, block), bf16),
            jax.ShapeDtypeStruct(stats_left.shape, f32),
            jax.ShapeDtypeStruct(stats_right.shape, f32),
            jax.ShapeDtypeStruct(variance.shape, f32),
        ),
        in_specs=[anywhere] * 5 + [scalars],
        out_specs=(pl.BlockSpec(memory_space=pltpu.VMEM),) + (anywhere,) * 3,
        scratch_shapes=[
            vmem((tokens, block), bf16),
            vmem((nz, rows_z, tokens), bf16),
            pltpu.SMEM((2 * devices,), jnp.int32),
            pltpu.SMEM((count,), jnp.int32),
            pltpu.SMEM((2,), f32),
            vmem((nz, nx, tokens, block), bf16),
            vmem((nz, nx, rows_i, rows_z, tokens), bf16),
            vmem((rows_i, rows_z, block), f32),
            vmem((4, block, block), f32),
            vmem((block // lane, strip * count, lane), f32),
            vmem((block // lane, strip * count, lane), f32),
            vmem(square, f32),
            vmem(square, f32),
        ]
        + [vmem(square, bf16)] * 6
        + [
            vmem((4, block, block), bf16),
            vmem((4, block, block), bf16),
            vmem((nx, rows_i, strip, block), i16),
            vmem((nx, 1, width), f32),
            vmem((nx, rows_i, strip, block), i16),
            vmem((nx, 1, width), f32),
            vmem((count, width), f32),
            vmem((count, width), f32),
            vmem((2, devices, strip, block), i16),
            vmem((devices, 4, width), f32),
            vmem((2, devices, strip, block), i16),
            vmem((devices, 4, width), f32),
            vmem((2, block, block), bf16),
            vmem((2, block, block), bf16),
            vmem(square, f32),
            vmem((2, block, block), bf16),
            vmem((2 * devices, strip, block), bf16),
            sem((2,)), sem((4,)), sem((4,)), sem((2, block // lane)),
            sem((nx - 1,)), sem((nx - 1,)),
            sem((nz - 1,)), sem((nz - 1,)),
            sem((2, half, nx)), sem((2, half, nx)),
            sem((nx - 1,)), sem((nx - 1,)),
            sem((nx, max(1, ny - 1))), sem((nx, max(1, ny - 1))),
            sem((nx, ny)), sem((nx, ny)),
        ]
        + [sem((nx - 1,))] * 4
        + [sem((2, devices - 1))] * 2
        + [sem((devices - 1,))] * 2
        + [sem((2, devices - 1))] * 2,
        compiler_params=pltpu.CompilerParams(
            collective_id=0, has_side_effects=True, vmem_limit_bytes=60 * 1024 * 1024
        ),
    )(act, cot, stats_left, stats_right, variance, owners)


def settle_kernel(
    left, right, variance, direction, left_out, right_out, variance_out, direction_out,
    held, taken, spread, turned, in_sem, out_sem, way_sem,
):
    block = variance.shape[1]
    count, strip = direction.shape[:2]
    lane = spread.shape[2]
    per, part = held.shape[0] // 5, held.shape[1]
    pairs = []
    for step in range(per):
        rows = pl.ds(step * part, part)
        for src, dst in ((left, left_out), (right, right_out)):
            pairs += [(src.at[s, rows, :], dst.at[s, rows, :]) for s in range(2)]
        pairs += [(variance.at[rows, :], variance_out.at[rows, :])]
    first = pltpu.make_async_copy(direction, taken, way_sem.at[0])
    last = pltpu.make_async_copy(turned, direction_out, way_sem.at[1])
    reads = [
        pltpu.make_async_copy(src, held.at[k], in_sem.at[k]) for k, (src, _) in enumerate(pairs)
    ]
    writes = [
        pltpu.make_async_copy(held.at[k], dst, out_sem.at[k]) for k, (_, dst) in enumerate(pairs)
    ]
    first.start()
    for copy in reads:
        copy.start()
    for k in range(len(pairs) // 2):
        reads[k].wait()
        writes[k].start()
    first.wait()
    value = taken[...].reshape(count * strip, block).astype(jnp.float32)
    for k in range(block // lane):
        spread[k] = value[:, k * lane : (k + 1) * lane]
    for r in range(strip):
        turned[r] = jnp.concatenate(
            [spread[k, pl.ds(r, count, stride=strip), :] for k in range(block // lane)], axis=1
        ).astype(turned.dtype)
    last.start()
    for k in range(len(pairs) // 2, len(pairs)):
        reads[k].wait()
        writes[k].start()
    for copy in writes:
        copy.wait()
    last.wait()


def settle(left, right, variance, direction):
    count, strip, block = direction.shape
    lane, part = min(block, 128), block // 4
    pieces = 5 * (block // part)
    anywhere = pl.BlockSpec(memory_space=pl.ANY)
    vmem, sem = pltpu.VMEM, pltpu.SemaphoreType.DMA
    return pl.pallas_call(
        settle_kernel,
        out_shape=tuple(jax.ShapeDtypeStruct(a.shape, a.dtype) for a in (left, right, variance))
        + (jax.ShapeDtypeStruct((strip, count, block), direction.dtype),),
        in_specs=[anywhere] * 4,
        out_specs=(anywhere,) * 4,
        scratch_shapes=[
            vmem((pieces, part, block), variance.dtype),
            vmem(direction.shape, direction.dtype),
            vmem((block // lane, count * strip, lane), jnp.float32),
            vmem((strip, count, block), direction.dtype),
            sem((pieces,)), sem((pieces,)), sem((2,)),
        ],
        compiler_params=pltpu.CompilerParams(vmem_limit_bytes=60 * 1024 * 1024),
    )(left, right, variance, direction)


def per_device(activations, cotangents, owners, stats_left, stats_right, variance):
    block = activations.shape[1]
    count = owners.shape[0]
    strip = variance.shape[1]
    direction, left_new, right_new, var_new = shampoo(
        activations, cotangents, stats_left[0, 0], stats_right[0, 0],
        variance.reshape(strip * count, block), owners[:, 0],
    )
    left_new, right_new, var_new, direction = settle(left_new, right_new, var_new, direction)
    return (direction[None], left_new[None, None], right_new[None, None], var_new.reshape(variance.shape))


def solution(mesh):
    fine = Mesh(mesh.devices.reshape(X, Z, Y, 2), ("x", "z", "y", "c"))
    dp, mp = ("x", "z"), ("y", "c")

    def whole(activations, cotangents, owners, stats_left, stats_right, variance):
        return per_device(activations, cotangents, owners, stats_left, stats_right, variance)

    return jax.shard_map(
        whole,
        mesh=fine,
        in_specs=(
            P(dp, mp),
            P(dp, mp),
            P(mp, None),
            P(mp, dp, None, None, None),
            P(mp, dp, None, None, None),
            P(mp, dp, None, None),
        ),
        out_specs=(
            P(mp, dp, None, None),
            P(mp, dp, None, None, None),
            P(mp, dp, None, None, None),
            P(mp, dp, None, None),
        ),
        check_vma=False,
    )
```

```python
import functools

import jax
import jax.numpy as jnp
from jax import lax
from jax.experimental import pallas as pl
from jax.experimental.pallas import tpu as pltpu
from jax.sharding import Mesh, PartitionSpec as P

X, Z, Y = 4, 8, 4
MESH = pl.DeviceIdType.MESH
COEFFICIENTS = (
    25 / 16, -5 / 16 - 3125 / 4096, 3125 / 4096, -1250 / 4096, 250 / 4096, -25 / 4096, 1 / 4096,
)


def halves(value):
    high = value.astype(jnp.bfloat16)
    return high, (value - high.astype(jnp.float32)).astype(jnp.bfloat16)


def dot(left, right):
    return jnp.dot(left, right, preferred_element_type=jnp.float32)


def tiled_product(left_high, left_low, right_high, right_low, order, finish):
    tile = order // 2

    def one(step, carry):
        rows = pl.ds(pl.multiple_of(step * tile, tile), tile)
        high, low = left_high[rows, :], left_low[rows, :]
        total = dot(high, right_low[...]) + dot(low, right_high[...])
        finish(rows, dot(high, right_high[...]) + total)
        return carry

    lax.fori_loop(0, 2, one, 0)


def step_kernel(
    sizes, act, cot, stats_left, stats_right, variance, owners,
    direction, left_new, right_new, var_new,
    act_in, act_t, source, targets, used, cbuf, abuf, grad, sbuf, vbuf, vt, matrix, m2, m_h, m_l, m2_h, m2_l, w_h, w_l, root_h, root_l,
    gsend, gsend_row, gq, gq_row, scale_rows, adam_rows, send_q, send_row, rq, rq_row,
    owned_h, owned_l, pre, finished, ret,
    own_sem, stat_sem, out_sem, var_sem, c1_s, c1_r, a1_s, a1_r, zr_s, zr_r, a2_s, a2_r,
    y_s, y_r, sib_s, sib_r, ex_s, ex_r, exr_s, exr_r, go_s, go_r, gor_s, gor_r, back_s, back_r,
):
    nx, nz, ny, block, strip, tokens, rows_i = sizes
    count, devices, width = rows_i * nx, nx * nz, rows_i * strip
    lane = vbuf.shape[2]
    half = nz // 2
    x, z = lax.axis_index("x"), lax.axis_index("z")
    y, c = lax.axis_index("y"), lax.axis_index("c")
    mine = 2 * y + c
    me = x * nz + z

    def remote(src, dst, send, recv, **where):
        return pltpu.make_async_remote_copy(
            src_ref=src, dst_ref=dst, send_sem=send, recv_sem=recv,
            device_id=where, device_id_type=MESH,
        )

    barrier = pltpu.get_barrier_semaphore()

    partners = [{"x": lax.rem(x + d, nx)} for d in range(1, nx)]
    partners += [{"z": lax.rem(z + d, nz)} for d in range(1, nz)]
    partners += [{"y": lax.rem(y + d, ny)} for d in range(1, ny)]
    partners += [{"c": 1 - c}]
    for partner in partners:
        pl.semaphore_signal(barrier, inc=1, device_id=partner, device_id_type=MESH)
    loads = [
        pltpu.make_async_copy(ref.at[slot], sbuf.at[2 * side + slot], stat_sem.at[2 * side + slot])
        for side, ref in enumerate((stats_left, stats_right))
        for slot in range(2)
    ]
    own_c = pltpu.make_async_copy(
        cot.at[:, pl.ds(pl.multiple_of(x * block, block), block)], cbuf.at[z, x], own_sem.at[0]
    )
    act_load = pltpu.make_async_copy(act, act_in, own_sem.at[1])
    loads += [
        pltpu.make_async_copy(
            variance.at[:, k * lane : (k + 1) * lane], vbuf.at[k], var_sem.at[0, k]
        )
        for k in range(block // lane)
    ]
    act_load.start()
    own_c.start()
    for load in loads:
        load.start()

    pl.semaphore_wait(barrier, len(partners))

    sends = []

    def launch(copy):
        copy.start()
        sends.append(copy)

    def c1(d):
        j = lax.rem(x + d, nx)
        return remote(
            cot.at[:, pl.ds(pl.multiple_of(j * block, block), block)],
            cbuf.at[z, x], c1_s.at[d - 1], c1_r.at[d - 1], x=j,
        )

    def a1(d):
        z2 = lax.rem(z + d, nz)
        return remote(act_t.at[z2], abuf.at[z, x, mine], a1_s.at[d - 1], a1_r.at[d - 1], z=z2)

    own = cot.at[:, pl.ds(pl.multiple_of(x * block, block), block)]

    def ring(way, hop, k, held=None):
        x2 = lax.rem(x - k + nx, nx)
        step = 1 if way == 0 else nz - 1
        origin = lax.rem(z - hop + nz, nz) if way == 0 else lax.rem(z + hop, nz)
        part = cbuf.at[origin, x2]
        return remote(
            part if held is None else held, part, zr_s.at[way, hop, k], zr_r.at[way, hop, k], z=lax.rem(z + step, nz)
        )

    def a2(d):
        part = abuf.at[:, x, mine]
        return remote(part, part, a2_s.at[d - 1], a2_r.at[d - 1], x=lax.rem(x + d, nx))

    def over_y(k, d):
        part = abuf.at[:, lax.rem(x - k + nx, nx), mine]
        return remote(
            part, part, y_s.at[k, d - 1], y_r.at[k, d - 1], y=lax.rem(y + d, ny)
        )

    def sibling(k, d):
        part = abuf.at[:, lax.rem(x - k + nx, nx), 2 * lax.rem(y - d + ny, ny) + c]
        return remote(part, part, sib_s.at[k, d], sib_r.at[k, d], c=1 - c)

    near = [1, nx - 1]
    for d in near:
        c1(d).start()
    for way in range(2):
        launch(ring(way, 0, 0, own))
    act_load.wait()
    turned = act_in[...].T
    for x2 in range(nx):
        for z2 in range(nz):
            first = (x2 * nz + z2) * strip
            act_t[z2, x2 * strip : (x2 + 1) * strip, :] = turned[first : first + strip]
    abuf[z, x, mine] = act_t[z]
    for d in range(1, nz):
        launch(a1(d))
    for d in near:
        c1(d).wait_send()
    for d in range(2, nx - 1):
        launch(c1(d))
    for k in near + list(range(2, nx - 1)):
        c1(k).wait_recv()
        for way in range(2):
            launch(ring(way, 0, k))
    for d in range(1, nz):
        a1(d).wait_recv()
    for d in range(1, nx):
        launch(a2(d))
    for d in range(1, ny):
        launch(over_y(0, d))
    launch(sibling(0, 0))
    own_c.wait()
    for load in loads:
        load.wait()

    def find_blocks(owner, carry):
        low, high = jnp.int32(count), jnp.int32(0)
        for b in range(count):
            hit = owners[b] == owner
            low = jnp.where(hit, jnp.minimum(low, b), low)
            high = jnp.where(hit, b, high)
        source[2 * owner] = jnp.where(low == count, 0, low)
        source[2 * owner + 1] = high
        return carry

    def find_target(b, carry):
        earlier = jnp.int32(0)
        for c2 in range(count):
            hit = jnp.logical_and(owners[c2] == owners[b], c2 < b)
            earlier = jnp.where(hit, earlier + 1, earlier)
        targets[b] = 2 * owners[b] + earlier
        return carry

    held = jnp.int32(0)
    for b in range(count):
        held = jnp.where(owners[b] == me, held + 1, held)
    for slot in range(2):
        used[slot] = jnp.where(held > slot, 1.0, 0.0)

    items = nx * (ny - 1)
    per_step = -(-items // 6)

    def one_matrix(q, carry):
        for t in range(3):
            n = 3 * q + t
            hop, place = n // nx + 1, lax.rem(n, nx)
            k = jnp.where(place == 2, nx - 1, jnp.where(place == 3, 2, place))
            ring(0, hop - 1, k).wait_recv()
            ring(1, hop - 1, k).wait_recv()
            inner = hop < half - 1

            @pl.when(jnp.logical_or(inner, place < nx // 2))
            def _():
                ring(0, hop, k).start()

            @pl.when(jnp.logical_or(inner, place >= nx // 2))
            def _():
                ring(1, hop, k).start()

            if t + 1 < nx:

                @pl.when(q == 0)
                def _():
                    a2(t + 1).wait_recv()
                    for d in range(1, ny):
                        over_y(t + 1, d).start()
                    sibling(t + 1, 0).start()

            for extra in range(per_step):
                item = (n - 3) * per_step + extra

                @pl.when(jnp.logical_and(n >= 3, item < items))
                def _():
                    k2, d2 = item // (ny - 1), lax.rem(item, ny - 1) + 1
                    over_y(k2, d2).wait_recv()
                    sibling(k2, d2).start()

            each = -(-devices // 12)
            lax.fori_loop(n * each, jnp.minimum(n * each + each, devices), find_blocks, 0)
            each = -(-count // 12)
            lax.fori_loop(n * each, jnp.minimum(n * each + each, count), find_target, 0)

            if t == 0:
                stat = sbuf[q]
                bound = jnp.max(jnp.sum(jnp.abs(stat), axis=1, keepdims=True), axis=0, keepdims=True)
                value = stat * (1.0 / bound)
                matrix[...] = value
                m_h[...], m_l[...] = halves(value)

                def finish(rows, value):
                    m2[rows, :] = value
                    m2_h[rows, :], m2_l[rows, :] = halves(value)
                    w_h[rows, :], w_l[rows, :] = halves(
                        COEFFICIENTS[5] * matrix[rows, :] + COEFFICIENTS[6] * value
                    )

                tiled_product(m_h, m_l, m_h, m_l, block, finish)
            elif t == 1:

                def finish(rows, value):
                    value += COEFFICIENTS[3] * matrix[rows, :] + COEFFICIENTS[4] * m2[rows, :]
                    m_h[rows, :], m_l[rows, :] = halves(value)

                tiled_product(m2_h, m2_l, w_h, w_l, block, finish)
            else:

                def finish(rows, value):
                    value += COEFFICIENTS[1] * matrix[rows, :] + COEFFICIENTS[2] * m2[rows, :]
                    ids = lax.broadcasted_iota(jnp.int32, value.shape, 0) + rows.start
                    columns = lax.broadcasted_iota(jnp.int32, value.shape, 1)
                    value += jnp.where(ids == columns, COEFFICIENTS[0], 0.0)
                    root_h[q, rows, :], root_l[q, rows, :] = halves(value)

                tiled_product(m2_h, m2_l, m_h, m_l, block, finish)

            each = -(-count // 12)
            for extra in range(each):
                b = n * each + extra

                @pl.when(b < count)
                def _():
                    rows = pl.ds(pl.multiple_of(b * strip, strip), strip)
                    for k in range(block // lane):
                        vt[k, rows, :] = vbuf[k, pl.ds(b, strip, stride=count), :]
        return carry

    lax.fori_loop(0, 4, one_matrix, 0)

    for k in range(nx):
        for d in range(ny):
            sibling(k, d).wait_recv()

    def shard(origin, rows=None):
        parts = []
        for x2 in range(nx):
            if rows is None:
                piece = abuf[origin, x2]
            else:
                piece = abuf[origin, x2, :, rows, :]
            parts.append(piece.reshape(-1, tokens))
        left = jnp.concatenate(parts, axis=1)
        return dot(left, cbuf[origin].reshape(nx * tokens, block))

    grad[...] = shard(z).reshape(grad.shape)

    def add(d, carry):
        grad[...] += shard(lax.rem(z + d + (d >= half).astype(jnp.int32), nz)).reshape(grad.shape)
        return carry

    lax.fori_loop(1, nz - 1, add, 0)

    for k in range(nx):
        ring(0 if k < nx // 2 else 1, half - 1, k).wait_recv()
    far = lax.rem(z + half, nz)

    def exchange(d):
        j = lax.rem(x + d, nx)
        return (
            remote(gsend.at[j], gq.at[x], ex_s.at[d - 1], ex_r.at[d - 1], x=j),
            remote(gsend_row.at[j], gq_row.at[x], exr_s.at[d - 1], exr_r.at[d - 1], x=j),
        )

    diagonal = lax.broadcasted_iota(jnp.int32, (width, width), 0) == lax.broadcasted_iota(
        jnp.int32, (width, width), 1
    )
    for d in [2, 1, nx - 1, 0]:
        j = lax.rem(x + d, nx)
        rows = pl.ds(pl.multiple_of(j * strip, strip), strip)
        value = grad[:, rows, :].reshape(width, block) + shard(far, rows)
        top = jnp.maximum(jnp.max(jnp.abs(value), axis=1, keepdims=True), 1e-30)
        coded = jnp.round(value * (32767.0 / top)).astype(jnp.int32).astype(jnp.int16)
        row = jnp.sum(jnp.where(diagonal, top * (1.0 / 32767.0), 0.0), axis=0, keepdims=True)
        if d:
            gsend[j] = coded.reshape(rows_i, strip, block)
            gsend_row[j] = row
            for copy in exchange(d):
                launch(copy)
        else:
            gq[x] = coded.reshape(rows_i, strip, block)
            gq_row[x] = row

    lanes = lax.broadcasted_iota(jnp.int32, (1, width), 1)

    def strips_of(j):
        row = gq_row[j]
        column = jnp.sum(jnp.where(diagonal, row, 0.0), axis=1, keepdims=True)
        for i in range(rows_i):
            b = i * nx + j
            value = gq[j, i].astype(jnp.float32) * column[i * strip : (i + 1) * strip]
            square = value * value
            rows = pl.ds(pl.multiple_of(b * strip, strip), strip)
            old = jnp.concatenate([vt[k, rows, :] for k in range(block // lane)], axis=1)
            fresh = 0.9 * old + 0.1 * square
            for k in range(block // lane):
                vt[k, rows, :] = fresh[:, k * lane : (k + 1) * lane]
            total = jnp.sum(square / fresh, axis=0, keepdims=True)
            adam_rows[pl.ds(b, 1), :] = sum(
                total[:, k * width : (k + 1) * width] for k in range(block // width)
            )
            inside = jnp.logical_and(lanes >= i * strip, lanes < (i + 1) * strip)
            scale_rows[pl.ds(b, 1), :] = jnp.where(inside, row, 0.0)

    strips_of(x)
    for d in (1, nx - 1, 2):
        for copy in exchange(d):
            copy.wait_recv()
        strips_of(lax.rem(x - d + nx, nx))

    def wrapped(value, size):
        return jnp.where(value >= size, value - size, value)

    turns = [half] + [dz for step in range(1, half) for dz in (step, nz - step)]

    def others(body, sign):
        ends = {dz: wrapped(z + (dz if sign > 0 else nz - dz), nz) for dz in turns}

        def one(dx, carry):
            x2 = wrapped(x + (dx if sign > 0 else nx - dx), nx)
            for dz in turns:
                body(dx * nz + dz, x2, ends[dz])

            @pl.when(dx > 0)
            def _():
                body(dx * nz, x2, z)

            return carry

        lax.fori_loop(0, nx, one, 0)

    def go(slot, d, x2, z2):
        return remote(
            send_q.at[slot, x2 * nz + z2], rq.at[slot, me],
            go_s.at[slot, d - 1], go_r.at[slot, d - 1], x=x2, z=z2,
        )

    def go_row(d, x2, z2):
        return remote(
            send_row.at[x2 * nz + z2], rq_row.at[me], gor_s.at[d - 1], gor_r.at[d - 1], x=x2, z=z2
        )

    def picked(slot, other):
        b = source[2 * other + slot]
        return gq[lax.rem(b, nx), b // nx]

    def picked_rows(other):
        return jnp.concatenate(
            [
                rows[pl.ds(source[2 * other + slot], 1), :]
                for slot in range(2)
                for rows in (scale_rows, adam_rows)
            ],
            axis=0,
        )

    for slot in range(2):

        def send(d, x2, z2):
            other = x2 * nz + z2
            send_q[slot, other] = picked(slot, other)
            go(slot, d, x2, z2).start()
            if slot == 0:
                send_row[other] = picked_rows(other)
                go_row(d, x2, z2).start()

        others(send, 1)
        rq[slot, me] = picked(slot, me)
        if slot == 0:
            rq_row[me] = picked_rows(me)

    def reorder(r, carry):
        rows = pl.ds(pl.multiple_of(r * count, count), count)
        for k in range(block // lane):
            vbuf[k, rows, :] = vt[k, pl.ds(r, count, stride=strip), :]
        return carry

    lax.fori_loop(0, strip, reorder, 0)
    outs = [
        pltpu.make_async_copy(
            vbuf.at[k], var_new.at[:, k * lane : (k + 1) * lane], var_sem.at[1, k]
        )
        for k in range(block // lane)
    ]
    for copy in outs:
        copy.start()

    def back(slot, d, x2, z2):
        rows = pl.ds(pl.multiple_of((x2 * nz + z2) * strip, strip), strip)
        return remote(
            finished.at[slot, rows, :], ret.at[2 * me + slot],
            back_s.at[slot, d - 1], back_r.at[slot, d - 1], x=x2, z=z2,
        )

    fits = lax.rem(lax.broadcasted_iota(jnp.int32, (strip, width), 1), strip) == (
        lax.broadcasted_iota(jnp.int32, (strip, width), 0)
    )
    for slot in range(2):
        keep = used[slot]

        def decode(p):
            row = rq_row[p, 2 * slot : 2 * slot + 1]
            column = jnp.sum(jnp.where(fits, row, 0.0), axis=1, keepdims=True) * keep
            value = rq[slot, p].astype(jnp.float32) * column
            rows = pl.ds(pl.multiple_of(p * strip, strip), strip)
            owned_h[slot, rows, :], owned_l[slot, rows, :] = halves(value)

        def receive(d, x2, z2):
            if slot == 0:
                go_row(d, x2, z2).wait_recv()
            go(slot, d, x2, z2).wait_recv()
            decode(x2 * nz + z2)

        decode(me)
        others(receive, -1)
        total = jnp.sum(rq_row[:, 2 * slot + 1 : 2 * slot + 2, :], axis=0)

        def finish(rows, value):
            m_h[rows, :], m_l[rows, :] = halves(value)

        tiled_product(
            root_h.at[slot], root_l.at[slot], owned_h.at[slot], owned_l.at[slot], block, finish
        )

        def finish(rows, value):
            pre[rows, :] = value

        tiled_product(m_h, m_l, root_h.at[2 + slot], root_l.at[2 + slot], block, finish)
        value = pre[...]
        squares = jnp.sum(jnp.sum(value * value, axis=0, keepdims=True), axis=1, keepdims=True)
        mean_adam = jnp.sum(total, axis=1, keepdims=True) * (1.0 / (block * block))
        ratio = jnp.sqrt(mean_adam / (squares * (1.0 / (block * block)) + 1e-6))
        finished[slot] = (value * ratio).astype(jnp.bfloat16)

        others(lambda d, x2, z2: back(slot, d, x2, z2).start(), 1)
        rows = pl.ds(pl.multiple_of(me * strip, strip), strip)
        ret[2 * me + slot] = finished[slot, rows, :]

    tile = block // 2
    for slot in range(2):

        def outer(step, carry):
            rows = pl.ds(pl.multiple_of(step * tile, tile), tile)

            def pair(dims, left_high, left_low):
                def one(left, right):
                    return lax.dot_general(
                        left, right, (dims, ((), ())), preferred_element_type=jnp.float32
                    )

                total = one(left_high, owned_l[slot]) + one(left_low, owned_h[slot])
                return one(left_high, owned_h[slot]) + total

            left = pair(((1,), (1,)), owned_h[slot, rows, :], owned_l[slot, rows, :])
            sbuf[slot, rows, :] = 0.9 * sbuf[slot, rows, :] + 0.1 * left
            right = pair(((0,), (0,)), owned_h[slot, :, rows], owned_l[slot, :, rows])
            sbuf[2 + slot, rows, :] = 0.9 * sbuf[2 + slot, rows, :] + 0.1 * right
            return carry

        lax.fori_loop(0, 2, outer, 0)
        outs.append(pltpu.make_async_copy(sbuf.at[slot], left_new.at[slot], out_sem.at[slot]))
        outs.append(
            pltpu.make_async_copy(sbuf.at[2 + slot], right_new.at[slot], out_sem.at[2 + slot])
        )
        for copy in outs[-2:]:
            copy.start()

    for slot in range(2):
        others(lambda d, x2, z2: back(slot, d, x2, z2).wait_recv(), -1)

    def choose(b, carry):
        direction[b] = ret[targets[b]]
        return carry

    lax.fori_loop(0, count, choose, 0)

    for copy in outs:
        copy.wait()
    for slot in range(2):
        others(lambda d, x2, z2: go(slot, d, x2, z2).wait_send(), 1)
        others(lambda d, x2, z2: back(slot, d, x2, z2).wait_send(), 1)
    others(lambda d, x2, z2: go_row(d, x2, z2).wait_send(), 1)
    for copy in sends:
        copy.wait_send()
    for hop in range(1, half):
        for k in range(nx):
            for way in range(2):
                if hop < half - 1 or (k < nx // 2) == (way == 0):
                    ring(way, hop, k).wait_send()
    for k in range(1, nx):
        for d in range(1, ny):
            over_y(k, d).wait_send()
    for k in range(nx):
        for d in range(ny):
            if (k, d) != (0, 0):
                sibling(k, d).wait_send()


def shampoo(act, cot, stats_left, stats_right, variance, owners):
    tokens = act.shape[0]
    nx, nz, ny = lax.axis_size("x"), lax.axis_size("z"), lax.axis_size("y")
    block = stats_left.shape[-1]
    strip = block // (nx * nz)
    rows_z = nx * strip
    rows_i = 2 * ny
    sizes = (nx, nz, ny, block, strip, tokens, rows_i)
    half = nz // 2
    count, devices, width = rows_i * nx, nx * nz, rows_i * strip
    lane = min(block, 128)
    bf16, f32, i16 = jnp.bfloat16, jnp.float32, jnp.int16
    sem, vmem = pltpu.SemaphoreType.DMA, pltpu.VMEM
    square = (block, block)
    anywhere = pl.BlockSpec(memory_space=pl.ANY)
    scalars = pl.BlockSpec(memory_space=pltpu.SMEM)
    return pl.pallas_call(
        functools.partial(step_kernel, sizes),
        out_shape=(
            jax.ShapeDtypeStruct((count, strip, block), bf16),
            jax.ShapeDtypeStruct(stats_left.shape, f32),
            jax.ShapeDtypeStruct(stats_right.shape, f32),
            jax.ShapeDtypeStruct(variance.shape, f32),
        ),
        in_specs=[anywhere] * 5 + [scalars],
        out_specs=(pl.BlockSpec(memory_space=pltpu.VMEM),) + (anywhere,) * 3,
        scratch_shapes=[
            vmem((tokens, block), bf16),
            vmem((nz, rows_z, tokens), bf16),
            pltpu.SMEM((2 * devices,), jnp.int32),
            pltpu.SMEM((count,), jnp.int32),
            pltpu.SMEM((2,), f32),
            vmem((nz, nx, tokens, block), bf16),
            vmem((nz, nx, rows_i, rows_z, tokens), bf16),
            vmem((rows_i, rows_z, block), f32),
            vmem((4, block, block), f32),
            vmem((block // lane, strip * count, lane), f32),
            vmem((block // lane, strip * count, lane), f32),
            vmem(square, f32),
            vmem(square, f32),
        ]
        + [vmem(square, bf16)] * 6
        + [
            vmem((4, block, block), bf16),
            vmem((4, block, block), bf16),
            vmem((nx, rows_i, strip, block), i16),
            vmem((nx, 1, width), f32),
            vmem((nx, rows_i, strip, block), i16),
            vmem((nx, 1, width), f32),
            vmem((count, width), f32),
            vmem((count, width), f32),
            vmem((2, devices, strip, block), i16),
            vmem((devices, 4, width), f32),
            vmem((2, devices, strip, block), i16),
            vmem((devices, 4, width), f32),
            vmem((2, block, block), bf16),
            vmem((2, block, block), bf16),
            vmem(square, f32),
            vmem((2, block, block), bf16),
            vmem((2 * devices, strip, block), bf16),
            sem((2,)), sem((4,)), sem((4,)), sem((2, block // lane)),
            sem((nx - 1,)), sem((nx - 1,)),
            sem((nz - 1,)), sem((nz - 1,)),
            sem((2, half, nx)), sem((2, half, nx)),
            sem((nx - 1,)), sem((nx - 1,)),
            sem((nx, max(1, ny - 1))), sem((nx, max(1, ny - 1))),
            sem((nx, ny)), sem((nx, ny)),
        ]
        + [sem((nx - 1,))] * 4
        + [sem((2, devices - 1))] * 2
        + [sem((devices - 1,))] * 2
        + [sem((2, devices - 1))] * 2,
        compiler_params=pltpu.CompilerParams(
            collective_id=0, has_side_effects=True, vmem_limit_bytes=60 * 1024 * 1024
        ),
    )(act, cot, stats_left, stats_right, variance, owners)


def settle_kernel(
    left, right, variance, direction, left_out, right_out, variance_out, direction_out,
    held, held_rows, taken, spread, turned, in_sem, out_sem, way_sem,
):
    count, strip, block = direction.shape
    lane = spread.shape[2]
    pairs = [(left.at[k], held.at[k], left_out.at[k]) for k in range(2)]
    pairs += [(right.at[k], held.at[2 + k], right_out.at[k]) for k in range(2)]
    pairs += [(variance, held_rows, variance_out)]
    first = pltpu.make_async_copy(direction, taken, way_sem.at[0])
    last = pltpu.make_async_copy(turned, direction_out, way_sem.at[1])
    reads = [
        pltpu.make_async_copy(src, mid, in_sem.at[k]) for k, (src, mid, _) in enumerate(pairs)
    ]
    writes = [
        pltpu.make_async_copy(mid, dst, out_sem.at[k]) for k, (_, mid, dst) in enumerate(pairs)
    ]
    first.start()
    for copy in reads:
        copy.start()
    first.wait()
    value = taken[...].reshape(count * strip, block).astype(jnp.float32)
    for k in range(block // lane):
        spread[k] = value[:, k * lane : (k + 1) * lane]
    for r in range(strip):
        turned[r] = jnp.concatenate(
            [spread[k, pl.ds(r, count, stride=strip), :] for k in range(block // lane)], axis=1
        ).astype(turned.dtype)
    last.start()
    for read, write in zip(reads, writes):
        read.wait()
        write.start()
    for copy in writes:
        copy.wait()
    last.wait()


def settle(left, right, variance, direction):
    count, strip, block = direction.shape
    lane = min(block, 128)
    anywhere = pl.BlockSpec(memory_space=pl.ANY)
    vmem, sem = pltpu.VMEM, pltpu.SemaphoreType.DMA
    return pl.pallas_call(
        settle_kernel,
        out_shape=tuple(jax.ShapeDtypeStruct(a.shape, a.dtype) for a in (left, right, variance))
        + (jax.ShapeDtypeStruct((strip, count, block), direction.dtype),),
        in_specs=[anywhere] * 4,
        out_specs=(anywhere,) * 4,
        scratch_shapes=[
            vmem((4, block, block), left.dtype),
            vmem(variance.shape, variance.dtype),
            vmem(direction.shape, direction.dtype),
            vmem((block // lane, count * strip, lane), jnp.float32),
            vmem((strip, count, block), direction.dtype),
            sem((5,)), sem((5,)), sem((2,)),
        ],
        compiler_params=pltpu.CompilerParams(vmem_limit_bytes=60 * 1024 * 1024),
    )(left, right, variance, direction)


def per_device(activations, cotangents, owners, stats_left, stats_right, variance):
    block = activations.shape[1]
    count = owners.shape[0]
    strip = variance.shape[1]
    direction, left_new, right_new, var_new = shampoo(
        activations, cotangents, stats_left[0, 0], stats_right[0, 0],
        variance.reshape(strip * count, block), owners[:, 0],
    )
    left_new, right_new, var_new, direction = settle(left_new, right_new, var_new, direction)
    return (direction[None], left_new[None, None], right_new[None, None], var_new.reshape(variance.shape))


def solution(mesh):
    fine = Mesh(mesh.devices.reshape(X, Z, Y, 2), ("x", "z", "y", "c"))
    dp, mp = ("x", "z"), ("y", "c")

    def whole(activations, cotangents, owners, stats_left, stats_right, variance):
        return per_device(activations, cotangents, owners, stats_left, stats_right, variance)

    return jax.shard_map(
        whole,
        mesh=fine,
        in_specs=(
            P(dp, mp),
            P(dp, mp),
            P(mp, None),
            P(mp, dp, None, None, None),
            P(mp, dp, None, None, None),
            P(mp, dp, None, None),
        ),
        out_specs=(
            P(mp, dp, None, None),
            P(mp, dp, None, None, None),
            P(mp, dp, None, None, None),
            P(mp, dp, None, None),
        ),
        check_vma=False,
    )
```

```python
import functools

import jax
import jax.numpy as jnp
from jax import lax
from jax.experimental import pallas as pl
from jax.experimental.pallas import tpu as pltpu
from jax.sharding import Mesh, PartitionSpec as P

X, Z, Y = 4, 8, 4
MESH = pl.DeviceIdType.MESH
COEFFICIENTS = (
    25 / 16, -5 / 16 - 3125 / 4096, 3125 / 4096, -1250 / 4096, 250 / 4096, -25 / 4096, 1 / 4096,
)


def halves(value):
    high = value.astype(jnp.bfloat16)
    return high, (value - high.astype(jnp.float32)).astype(jnp.bfloat16)


def dot(left, right):
    return jnp.dot(left, right, preferred_element_type=jnp.float32)


def half_product(step, left_high, left_low, right_high, right_low, order, finish):
    tile = order // 2
    rows = pl.ds(step * tile, tile)
    if not isinstance(step, int):
        rows = pl.ds(pl.multiple_of(step * tile, tile), tile)
    high, low = left_high[rows, :], left_low[rows, :]
    total = dot(high, right_low[...]) + dot(low, right_high[...])
    finish(rows, dot(high, right_high[...]) + total)


def tiled_product(left_high, left_low, right_high, right_low, order, finish):
    def one(step, carry):
        half_product(step, left_high, left_low, right_high, right_low, order, finish)
        return carry

    lax.fori_loop(0, 2, one, 0)


def step_kernel(
    sizes, act, cot, stats_left, stats_right, variance, owners,
    direction, left_new, right_new, var_new,
    act_in, act_t, source, targets, used, cbuf, abuf, grad, sbuf, vbuf, vt, matrix, m2, m_h, m_l, m2_h, m2_l, w_h, w_l, root_h, root_l,
    gsend, gsend_row, gq_first, gq_second, gq_row, scale_rows, adam_rows, send_q, send_both, send_row, rq, rq_both,
    rq_row,
    owned_h, owned_l, pre, finished, ret,
    own_sem, stat_sem, out_sem, var_sem, c1_s, c1_r, a1_s, a1_r, zr_s, zr_r, a2_s, a2_r,
    y_s, y_r, sib_s, sib_r, ex_s, ex_r, exr_s, exr_r, go_s, go_r, both_s, both_r,
    gor_s, gor_r, back_s, back_r,
):
    nx, nz, ny, block, strip, tokens, rows_i = sizes
    count, devices, width = rows_i * nx, nx * nz, rows_i * strip
    lane = vbuf.shape[2]
    wide = block // 2
    gq = (gq_first, gq_second)
    half = nz // 2
    x, z = lax.axis_index("x"), lax.axis_index("z")
    y, c = lax.axis_index("y"), lax.axis_index("c")
    mine = 2 * y + c
    me = x * nz + z

    def remote(src, dst, send, recv, **where):
        return pltpu.make_async_remote_copy(
            src_ref=src, dst_ref=dst, send_sem=send, recv_sem=recv,
            device_id=where, device_id_type=MESH,
        )

    barrier = pltpu.get_barrier_semaphore()

    partners = [{"x": lax.rem(x + d, nx)} for d in range(1, nx)]
    partners += [{"z": lax.rem(z + d, nz)} for d in range(1, nz)]
    partners += [{"y": lax.rem(y + d, ny)} for d in range(1, ny)]
    partners += [{"c": 1 - c}]
    for partner in partners:
        pl.semaphore_signal(barrier, inc=1, device_id=partner, device_id_type=MESH)
    loads = [
        pltpu.make_async_copy(ref.at[slot], sbuf.at[2 * side + slot], stat_sem.at[2 * side + slot])
        for side, ref in enumerate((stats_left, stats_right))
        for slot in range(2)
    ]

    def columns(j, p):
        return cot.at[:, pl.ds(pl.multiple_of(j * block + p * wide, wide), wide)]

    own_c = [
        pltpu.make_async_copy(columns(x, p), cbuf.at[p, z, x], own_sem.at[2 * p]) for p in range(2)
    ]
    act_load = pltpu.make_async_copy(act, act_in, own_sem.at[1])
    loads += [
        pltpu.make_async_copy(
            variance.at[:, k * lane : (k + 1) * lane], vbuf.at[k], var_sem.at[0, k]
        )
        for k in range(block // lane)
    ]
    act_load.start()
    for copy in own_c:
        copy.start()
    for load in loads:
        load.start()

    pl.semaphore_wait(barrier, len(partners))

    sends = []

    def launch(copy):
        copy.start()
        sends.append(copy)

    def c1(d, p):
        j = lax.rem(x + d, nx)
        return remote(
            columns(j, p), cbuf.at[p, z, x], c1_s.at[p, d - 1], c1_r.at[p, d - 1], x=j
        )

    def a1(d):
        z2 = lax.rem(z + d, nz)
        return remote(act_t.at[z2], abuf.at[z, x, mine], a1_s.at[d - 1], a1_r.at[d - 1], z=z2)

    def ring(way, hop, k, p, held=None):
        x2 = lax.rem(x - k + nx, nx)
        step = 1 if way == 0 else nz - 1
        origin = lax.rem(z - hop + nz, nz) if way == 0 else lax.rem(z + hop, nz)
        part = cbuf.at[p, origin, x2]
        return remote(
            part if held is None else held, part, zr_s.at[p, way, hop, k], zr_r.at[p, way, hop, k], z=lax.rem(z + step, nz)
        )

    def a2(d):
        part = abuf.at[:, x, mine]
        return remote(part, part, a2_s.at[d - 1], a2_r.at[d - 1], x=lax.rem(x + d, nx))

    def over_y(k, d):
        part = abuf.at[:, lax.rem(x - k + nx, nx), mine]
        return remote(
            part, part, y_s.at[k, d - 1], y_r.at[k, d - 1], y=lax.rem(y + d, ny)
        )

    def sibling(k, d):
        part = abuf.at[:, lax.rem(x - k + nx, nx), 2 * lax.rem(y - d + ny, ny) + c]
        return remote(part, part, sib_s.at[k, d], sib_r.at[k, d], c=1 - c)

    near, far_x = [1, nx - 1], list(range(2, nx - 1))
    for d in near:
        c1(d, 0).start()
    for way in range(2):
        launch(ring(way, 0, 0, 0, columns(x, 0)))
    act_load.wait()
    turned = act_in[...].T
    for x2 in range(nx):
        for z2 in range(nz):
            first = (x2 * nz + z2) * strip
            act_t[z2, x2 * strip : (x2 + 1) * strip, :] = turned[first : first + strip]
    abuf[z, x, mine] = act_t[z]
    for d in range(1, nz):
        launch(a1(d))
    for way in range(2):
        launch(ring(way, 0, 0, 1, columns(x, 1)))
    for d in near:
        c1(d, 0).wait_send()
    for d in far_x:
        launch(c1(d, 0))
    for d in near + far_x:
        launch(c1(d, 1))
    for p in range(2):
        for k in near + far_x:
            c1(k, p).wait_recv()
            for way in range(2):
                launch(ring(way, 0, k, p))
    for d in range(1, nz):
        a1(d).wait_recv()
    for d in range(1, nx):
        launch(a2(d))
    for d in range(1, ny):
        launch(over_y(0, d))
    launch(sibling(0, 0))
    for copy in own_c:
        copy.wait()
    for load in loads:
        load.wait()

    def find_blocks(owner, carry):
        low, high = jnp.int32(count), jnp.int32(0)
        for b in range(count):
            hit = owners[b] == owner
            low = jnp.where(hit, jnp.minimum(low, b), low)
            high = jnp.where(hit, b, high)
        source[2 * owner] = jnp.where(low == count, 0, low)
        source[2 * owner + 1] = high
        return carry

    def find_target(b, carry):
        earlier = jnp.int32(0)
        for c2 in range(count):
            hit = jnp.logical_and(owners[c2] == owners[b], c2 < b)
            earlier = jnp.where(hit, earlier + 1, earlier)
        targets[b] = 2 * owners[b] + earlier
        return carry

    held = jnp.int32(0)
    for b in range(count):
        held = jnp.where(owners[b] == me, held + 1, held)
    for slot in range(2):
        used[slot] = jnp.where(held > slot, 1.0, 0.0)

    items = nx * (ny - 1)

    def shard(origin, p, rows=None):
        parts = []
        for x2 in range(nx):
            if rows is None:
                piece = abuf[origin, x2]
            else:
                piece = abuf[origin, x2, :, rows, :]
            parts.append(piece.reshape(-1, tokens))
        left = jnp.concatenate(parts, axis=1)
        return dot(left, cbuf[p, origin].reshape(nx * tokens, wide))

    diagonal = lax.broadcasted_iota(jnp.int32, (width, width), 0) == lax.broadcasted_iota(
        jnp.int32, (width, width), 1
    )

    def exchange(d, p):
        j = lax.rem(x + d, nx)
        return (
            remote(gsend.at[p, j], gq[p].at[x], ex_s.at[p, d - 1], ex_r.at[p, d - 1], x=j),
            remote(
                gsend_row.at[p, j], gq_row.at[p, x], exr_s.at[p, d - 1], exr_r.at[p, d - 1], x=j
            ),
        )

    def finish_columns(p):
        grad[...] = shard(z, p).reshape(grad.shape)

        def add(d, carry):
            origin = lax.rem(z + d + (d >= half).astype(jnp.int32), nz)
            grad[...] += shard(origin, p).reshape(grad.shape)
            return carry

        lax.fori_loop(1, nz - 1, add, 0)
        for k in range(nx):
            ring(0 if k < nx // 2 else 1, half - 1, k, p).wait_recv()
        far = lax.rem(z + half, nz)
        for d in [2, 1, nx - 1, 0]:
            j = lax.rem(x + d, nx)
            rows = pl.ds(pl.multiple_of(j * strip, strip), strip)
            value = grad[:, rows, :].reshape(width, wide) + shard(far, p, rows)
            top = jnp.maximum(jnp.max(jnp.abs(value), axis=1, keepdims=True), 1e-30)
            coded = jnp.round(value * (32767.0 / top)).astype(jnp.int32).astype(jnp.int16)
            row = jnp.sum(jnp.where(diagonal, top * (1.0 / 32767.0), 0.0), axis=0, keepdims=True)
            if d:
                gsend[p, j] = coded.reshape(rows_i, strip, wide)
                gsend_row[p, j] = row
                for copy in exchange(d, p):
                    copy.start()
            else:
                gq[p][x] = coded.reshape(rows_i, strip, wide)
                gq_row[p, x] = row

    def one_matrix(q, carry):
        p = (q >= 2).astype(jnp.int32)
        for u in range(6):
            t, tile = u // 2, u % 2
            n = 6 * q + u
            inner_n = n - 12 * p
            hop, place = inner_n // nx + 1, lax.rem(inner_n, nx)
            k = jnp.where(place == 2, nx - 1, jnp.where(place == 3, 2, place))
            ring(0, hop - 1, k, p).wait_recv()
            ring(1, hop - 1, k, p).wait_recv()
            inner = hop < half - 1

            @pl.when(jnp.logical_or(inner, place < nx // 2))
            def _():
                ring(0, hop, k, p).start()

            @pl.when(jnp.logical_or(inner, place >= nx // 2))
            def _():
                ring(1, hop, k, p).start()

            if u + 1 < nx:

                @pl.when(q == 0)
                def _():
                    a2(u + 1).wait_recv()
                    for d in range(1, ny):
                        over_y(u + 1, d).start()
                    sibling(u + 1, 0).start()

            item = n - 5
            if ny > 1:

                @pl.when(jnp.logical_and(item >= 0, item < items))
                def _():
                    k2, d2 = item // (ny - 1), lax.rem(item, ny - 1) + 1
                    over_y(k2, d2).wait_recv()
                    sibling(k2, d2).start()

            if u == 2:

                @pl.when(q == 3)
                def _():
                    for k3 in range(nx):
                        for d in range(ny):
                            sibling(k3, d).wait_recv()
                    finish_columns(0)

            each = -(-devices // 24)
            lax.fori_loop(n * each, jnp.minimum(n * each + each, devices), find_blocks, 0)
            each = -(-count // 24)
            lax.fori_loop(n * each, jnp.minimum(n * each + each, count), find_target, 0)

            if t == 0:
                if tile == 0:
                    stat = sbuf[q]
                    bound = jnp.max(
                        jnp.sum(jnp.abs(stat), axis=1, keepdims=True), axis=0, keepdims=True
                    )
                    value = stat * (1.0 / bound)
                    matrix[...] = value
                    m_h[...], m_l[...] = halves(value)

                def finish(rows, value):
                    m2[rows, :] = value
                    m2_h[rows, :], m2_l[rows, :] = halves(value)
                    w_h[rows, :], w_l[rows, :] = halves(
                        COEFFICIENTS[5] * matrix[rows, :] + COEFFICIENTS[6] * value
                    )

                half_product(tile, m_h, m_l, m_h, m_l, block, finish)
            elif t == 1:

                def finish(rows, value):
                    value += COEFFICIENTS[3] * matrix[rows, :] + COEFFICIENTS[4] * m2[rows, :]
                    m_h[rows, :], m_l[rows, :] = halves(value)

                half_product(tile, m2_h, m2_l, w_h, w_l, block, finish)
            else:

                def finish(rows, value):
                    value += COEFFICIENTS[1] * matrix[rows, :] + COEFFICIENTS[2] * m2[rows, :]
                    ids = lax.broadcasted_iota(jnp.int32, value.shape, 0) + rows.start
                    columns = lax.broadcasted_iota(jnp.int32, value.shape, 1)
                    value += jnp.where(ids == columns, COEFFICIENTS[0], 0.0)
                    root_h[q, rows, :], root_l[q, rows, :] = halves(value)

                half_product(tile, m2_h, m2_l, m_h, m_l, block, finish)

            each = -(-count // 24)
            for extra in range(each):
                b = n * each + extra

                @pl.when(b < count)
                def _():
                    rows = pl.ds(pl.multiple_of(b * strip, strip), strip)
                    for k in range(block // lane):
                        vt[k, rows, :] = vbuf[k, pl.ds(b, strip, stride=count), :]
        return carry

    lax.fori_loop(0, 4, one_matrix, 0)

    lanes = lax.broadcasted_iota(jnp.int32, (1, width), 1)

    def strips_of(j, p):
        row = gq_row[p, j]
        column = jnp.sum(jnp.where(diagonal, row, 0.0), axis=1, keepdims=True)
        chunks = range(p * wide // lane, (p + 1) * wide // lane)
        for i in range(rows_i):
            b = i * nx + j
            value = gq[p][j, i].astype(jnp.float32) * column[i * strip : (i + 1) * strip]
            square = value * value
            rows = pl.ds(pl.multiple_of(b * strip, strip), strip)
            old = jnp.concatenate([vt[k, rows, :] for k in chunks], axis=1)
            fresh = 0.9 * old + 0.1 * square
            for at, k in enumerate(chunks):
                vt[k, rows, :] = fresh[:, at * lane : (at + 1) * lane]
            total = jnp.sum(square / fresh, axis=0, keepdims=True)
            folded = sum(total[:, k * width : (k + 1) * width] for k in range(wide // width))
            inside = jnp.logical_and(lanes >= i * strip, lanes < (i + 1) * strip)
            adam_rows[p, pl.ds(b, 1), :] = folded
            scale_rows[p, pl.ds(b, 1), :] = jnp.where(inside, row, 0.0)

    def strips_half(p):
        strips_of(x, p)
        for d in (1, nx - 1, 2):
            for copy in exchange(d, p):
                copy.wait_recv()
            strips_of(lax.rem(x - d + nx, nx), p)

    def wrapped(value, size):
        return jnp.where(value >= size, value - size, value)

    turns = [half] + [dz for step in range(1, half) for dz in (step, nz - step)]

    def others(body, sign):
        ends = {dz: wrapped(z + (dz if sign > 0 else nz - dz), nz) for dz in turns}

        def one(dx, carry):
            x2 = wrapped(x + (dx if sign > 0 else nx - dx), nx)
            for dz in turns:
                body(dx * nz + dz, x2, ends[dz])

            @pl.when(dx > 0)
            def _():
                body(dx * nz, x2, z)

            return carry

        lax.fori_loop(0, nx, one, 0)

    def go(slot, d, x2, z2):
        return remote(
            send_q.at[slot, x2 * nz + z2], rq.at[slot, me],
            go_s.at[slot, d - 1], go_r.at[slot, d - 1], x=x2, z=z2,
        )

    def go_both(d, x2, z2):
        return remote(
            send_both.at[x2 * nz + z2], rq_both.at[me],
            both_s.at[d - 1], both_r.at[d - 1], x=x2, z=z2,
        )

    def go_row(d, x2, z2):
        return remote(
            send_row.at[x2 * nz + z2], rq_row.at[me], gor_s.at[d - 1], gor_r.at[d - 1], x=x2, z=z2
        )

    def picked(slot, other, p):
        b = source[2 * other + slot]
        return gq[p][lax.rem(b, nx), b // nx]

    def picked_rows(other):
        return jnp.concatenate(
            [
                rows[p, pl.ds(source[2 * other + slot], 1), :]
                for slot in range(2)
                for rows in (scale_rows, adam_rows)
                for p in range(2)
            ],
            axis=0,
        )

    strips_half(0)

    def send_first(d, x2, z2):
        other = x2 * nz + z2
        for slot in range(2):
            send_both[other, slot] = picked(slot, other, 0)
        go_both(d, x2, z2).start()

    others(send_first, 1)
    for slot in range(2):
        rq_both[me, slot] = picked(slot, me, 0)
    finish_columns(1)
    strips_half(1)
    for slot in range(2):

        def send(d, x2, z2):
            other = x2 * nz + z2
            send_q[slot, other] = picked(slot, other, 1)
            if slot == 0:
                send_row[other] = picked_rows(other)
                go_row(d, x2, z2).start()
            go(slot, d, x2, z2).start()

        others(send, 1)
        rq[slot, me] = picked(slot, me, 1)
        if slot == 0:
            rq_row[me] = picked_rows(me)

    def reorder(r, carry):
        rows = pl.ds(pl.multiple_of(r * count, count), count)
        for k in range(block // lane):
            vbuf[k, rows, :] = vt[k, pl.ds(r, count, stride=strip), :]
        return carry

    lax.fori_loop(0, strip, reorder, 0)
    outs = [
        pltpu.make_async_copy(
            vbuf.at[k], var_new.at[:, k * lane : (k + 1) * lane], var_sem.at[1, k]
        )
        for k in range(block // lane)
    ]
    for copy in outs:
        copy.start()

    def back(slot, d, x2, z2):
        rows = pl.ds(pl.multiple_of((x2 * nz + z2) * strip, strip), strip)
        return remote(
            finished.at[slot, rows, :], ret.at[2 * me + slot],
            back_s.at[slot, d - 1], back_r.at[slot, d - 1], x=x2, z=z2,
        )

    fits = lax.rem(lax.broadcasted_iota(jnp.int32, (strip, width), 1), strip) == (
        lax.broadcasted_iota(jnp.int32, (strip, width), 0)
    )
    for slot in range(2):
        keep = used[slot]

        def decode(other):
            values = []
            for p, data in enumerate((rq_both[other, slot], rq[slot, other])):
                row = rq_row[other, 4 * slot + p : 4 * slot + p + 1]
                column = jnp.sum(jnp.where(fits, row, 0.0), axis=1, keepdims=True) * keep
                values.append(data.astype(jnp.float32) * column)
            rows = pl.ds(pl.multiple_of(other * strip, strip), strip)
            value = jnp.concatenate(values, axis=1)
            owned_h[slot, rows, :], owned_l[slot, rows, :] = halves(value)

        def receive(d, x2, z2):
            if slot == 0:
                go_both(d, x2, z2).wait_recv()
                go_row(d, x2, z2).wait_recv()
            go(slot, d, x2, z2).wait_recv()
            decode(x2 * nz + z2)

        decode(me)
        others(receive, -1)
        total = jnp.sum(
            rq_row[:, 4 * slot + 2 : 4 * slot + 3, :] + rq_row[:, 4 * slot + 3 : 4 * slot + 4, :],
            axis=0,
        )

        def finish(rows, value):
            m_h[rows, :], m_l[rows, :] = halves(value)

        tiled_product(
            root_h.at[slot], root_l.at[slot], owned_h.at[slot], owned_l.at[slot], block, finish
        )

        def finish(rows, value):
            pre[rows, :] = value

        tiled_product(m_h, m_l, root_h.at[2 + slot], root_l.at[2 + slot], block, finish)
        value = pre[...]
        squares = jnp.sum(jnp.sum(value * value, axis=0, keepdims=True), axis=1, keepdims=True)
        mean_adam = jnp.sum(total, axis=1, keepdims=True) * (1.0 / (block * block))
        ratio = jnp.sqrt(mean_adam / (squares * (1.0 / (block * block)) + 1e-6))
        finished[slot] = (value * ratio).astype(jnp.bfloat16)

        others(lambda d, x2, z2: back(slot, d, x2, z2).start(), 1)
        rows = pl.ds(pl.multiple_of(me * strip, strip), strip)
        ret[2 * me + slot] = finished[slot, rows, :]

    tile = block // 2
    for slot in range(2):

        def outer(step, carry):
            rows = pl.ds(pl.multiple_of(step * tile, tile), tile)

            def pair(dims, left_high, left_low):
                def one(left, right):
                    return lax.dot_general(
                        left, right, (dims, ((), ())), preferred_element_type=jnp.float32
                    )

                total = one(left_high, owned_l[slot]) + one(left_low, owned_h[slot])
                return one(left_high, owned_h[slot]) + total

            left = pair(((1,), (1,)), owned_h[slot, rows, :], owned_l[slot, rows, :])
            sbuf[slot, rows, :] = 0.9 * sbuf[slot, rows, :] + 0.1 * left
            right = pair(((0,), (0,)), owned_h[slot, :, rows], owned_l[slot, :, rows])
            sbuf[2 + slot, rows, :] = 0.9 * sbuf[2 + slot, rows, :] + 0.1 * right
            return carry

        lax.fori_loop(0, 2, outer, 0)
        outs.append(pltpu.make_async_copy(sbuf.at[slot], left_new.at[slot], out_sem.at[slot]))
        outs.append(
            pltpu.make_async_copy(sbuf.at[2 + slot], right_new.at[slot], out_sem.at[2 + slot])
        )
        for copy in outs[-2:]:
            copy.start()

    for slot in range(2):
        others(lambda d, x2, z2: back(slot, d, x2, z2).wait_recv(), -1)

    def choose(b, carry):
        direction[b] = ret[targets[b]]
        return carry

    lax.fori_loop(0, count, choose, 0)

    for copy in outs:
        copy.wait()
    for slot in range(2):
        others(lambda d, x2, z2: go(slot, d, x2, z2).wait_send(), 1)
        others(lambda d, x2, z2: back(slot, d, x2, z2).wait_send(), 1)
    others(lambda d, x2, z2: go_row(d, x2, z2).wait_send(), 1)
    others(lambda d, x2, z2: go_both(d, x2, z2).wait_send(), 1)
    for p in range(2):
        for d in range(1, nx):
            for copy in exchange(d, p):
                copy.wait_send()
    for copy in sends:
        copy.wait_send()
    for p in range(2):
        for hop in range(1, half):
            for k in range(nx):
                for way in range(2):
                    if hop < half - 1 or (k < nx // 2) == (way == 0):
                        ring(way, hop, k, p).wait_send()
    for k in range(1, nx):
        for d in range(1, ny):
            over_y(k, d).wait_send()
    for k in range(nx):
        for d in range(ny):
            if (k, d) != (0, 0):
                sibling(k, d).wait_send()


def shampoo(act, cot, stats_left, stats_right, variance, owners):
    tokens = act.shape[0]
    nx, nz, ny = lax.axis_size("x"), lax.axis_size("z"), lax.axis_size("y")
    block = stats_left.shape[-1]
    strip = block // (nx * nz)
    rows_z = nx * strip
    rows_i = 2 * ny
    sizes = (nx, nz, ny, block, strip, tokens, rows_i)
    half = nz // 2
    count, devices, width = rows_i * nx, nx * nz, rows_i * strip
    lane = min(block // 2, 128)
    wide = block // 2
    bf16, f32, i16 = jnp.bfloat16, jnp.float32, jnp.int16
    sem, vmem = pltpu.SemaphoreType.DMA, pltpu.VMEM
    square = (block, block)
    anywhere = pl.BlockSpec(memory_space=pl.ANY)
    scalars = pl.BlockSpec(memory_space=pltpu.SMEM)
    return pl.pallas_call(
        functools.partial(step_kernel, sizes),
        out_shape=(
            jax.ShapeDtypeStruct((count, strip, block), bf16),
            jax.ShapeDtypeStruct(stats_left.shape, f32),
            jax.ShapeDtypeStruct(stats_right.shape, f32),
            jax.ShapeDtypeStruct(variance.shape, f32),
        ),
        in_specs=[anywhere] * 5 + [scalars],
        out_specs=(pl.BlockSpec(memory_space=pltpu.VMEM),) + (anywhere,) * 3,
        scratch_shapes=[
            vmem((tokens, block), bf16),
            vmem((nz, rows_z, tokens), bf16),
            pltpu.SMEM((2 * devices,), jnp.int32),
            pltpu.SMEM((count,), jnp.int32),
            pltpu.SMEM((2,), f32),
            vmem((2, nz, nx, tokens, wide), bf16),
            vmem((nz, nx, rows_i, rows_z, tokens), bf16),
            vmem((rows_i, rows_z, wide), f32),
            vmem((4, block, block), f32),
            vmem((block // lane, strip * count, lane), f32),
            vmem((block // lane, strip * count, lane), f32),
            vmem(square, f32),
            vmem(square, f32),
        ]
        + [vmem(square, bf16)] * 6
        + [
            vmem((4, block, block), bf16),
            vmem((4, block, block), bf16),
            vmem((2, nx, rows_i, strip, wide), i16),
            vmem((2, nx, 1, width), f32),
            vmem((nx, rows_i, strip, wide), i16),
            vmem((nx, rows_i, strip, wide), i16),
            vmem((2, nx, 1, width), f32),
            vmem((2, count, width), f32),
            vmem((2, count, width), f32),
            vmem((2, devices, strip, wide), i16),
            vmem((devices, 2, strip, wide), i16),
            vmem((devices, 8, width), f32),
            vmem((2, devices, strip, wide), i16),
            vmem((devices, 2, strip, wide), i16),
            vmem((devices, 8, width), f32),
            vmem((2, block, block), bf16),
            vmem((2, block, block), bf16),
            vmem(square, f32),
            vmem((2, block, block), bf16),
            vmem((2 * devices, strip, block), bf16),
            sem((3,)), sem((4,)), sem((4,)), sem((2, block // lane)),
            sem((2, nx - 1)), sem((2, nx - 1)),
            sem((nz - 1,)), sem((nz - 1,)),
            sem((2, 2, half, nx)), sem((2, 2, half, nx)),
            sem((nx - 1,)), sem((nx - 1,)),
            sem((nx, max(1, ny - 1))), sem((nx, max(1, ny - 1))),
            sem((nx, ny)), sem((nx, ny)),
        ]
        + [sem((2, nx - 1))] * 4
        + [sem((2, devices - 1))] * 2
        + [sem((devices - 1,))] * 4
        + [sem((2, devices - 1))] * 2,
        compiler_params=pltpu.CompilerParams(
            collective_id=0, has_side_effects=True, vmem_limit_bytes=60 * 1024 * 1024
        ),
    )(act, cot, stats_left, stats_right, variance, owners)


def settle_kernel(
    left, right, variance, direction, left_out, right_out, variance_out, direction_out,
    held, held_rows, taken, spread, turned, in_sem, out_sem, way_sem,
):
    count, strip, block = direction.shape
    lane = spread.shape[2]
    pairs = [(left.at[k], held.at[k], left_out.at[k]) for k in range(2)]
    pairs += [(right.at[k], held.at[2 + k], right_out.at[k]) for k in range(2)]
    pairs += [(variance, held_rows, variance_out)]
    first = pltpu.make_async_copy(direction, taken, way_sem.at[0])
    last = pltpu.make_async_copy(turned, direction_out, way_sem.at[1])
    reads = [
        pltpu.make_async_copy(src, mid, in_sem.at[k]) for k, (src, mid, _) in enumerate(pairs)
    ]
    writes = [
        pltpu.make_async_copy(mid, dst, out_sem.at[k]) for k, (_, mid, dst) in enumerate(pairs)
    ]
    first.start()
    for copy in reads:
        copy.start()
    first.wait()
    value = taken[...].reshape(count * strip, block).astype(jnp.float32)
    for k in range(block // lane):
        spread[k] = value[:, k * lane : (k + 1) * lane]
    for r in range(strip):
        turned[r] = jnp.concatenate(
            [spread[k, pl.ds(r, count, stride=strip), :] for k in range(block // lane)], axis=1
        ).astype(turned.dtype)
    last.start()
    for read, write in zip(reads, writes):
        read.wait()
        write.start()
    for copy in writes:
        copy.wait()
    last.wait()


def settle(left, right, variance, direction):
    count, strip, block = direction.shape
    lane = min(block, 128)
    anywhere = pl.BlockSpec(memory_space=pl.ANY)
    vmem, sem = pltpu.VMEM, pltpu.SemaphoreType.DMA
    return pl.pallas_call(
        settle_kernel,
        out_shape=tuple(jax.ShapeDtypeStruct(a.shape, a.dtype) for a in (left, right, variance))
        + (jax.ShapeDtypeStruct((strip, count, block), direction.dtype),),
        in_specs=[anywhere] * 4,
        out_specs=(anywhere,) * 4,
        scratch_shapes=[
            vmem((4, block, block), left.dtype),
            vmem(variance.shape, variance.dtype),
            vmem(direction.shape, direction.dtype),
            vmem((block // lane, count * strip, lane), jnp.float32),
            vmem((strip, count, block), direction.dtype),
            sem((5,)), sem((5,)), sem((2,)),
        ],
        compiler_params=pltpu.CompilerParams(vmem_limit_bytes=60 * 1024 * 1024),
    )(left, right, variance, direction)


def per_device(activations, cotangents, owners, stats_left, stats_right, variance):
    block = activations.shape[1]
    count = owners.shape[0]
    strip = variance.shape[1]
    direction, left_new, right_new, var_new = shampoo(
        activations, cotangents, stats_left[0, 0], stats_right[0, 0],
        variance.reshape(strip * count, block), owners[:, 0],
    )
    left_new, right_new, var_new, direction = settle(left_new, right_new, var_new, direction)
    return (direction[None], left_new[None, None], right_new[None, None], var_new.reshape(variance.shape))


def solution(mesh):
    fine = Mesh(mesh.devices.reshape(X, Z, Y, 2), ("x", "z", "y", "c"))
    dp, mp = ("x", "z"), ("y", "c")

    def whole(activations, cotangents, owners, stats_left, stats_right, variance):
        return per_device(activations, cotangents, owners, stats_left, stats_right, variance)

    return jax.shard_map(
        whole,
        mesh=fine,
        in_specs=(
            P(dp, mp),
            P(dp, mp),
            P(mp, None),
            P(mp, dp, None, None, None),
            P(mp, dp, None, None, None),
            P(mp, dp, None, None),
        ),
        out_specs=(
            P(mp, dp, None, None),
            P(mp, dp, None, None, None),
            P(mp, dp, None, None, None),
            P(mp, dp, None, None),
        ),
        check_vma=False,
    )
```

```python
import functools

import jax
import jax.numpy as jnp
from jax import lax
from jax.experimental import pallas as pl
from jax.experimental.pallas import tpu as pltpu
from jax.sharding import Mesh, PartitionSpec as P

X, Z, Y = 4, 8, 4
MESH = pl.DeviceIdType.MESH
COEFFICIENTS = (
    25 / 16, -5 / 16 - 3125 / 4096, 3125 / 4096, -1250 / 4096, 250 / 4096, -25 / 4096, 1 / 4096,
)


def halves(value):
    high = value.astype(jnp.bfloat16)
    return high, (value - high.astype(jnp.float32)).astype(jnp.bfloat16)


def dot(left, right):
    return jnp.dot(left, right, preferred_element_type=jnp.float32)


def half_product(step, left_high, left_low, right_high, right_low, order, finish):
    tile = order // 2
    rows = pl.ds(step * tile, tile)
    if not isinstance(step, int):
        rows = pl.ds(pl.multiple_of(step * tile, tile), tile)
    high, low = left_high[rows, :], left_low[rows, :]
    total = dot(high, right_low[...]) + dot(low, right_high[...])
    finish(rows, dot(high, right_high[...]) + total)


def tiled_product(left_high, left_low, right_high, right_low, order, finish):
    def one(step, carry):
        half_product(step, left_high, left_low, right_high, right_low, order, finish)
        return carry

    lax.fori_loop(0, 2, one, 0)


def step_kernel(
    sizes, act, cot, stats_left, stats_right, variance, owners,
    direction, left_new, right_new, var_new,
    act_in, act_t, source, targets, used, cbuf, abuf, grad, sbuf, vbuf, vt, matrix, m2, m_h, m_l, m2_h, m2_l, w_h, w_l, root_h, root_l,
    gsend, gsend_row, gq_first, gq_second, gq_row, scale_rows, send_q, send_both, send_row, rq, rq_both,
    rq_row,
    owned_h, owned_l, pre, finished, ret,
    own_sem, stat_sem, out_sem, var_sem, c1_s, c1_r, a1_s, a1_r, zr_s, zr_r, a2_s, a2_r,
    y_s, y_r, sib_s, sib_r, ex_s, ex_r, exr_s, exr_r, go_s, go_r, both_s, both_r,
    gor_s, gor_r, back_s, back_r,
):
    nx, nz, ny, block, strip, tokens, rows_i = sizes
    count, devices, width = rows_i * nx, nx * nz, rows_i * strip
    lane = vbuf.shape[2]
    wide = block // 2
    gq = (gq_first, gq_second)
    half = nz // 2
    x, z = lax.axis_index("x"), lax.axis_index("z")
    y, c = lax.axis_index("y"), lax.axis_index("c")
    mine = 2 * y + c
    me = x * nz + z

    def remote(src, dst, send, recv, **where):
        return pltpu.make_async_remote_copy(
            src_ref=src, dst_ref=dst, send_sem=send, recv_sem=recv,
            device_id=where, device_id_type=MESH,
        )

    barrier = pltpu.get_barrier_semaphore()

    partners = [{"x": lax.rem(x + d, nx)} for d in range(1, nx)]
    partners += [{"z": lax.rem(z + d, nz)} for d in range(1, nz)]
    partners += [{"y": lax.rem(y + d, ny)} for d in range(1, ny)]
    partners += [{"c": 1 - c}]
    for partner in partners:
        pl.semaphore_signal(barrier, inc=1, device_id=partner, device_id_type=MESH)
    loads = [
        pltpu.make_async_copy(ref.at[slot], sbuf.at[2 * side + slot], stat_sem.at[2 * side + slot])
        for side, ref in enumerate((stats_left, stats_right))
        for slot in range(2)
    ]

    def columns(j, p):
        return cot.at[:, pl.ds(pl.multiple_of(j * block + p * wide, wide), wide)]

    own_c = [
        pltpu.make_async_copy(columns(x, p), cbuf.at[p, z, x], own_sem.at[2 * p]) for p in range(2)
    ]
    act_load = pltpu.make_async_copy(act, act_in, own_sem.at[1])
    loads += [
        pltpu.make_async_copy(
            variance.at[:, k * lane : (k + 1) * lane], vbuf.at[k], var_sem.at[0, k]
        )
        for k in range(block // lane)
    ]
    act_load.start()
    for copy in own_c:
        copy.start()
    for load in loads:
        load.start()

    pl.semaphore_wait(barrier, len(partners))

    sends = []

    def launch(copy):
        copy.start()
        sends.append(copy)

    def c1(d, p):
        j = lax.rem(x + d, nx)
        return remote(
            columns(j, p), cbuf.at[p, z, x], c1_s.at[p, d - 1], c1_r.at[p, d - 1], x=j
        )

    def a1(d):
        z2 = lax.rem(z + d, nz)
        return remote(act_t.at[z2], abuf.at[z, x, mine], a1_s.at[d - 1], a1_r.at[d - 1], z=z2)

    def ring(way, hop, k, p, held=None):
        x2 = lax.rem(x - k + nx, nx)
        step = 1 if way == 0 else nz - 1
        origin = lax.rem(z - hop + nz, nz) if way == 0 else lax.rem(z + hop, nz)
        part = cbuf.at[p, origin, x2]
        return remote(
            part if held is None else held, part, zr_s.at[p, way, hop, k], zr_r.at[p, way, hop, k], z=lax.rem(z + step, nz)
        )

    def a2(d):
        part = abuf.at[:, x, mine]
        return remote(part, part, a2_s.at[d - 1], a2_r.at[d - 1], x=lax.rem(x + d, nx))

    def over_y(k, d):
        part = abuf.at[:, lax.rem(x - k + nx, nx), mine]
        return remote(
            part, part, y_s.at[k, d - 1], y_r.at[k, d - 1], y=lax.rem(y + d, ny)
        )

    def sibling(k, d):
        part = abuf.at[:, lax.rem(x - k + nx, nx), 2 * lax.rem(y - d + ny, ny) + c]
        return remote(part, part, sib_s.at[k, d], sib_r.at[k, d], c=1 - c)

    near, far_x = [1, nx - 1], list(range(2, nx - 1))
    for d in near:
        c1(d, 0).start()
    for way in range(2):
        launch(ring(way, 0, 0, 0, columns(x, 0)))
    act_load.wait()
    turned = act_in[...].T
    for x2 in range(nx):
        for z2 in range(nz):
            first = (x2 * nz + z2) * strip
            act_t[z2, x2 * strip : (x2 + 1) * strip, :] = turned[first : first + strip]
    abuf[z, x, mine] = act_t[z]
    for d in range(1, nz):
        launch(a1(d))
    for way in range(2):
        launch(ring(way, 0, 0, 1, columns(x, 1)))
    for d in near:
        c1(d, 0).wait_send()
    for d in far_x:
        launch(c1(d, 0))
    for d in near + far_x:
        launch(c1(d, 1))
    for p in range(2):
        for k in near + far_x:
            c1(k, p).wait_recv()
            for way in range(2):
                launch(ring(way, 0, k, p))
    for d in range(1, nz):
        a1(d).wait_recv()
    for d in range(1, nx):
        launch(a2(d))
    for d in range(1, ny):
        launch(over_y(0, d))
    launch(sibling(0, 0))
    for copy in own_c:
        copy.wait()
    for load in loads:
        load.wait()

    def find_blocks(owner, carry):
        low, high = jnp.int32(count), jnp.int32(0)
        for b in range(count):
            hit = owners[b] == owner
            low = jnp.where(hit, jnp.minimum(low, b), low)
            high = jnp.where(hit, b, high)
        source[2 * owner] = jnp.where(low == count, 0, low)
        source[2 * owner + 1] = high
        return carry

    def find_target(b, carry):
        earlier = jnp.int32(0)
        for c2 in range(count):
            hit = jnp.logical_and(owners[c2] == owners[b], c2 < b)
            earlier = jnp.where(hit, earlier + 1, earlier)
        targets[b] = 2 * owners[b] + earlier
        return carry

    held = jnp.int32(0)
    for b in range(count):
        held = jnp.where(owners[b] == me, held + 1, held)
    for slot in range(2):
        used[slot] = jnp.where(held > slot, 1.0, 0.0)

    items = nx * (ny - 1)

    def shard(origin, p, rows=None):
        parts = []
        for x2 in range(nx):
            if rows is None:
                piece = abuf[origin, x2]
            else:
                piece = abuf[origin, x2, :, rows, :]
            parts.append(piece.reshape(-1, tokens))
        left = jnp.concatenate(parts, axis=1)
        return dot(left, cbuf[p, origin].reshape(nx * tokens, wide))

    diagonal = lax.broadcasted_iota(jnp.int32, (width, width), 0) == lax.broadcasted_iota(
        jnp.int32, (width, width), 1
    )

    def exchange(d, p):
        j = lax.rem(x + d, nx)
        return (
            remote(gsend.at[p, j], gq[p].at[x], ex_s.at[p, d - 1], ex_r.at[p, d - 1], x=j),
            remote(
                gsend_row.at[p, j], gq_row.at[p, x], exr_s.at[p, d - 1], exr_r.at[p, d - 1], x=j
            ),
        )

    def finish_columns(p):
        grad[...] = shard(z, p).reshape(grad.shape)

        def add(d, carry):
            origin = lax.rem(z + d + (d >= half).astype(jnp.int32), nz)
            grad[...] += shard(origin, p).reshape(grad.shape)
            return carry

        lax.fori_loop(1, nz - 1, add, 0)
        for k in range(nx):
            ring(0 if k < nx // 2 else 1, half - 1, k, p).wait_recv()
        far = lax.rem(z + half, nz)
        for d in [2, 1, nx - 1, 0]:
            j = lax.rem(x + d, nx)
            rows = pl.ds(pl.multiple_of(j * strip, strip), strip)
            value = grad[:, rows, :].reshape(width, wide) + shard(far, p, rows)
            top = jnp.maximum(jnp.max(jnp.abs(value), axis=1, keepdims=True), 1e-30)
            coded = jnp.round(value * (32767.0 / top)).astype(jnp.int32).astype(jnp.int16)
            row = jnp.sum(jnp.where(diagonal, top * (1.0 / 32767.0), 0.0), axis=0, keepdims=True)
            if d:
                gsend[p, j] = coded.reshape(rows_i, strip, wide)
                gsend_row[p, j] = row
                for copy in exchange(d, p):
                    copy.start()
            else:
                gq[p][x] = coded.reshape(rows_i, strip, wide)
                gq_row[p, x] = row

    def one_matrix(q, carry):
        p = (q >= 2).astype(jnp.int32)
        for u in range(6):
            t, tile = u // 2, u % 2
            n = 6 * q + u
            inner_n = n - 12 * p
            hop, place = inner_n // nx + 1, lax.rem(inner_n, nx)
            k = jnp.where(place == 2, nx - 1, jnp.where(place == 3, 2, place))
            ring(0, hop - 1, k, p).wait_recv()
            ring(1, hop - 1, k, p).wait_recv()
            inner = hop < half - 1

            @pl.when(jnp.logical_or(inner, place < nx // 2))
            def _():
                ring(0, hop, k, p).start()

            @pl.when(jnp.logical_or(inner, place >= nx // 2))
            def _():
                ring(1, hop, k, p).start()

            if u + 1 < nx:

                @pl.when(q == 0)
                def _():
                    a2(u + 1).wait_recv()
                    for d in range(1, ny):
                        over_y(u + 1, d).start()
                    sibling(u + 1, 0).start()

            item = n - 5
            if ny > 1:

                @pl.when(jnp.logical_and(item >= 0, item < items))
                def _():
                    k2, d2 = item // (ny - 1), lax.rem(item, ny - 1) + 1
                    over_y(k2, d2).wait_recv()
                    sibling(k2, d2).start()

            if u == 2:

                @pl.when(q == 3)
                def _():
                    for k3 in range(nx):
                        for d in range(ny):
                            sibling(k3, d).wait_recv()
                    finish_columns(0)

            each = -(-devices // 24)
            lax.fori_loop(n * each, jnp.minimum(n * each + each, devices), find_blocks, 0)
            each = -(-count // 24)
            lax.fori_loop(n * each, jnp.minimum(n * each + each, count), find_target, 0)

            if t == 0:
                if tile == 0:
                    stat = sbuf[q]
                    bound = jnp.max(
                        jnp.sum(jnp.abs(stat), axis=1, keepdims=True), axis=0, keepdims=True
                    )
                    value = stat * (1.0 / bound)
                    matrix[...] = value
                    m_h[...], m_l[...] = halves(value)

                def finish(rows, value):
                    m2[rows, :] = value
                    m2_h[rows, :], m2_l[rows, :] = halves(value)
                    w_h[rows, :], w_l[rows, :] = halves(
                        COEFFICIENTS[5] * matrix[rows, :] + COEFFICIENTS[6] * value
                    )

                half_product(tile, m_h, m_l, m_h, m_l, block, finish)
            elif t == 1:

                def finish(rows, value):
                    value += COEFFICIENTS[3] * matrix[rows, :] + COEFFICIENTS[4] * m2[rows, :]
                    m_h[rows, :], m_l[rows, :] = halves(value)

                half_product(tile, m2_h, m2_l, w_h, w_l, block, finish)
            else:

                def finish(rows, value):
                    value += COEFFICIENTS[1] * matrix[rows, :] + COEFFICIENTS[2] * m2[rows, :]
                    ids = lax.broadcasted_iota(jnp.int32, value.shape, 0) + rows.start
                    columns = lax.broadcasted_iota(jnp.int32, value.shape, 1)
                    value += jnp.where(ids == columns, COEFFICIENTS[0], 0.0)
                    root_h[q, rows, :], root_l[q, rows, :] = halves(value)

                half_product(tile, m2_h, m2_l, m_h, m_l, block, finish)

            each = -(-count // 24)
            for extra in range(each):
                b = n * each + extra

                @pl.when(b < count)
                def _():
                    rows = pl.ds(pl.multiple_of(b * strip, strip), strip)
                    for k in range(block // lane):
                        vt[k, rows, :] = vbuf[k, pl.ds(b, strip, stride=count), :]
        return carry

    lax.fori_loop(0, 4, one_matrix, 0)

    lanes = lax.broadcasted_iota(jnp.int32, (1, width), 1)

    def strips_of(j, p):
        row = gq_row[p, j]
        column = jnp.sum(jnp.where(diagonal, row, 0.0), axis=1, keepdims=True)
        chunks = range(p * wide // lane, (p + 1) * wide // lane)
        for i in range(rows_i):
            b = i * nx + j
            value = gq[p][j, i].astype(jnp.float32) * column[i * strip : (i + 1) * strip]
            square = value * value
            rows = pl.ds(pl.multiple_of(b * strip, strip), strip)
            old = jnp.concatenate([vt[k, rows, :] for k in chunks], axis=1)
            fresh = 0.9 * old + 0.1 * square
            for at, k in enumerate(chunks):
                vt[k, rows, :] = fresh[:, at * lane : (at + 1) * lane]
            total = jnp.sum(square / fresh, axis=0, keepdims=True)
            total = jnp.sum(total, axis=1, keepdims=True)
            inside = jnp.logical_and(lanes >= p * strip, lanes < (p + 1) * strip)
            moved = pltpu.roll(row, (p - i) * strip % width, 1)
            packed = jnp.where(inside, moved, 0.0) + jnp.where(lanes == width - 1, total, 0.0)
            if p:
                packed += scale_rows[pl.ds(b, 1), :]
            scale_rows[pl.ds(b, 1), :] = packed

    def strips_half(p):
        strips_of(x, p)
        for d in (1, nx - 1, 2):
            for copy in exchange(d, p):
                copy.wait_recv()
            strips_of(lax.rem(x - d + nx, nx), p)

    def wrapped(value, size):
        return jnp.where(value >= size, value - size, value)

    turns = [half] + [dz for step in range(1, half) for dz in (step, nz - step)]

    def others(body, sign):
        ends = {dz: wrapped(z + (dz if sign > 0 else nz - dz), nz) for dz in turns}

        def one(dx, carry):
            x2 = wrapped(x + (dx if sign > 0 else nx - dx), nx)
            for dz in turns:
                body(dx * nz + dz, x2, ends[dz])

            @pl.when(dx > 0)
            def _():
                body(dx * nz, x2, z)

            return carry

        lax.fori_loop(0, nx, one, 0)

    def go(slot, d, x2, z2):
        return remote(
            send_q.at[slot, x2 * nz + z2], rq.at[slot, me],
            go_s.at[slot, d - 1], go_r.at[slot, d - 1], x=x2, z=z2,
        )

    def go_both(d, x2, z2):
        return remote(
            send_both.at[x2 * nz + z2], rq_both.at[me],
            both_s.at[d - 1], both_r.at[d - 1], x=x2, z=z2,
        )

    def go_row(d, x2, z2):
        return remote(
            send_row.at[x2 * nz + z2], rq_row.at[me], gor_s.at[d - 1], gor_r.at[d - 1], x=x2, z=z2
        )

    def picked(slot, other, p):
        b = source[2 * other + slot]
        return gq[p][lax.rem(b, nx), b // nx]

    def picked_rows(other):
        return jnp.concatenate(
            [scale_rows[pl.ds(source[2 * other + slot], 1), :] for slot in range(2)], axis=0
        )

    strips_half(0)

    def send_first(d, x2, z2):
        other = x2 * nz + z2
        for slot in range(2):
            send_both[other, slot] = picked(slot, other, 0)
        go_both(d, x2, z2).start()

    others(send_first, 1)
    for slot in range(2):
        rq_both[me, slot] = picked(slot, me, 0)
    finish_columns(1)
    strips_half(1)
    for slot in range(2):

        def send(d, x2, z2):
            other = x2 * nz + z2
            send_q[slot, other] = picked(slot, other, 1)
            if slot == 0:
                send_row[other] = picked_rows(other)
                go_row(d, x2, z2).start()
            go(slot, d, x2, z2).start()

        others(send, 1)
        rq[slot, me] = picked(slot, me, 1)
        if slot == 0:
            rq_row[me] = picked_rows(me)

    def reorder(r, carry):
        rows = pl.ds(pl.multiple_of(r * count, count), count)
        for k in range(block // lane):
            vbuf[k, rows, :] = vt[k, pl.ds(r, count, stride=strip), :]
        return carry

    lax.fori_loop(0, strip, reorder, 0)
    outs = [
        pltpu.make_async_copy(
            vbuf.at[k], var_new.at[:, k * lane : (k + 1) * lane], var_sem.at[1, k]
        )
        for k in range(block // lane)
    ]
    for copy in outs:
        copy.start()

    def back(slot, d, x2, z2):
        rows = pl.ds(pl.multiple_of((x2 * nz + z2) * strip, strip), strip)
        return remote(
            finished.at[slot, rows, :], ret.at[2 * me + slot],
            back_s.at[slot, d - 1], back_r.at[slot, d - 1], x=x2, z=z2,
        )

    fits = [
        lax.broadcasted_iota(jnp.int32, (strip, width), 1)
        == lax.broadcasted_iota(jnp.int32, (strip, width), 0) + p * strip
        for p in range(2)
    ]
    for slot in range(2):
        keep = used[slot]

        def decode(other):
            values = []
            for p, data in enumerate((rq_both[other, slot], rq[slot, other])):
                row = rq_row[other, slot : slot + 1]
                column = jnp.sum(jnp.where(fits[p], row, 0.0), axis=1, keepdims=True) * keep
                values.append(data.astype(jnp.float32) * column)
            rows = pl.ds(pl.multiple_of(other * strip, strip), strip)
            value = jnp.concatenate(values, axis=1)
            owned_h[slot, rows, :], owned_l[slot, rows, :] = halves(value)

        def receive(d, x2, z2):
            if slot == 0:
                go_both(d, x2, z2).wait_recv()
                go_row(d, x2, z2).wait_recv()
            go(slot, d, x2, z2).wait_recv()
            decode(x2 * nz + z2)

        decode(me)
        others(receive, -1)
        total = jnp.sum(rq_row[:, slot : slot + 1, :], axis=0)
        total = jnp.where(lanes == width - 1, total, 0.0)

        def finish(rows, value):
            m_h[rows, :], m_l[rows, :] = halves(value)

        tiled_product(
            root_h.at[slot], root_l.at[slot], owned_h.at[slot], owned_l.at[slot], block, finish
        )

        def finish(rows, value):
            pre[rows, :] = value

        tiled_product(m_h, m_l, root_h.at[2 + slot], root_l.at[2 + slot], block, finish)
        value = pre[...]
        squares = jnp.sum(jnp.sum(value * value, axis=0, keepdims=True), axis=1, keepdims=True)
        mean_adam = jnp.sum(total, axis=1, keepdims=True) * (1.0 / (block * block))
        ratio = jnp.sqrt(mean_adam / (squares * (1.0 / (block * block)) + 1e-6))
        finished[slot] = (value * ratio).astype(jnp.bfloat16)

        others(lambda d, x2, z2: back(slot, d, x2, z2).start(), 1)
        rows = pl.ds(pl.multiple_of(me * strip, strip), strip)
        ret[2 * me + slot] = finished[slot, rows, :]

    tile = block // 2
    for slot in range(2):

        def outer(step, carry):
            rows = pl.ds(pl.multiple_of(step * tile, tile), tile)

            def pair(dims, left_high, left_low):
                def one(left, right):
                    return lax.dot_general(
                        left, right, (dims, ((), ())), preferred_element_type=jnp.float32
                    )

                total = one(left_high, owned_l[slot]) + one(left_low, owned_h[slot])
                return one(left_high, owned_h[slot]) + total

            left = pair(((1,), (1,)), owned_h[slot, rows, :], owned_l[slot, rows, :])
            sbuf[slot, rows, :] = 0.9 * sbuf[slot, rows, :] + 0.1 * left
            right = pair(((0,), (0,)), owned_h[slot, :, rows], owned_l[slot, :, rows])
            sbuf[2 + slot, rows, :] = 0.9 * sbuf[2 + slot, rows, :] + 0.1 * right
            return carry

        lax.fori_loop(0, 2, outer, 0)
        outs.append(pltpu.make_async_copy(sbuf.at[slot], left_new.at[slot], out_sem.at[slot]))
        outs.append(
            pltpu.make_async_copy(sbuf.at[2 + slot], right_new.at[slot], out_sem.at[2 + slot])
        )
        for copy in outs[-2:]:
            copy.start()

    for slot in range(2):
        others(lambda d, x2, z2: go(slot, d, x2, z2).wait_send(), 1)
    others(lambda d, x2, z2: go_row(d, x2, z2).wait_send(), 1)
    others(lambda d, x2, z2: go_both(d, x2, z2).wait_send(), 1)
    for p in range(2):
        for d in range(1, nx):
            for copy in exchange(d, p):
                copy.wait_send()
    for copy in sends:
        copy.wait_send()
    for p in range(2):
        for hop in range(1, half):
            for k in range(nx):
                for way in range(2):
                    if hop < half - 1 or (k < nx // 2) == (way == 0):
                        ring(way, hop, k, p).wait_send()
    for k in range(1, nx):
        for d in range(1, ny):
            over_y(k, d).wait_send()
    for k in range(nx):
        for d in range(ny):
            if (k, d) != (0, 0):
                sibling(k, d).wait_send()

    for slot in range(2):
        others(lambda d, x2, z2: back(slot, d, x2, z2).wait_recv(), -1)
        others(lambda d, x2, z2: back(slot, d, x2, z2).wait_send(), 1)

    def choose(b, carry):
        direction[b] = ret[targets[b]]
        return carry

    lax.fori_loop(0, count, choose, 0)

    for copy in outs:
        copy.wait()


def shampoo(act, cot, stats_left, stats_right, variance, owners):
    tokens = act.shape[0]
    nx, nz, ny = lax.axis_size("x"), lax.axis_size("z"), lax.axis_size("y")
    block = stats_left.shape[-1]
    strip = block // (nx * nz)
    rows_z = nx * strip
    rows_i = 2 * ny
    sizes = (nx, nz, ny, block, strip, tokens, rows_i)
    half = nz // 2
    count, devices, width = rows_i * nx, nx * nz, rows_i * strip
    lane = min(block // 2, 128)
    wide = block // 2
    bf16, f32, i16 = jnp.bfloat16, jnp.float32, jnp.int16
    sem, vmem = pltpu.SemaphoreType.DMA, pltpu.VMEM
    square = (block, block)
    anywhere = pl.BlockSpec(memory_space=pl.ANY)
    scalars = pl.BlockSpec(memory_space=pltpu.SMEM)
    return pl.pallas_call(
        functools.partial(step_kernel, sizes),
        out_shape=(
            jax.ShapeDtypeStruct((count, strip, block), bf16),
            jax.ShapeDtypeStruct(stats_left.shape, f32),
            jax.ShapeDtypeStruct(stats_right.shape, f32),
            jax.ShapeDtypeStruct(variance.shape, f32),
        ),
        in_specs=[anywhere] * 5 + [scalars],
        out_specs=(pl.BlockSpec(memory_space=pltpu.VMEM),) + (anywhere,) * 3,
        scratch_shapes=[
            vmem((tokens, block), bf16),
            vmem((nz, rows_z, tokens), bf16),
            pltpu.SMEM((2 * devices,), jnp.int32),
            pltpu.SMEM((count,), jnp.int32),
            pltpu.SMEM((2,), f32),
            vmem((2, nz, nx, tokens, wide), bf16),
            vmem((nz, nx, rows_i, rows_z, tokens), bf16),
            vmem((rows_i, rows_z, wide), f32),
            vmem((4, block, block), f32),
            vmem((block // lane, strip * count, lane), f32),
            vmem((block // lane, strip * count, lane), f32),
            vmem(square, f32),
            vmem(square, f32),
        ]
        + [vmem(square, bf16)] * 6
        + [
            vmem((4, block, block), bf16),
            vmem((4, block, block), bf16),
            vmem((2, nx, rows_i, strip, wide), i16),
            vmem((2, nx, 1, width), f32),
            vmem((nx, rows_i, strip, wide), i16),
            vmem((nx, rows_i, strip, wide), i16),
            vmem((2, nx, 1, width), f32),
            vmem((count, width), f32),
            vmem((2, devices, strip, wide), i16),
            vmem((devices, 2, strip, wide), i16),
            vmem((devices, 2, width), f32),
            vmem((2, devices, strip, wide), i16),
            vmem((devices, 2, strip, wide), i16),
            vmem((devices, 2, width), f32),
            vmem((2, block, block), bf16),
            vmem((2, block, block), bf16),
            vmem(square, f32),
            vmem((2, block, block), bf16),
            vmem((2 * devices, strip, block), bf16),
            sem((3,)), sem((4,)), sem((4,)), sem((2, block // lane)),
            sem((2, nx - 1)), sem((2, nx - 1)),
            sem((nz - 1,)), sem((nz - 1,)),
            sem((2, 2, half, nx)), sem((2, 2, half, nx)),
            sem((nx - 1,)), sem((nx - 1,)),
            sem((nx, max(1, ny - 1))), sem((nx, max(1, ny - 1))),
            sem((nx, ny)), sem((nx, ny)),
        ]
        + [sem((2, nx - 1))] * 4
        + [sem((2, devices - 1))] * 2
        + [sem((devices - 1,))] * 4
        + [sem((2, devices - 1))] * 2,
        compiler_params=pltpu.CompilerParams(
            collective_id=0, has_side_effects=True, vmem_limit_bytes=60 * 1024 * 1024
        ),
    )(act, cot, stats_left, stats_right, variance, owners)


def settle_kernel(
    left, right, variance, direction, left_out, right_out, variance_out, direction_out,
    held, held_rows, taken, spread, turned, in_sem, out_sem, way_sem,
):
    count, strip, block = direction.shape
    lane = spread.shape[2]
    pairs = [(left.at[k], held.at[k], left_out.at[k]) for k in range(2)]
    pairs += [(right.at[k], held.at[2 + k], right_out.at[k]) for k in range(2)]
    pairs += [(variance, held_rows, variance_out)]
    first = pltpu.make_async_copy(direction, taken, way_sem.at[0])
    last = pltpu.make_async_copy(turned, direction_out, way_sem.at[1])
    reads = [
        pltpu.make_async_copy(src, mid, in_sem.at[k]) for k, (src, mid, _) in enumerate(pairs)
    ]
    writes = [
        pltpu.make_async_copy(mid, dst, out_sem.at[k]) for k, (_, mid, dst) in enumerate(pairs)
    ]
    first.start()
    for copy in reads:
        copy.start()
    first.wait()
    value = taken[...].reshape(count * strip, block).astype(jnp.float32)
    for k in range(block // lane):
        spread[k] = value[:, k * lane : (k + 1) * lane]
    for r in range(strip):
        turned[r] = jnp.concatenate(
            [spread[k, pl.ds(r, count, stride=strip), :] for k in range(block // lane)], axis=1
        ).astype(turned.dtype)
    last.start()
    for read, write in zip(reads, writes):
        read.wait()
        write.start()
    for copy in writes:
        copy.wait()
    last.wait()


def settle(left, right, variance, direction):
    count, strip, block = direction.shape
    lane = min(block, 128)
    anywhere = pl.BlockSpec(memory_space=pl.ANY)
    vmem, sem = pltpu.VMEM, pltpu.SemaphoreType.DMA
    return pl.pallas_call(
        settle_kernel,
        out_shape=tuple(jax.ShapeDtypeStruct(a.shape, a.dtype) for a in (left, right, variance))
        + (jax.ShapeDtypeStruct((strip, count, block), direction.dtype),),
        in_specs=[anywhere] * 4,
        out_specs=(anywhere,) * 4,
        scratch_shapes=[
            vmem((4, block, block), left.dtype),
            vmem(variance.shape, variance.dtype),
            vmem(direction.shape, direction.dtype),
            vmem((block // lane, count * strip, lane), jnp.float32),
            vmem((strip, count, block), direction.dtype),
            sem((5,)), sem((5,)), sem((2,)),
        ],
        compiler_params=pltpu.CompilerParams(vmem_limit_bytes=60 * 1024 * 1024),
    )(left, right, variance, direction)


def per_device(activations, cotangents, owners, stats_left, stats_right, variance):
    block = activations.shape[1]
    count = owners.shape[0]
    strip = variance.shape[1]
    direction, left_new, right_new, var_new = shampoo(
        activations, cotangents, stats_left[0, 0], stats_right[0, 0],
        variance.reshape(strip * count, block), owners[:, 0],
    )
    left_new, right_new, var_new, direction = settle(left_new, right_new, var_new, direction)
    return (direction[None], left_new[None, None], right_new[None, None], var_new.reshape(variance.shape))


def solution(mesh):
    fine = Mesh(mesh.devices.reshape(X, Z, Y, 2), ("x", "z", "y", "c"))
    dp, mp = ("x", "z"), ("y", "c")

    def whole(activations, cotangents, owners, stats_left, stats_right, variance):
        return per_device(activations, cotangents, owners, stats_left, stats_right, variance)

    return jax.shard_map(
        whole,
        mesh=fine,
        in_specs=(
            P(dp, mp),
            P(dp, mp),
            P(mp, None),
            P(mp, dp, None, None, None),
            P(mp, dp, None, None, None),
            P(mp, dp, None, None),
        ),
        out_specs=(
            P(mp, dp, None, None),
            P(mp, dp, None, None, None),
            P(mp, dp, None, None, None),
            P(mp, dp, None, None),
        ),
        check_vma=False,
    )
```

```python
import functools

import jax
import jax.numpy as jnp
from jax import lax
from jax.experimental import pallas as pl
from jax.experimental.pallas import tpu as pltpu
from jax.sharding import Mesh, PartitionSpec as P

X, Z, Y = 4, 8, 4
MESH = pl.DeviceIdType.MESH
COEFFICIENTS = (
    25 / 16, -5 / 16 - 3125 / 4096, 3125 / 4096, -1250 / 4096, 250 / 4096, -25 / 4096, 1 / 4096,
)


def halves(value):
    high = value.astype(jnp.bfloat16)
    return high, (value - high.astype(jnp.float32)).astype(jnp.bfloat16)


def dot(left, right):
    return jnp.dot(left, right, preferred_element_type=jnp.float32)


def half_product(step, left_high, left_low, right_high, right_low, order, finish):
    tile = order // 2
    rows = pl.ds(step * tile, tile)
    if not isinstance(step, int):
        rows = pl.ds(pl.multiple_of(step * tile, tile), tile)
    high, low = left_high[rows, :], left_low[rows, :]
    total = dot(high, right_low[...]) + dot(low, right_high[...])
    finish(rows, dot(high, right_high[...]) + total)


def tiled_product(left_high, left_low, right_high, right_low, order, finish):
    def one(step, carry):
        half_product(step, left_high, left_low, right_high, right_low, order, finish)
        return carry

    lax.fori_loop(0, 2, one, 0)


def step_kernel(
    sizes, act, cot, stats_left, stats_right, variance, owners,
    direction, left_new, right_new, var_new,
    act_in, act_t, source, targets, used, cbuf, abuf, grad, sbuf, vbuf, vt, matrix, m2, m_h, m_l, m2_h, m2_l, w_h, w_l, root_h, root_l,
    gsend, gsend_row, gq_first, gq_second, gq_row, scale_rows, send_q, send_both, send_row, rq, rq_both,
    rq_row,
    owned_h, owned_l, pre, finished, ret,
    own_sem, stat_sem, out_sem, var_sem, c1_s, c1_r, a1_s, a1_r, zr_s, zr_r, a2_s, a2_r,
    y_s, y_r, sib_s, sib_r, ex_s, ex_r, exr_s, exr_r, go_s, go_r, both_s, both_r,
    gor_s, gor_r, back_s, back_r,
):
    nx, nz, ny, block, strip, tokens, rows_i = sizes
    count, devices, width = rows_i * nx, nx * nz, rows_i * strip
    lane = vbuf.shape[2]
    wide = block // 2
    gq = (gq_first, gq_second)
    half = nz // 2
    x, z = lax.axis_index("x"), lax.axis_index("z")
    y, c = lax.axis_index("y"), lax.axis_index("c")
    mine = 2 * y + c
    me = x * nz + z

    def remote(src, dst, send, recv, **where):
        return pltpu.make_async_remote_copy(
            src_ref=src, dst_ref=dst, send_sem=send, recv_sem=recv,
            device_id=where, device_id_type=MESH,
        )

    barrier = pltpu.get_barrier_semaphore()

    partners = [{"x": lax.rem(x + d, nx)} for d in range(1, nx)]
    partners += [{"z": lax.rem(z + d, nz)} for d in range(1, nz)]
    partners += [{"y": lax.rem(y + d, ny)} for d in range(1, ny)]
    partners += [{"c": 1 - c}]
    for partner in partners:
        pl.semaphore_signal(barrier, inc=1, device_id=partner, device_id_type=MESH)
    loads = [
        pltpu.make_async_copy(ref.at[slot], sbuf.at[2 * side + slot], stat_sem.at[2 * side + slot])
        for side, ref in enumerate((stats_left, stats_right))
        for slot in range(2)
    ]

    def columns(j, p):
        return cot.at[:, pl.ds(pl.multiple_of(j * block + p * wide, wide), wide)]

    own_c = [
        pltpu.make_async_copy(columns(x, p), cbuf.at[p, z, x], own_sem.at[2 * p]) for p in range(2)
    ]
    act_load = pltpu.make_async_copy(act, act_in, own_sem.at[1])
    loads += [
        pltpu.make_async_copy(
            variance.at[:, k * lane : (k + 1) * lane], vbuf.at[k], var_sem.at[0, k]
        )
        for k in range(block // lane)
    ]
    act_load.start()
    for copy in own_c:
        copy.start()
    for load in loads:
        load.start()

    pl.semaphore_wait(barrier, len(partners))

    sends = []

    def launch(copy):
        copy.start()
        sends.append(copy)

    def c1(d, p):
        j = lax.rem(x + d, nx)
        return remote(
            columns(j, p), cbuf.at[p, z, x], c1_s.at[p, d - 1], c1_r.at[p, d - 1], x=j
        )

    def a1(d):
        z2 = lax.rem(z + d, nz)
        return remote(act_t.at[z2], abuf.at[z, x, mine], a1_s.at[d - 1], a1_r.at[d - 1], z=z2)

    def ring(way, hop, k, p, held=None):
        x2 = lax.rem(x - k + nx, nx)
        step = 1 if way == 0 else nz - 1
        origin = lax.rem(z - hop + nz, nz) if way == 0 else lax.rem(z + hop, nz)
        part = cbuf.at[p, origin, x2]
        return remote(
            part if held is None else held, part, zr_s.at[p, way, hop, k], zr_r.at[p, way, hop, k], z=lax.rem(z + step, nz)
        )

    def a2(d):
        part = abuf.at[:, x, mine]
        return remote(part, part, a2_s.at[d - 1], a2_r.at[d - 1], x=lax.rem(x + d, nx))

    def over_y(k, d):
        part = abuf.at[:, lax.rem(x - k + nx, nx), mine]
        return remote(
            part, part, y_s.at[k, d - 1], y_r.at[k, d - 1], y=lax.rem(y + d, ny)
        )

    def sibling(k, d):
        part = abuf.at[:, lax.rem(x - k + nx, nx), 2 * lax.rem(y - d + ny, ny) + c]
        return remote(part, part, sib_s.at[k, d], sib_r.at[k, d], c=1 - c)

    near, far_x = [1, nx - 1], list(range(2, nx - 1))
    for d in near:
        c1(d, 0).start()
    for way in range(2):
        launch(ring(way, 0, 0, 0, columns(x, 0)))
    act_load.wait()
    turned = act_in[...].T
    for x2 in range(nx):
        for z2 in range(nz):
            first = (x2 * nz + z2) * strip
            act_t[z2, x2 * strip : (x2 + 1) * strip, :] = turned[first : first + strip]
    abuf[z, x, mine] = act_t[z]
    for d in range(1, nz):
        launch(a1(d))
    for way in range(2):
        launch(ring(way, 0, 0, 1, columns(x, 1)))
    for d in near:
        c1(d, 0).wait_send()
    for d in far_x:
        launch(c1(d, 0))
    for d in near + far_x:
        launch(c1(d, 1))
    for p in range(2):
        for k in near + far_x:
            c1(k, p).wait_recv()
            for way in range(2):
                launch(ring(way, 0, k, p))
    for d in range(1, nz):
        a1(d).wait_recv()
    for d in range(1, nx):
        launch(a2(d))
    for d in range(1, ny):
        launch(over_y(0, d))
    launch(sibling(0, 0))
    for copy in own_c:
        copy.wait()
    for load in loads:
        load.wait()

    def find_blocks(owner, carry):
        low, high = jnp.int32(count), jnp.int32(0)
        for b in range(count):
            hit = owners[b] == owner
            low = jnp.where(hit, jnp.minimum(low, b), low)
            high = jnp.where(hit, b, high)
        source[2 * owner] = jnp.where(low == count, 0, low)
        source[2 * owner + 1] = high
        return carry

    def find_target(b, carry):
        earlier = jnp.int32(0)
        for c2 in range(count):
            hit = jnp.logical_and(owners[c2] == owners[b], c2 < b)
            earlier = jnp.where(hit, earlier + 1, earlier)
        targets[b] = 2 * owners[b] + earlier
        return carry

    held = jnp.int32(0)
    for b in range(count):
        held = jnp.where(owners[b] == me, held + 1, held)
    for slot in range(2):
        used[slot] = jnp.where(held > slot, 1.0, 0.0)

    items = nx * (ny - 1)

    def shard(origin, p, rows=None):
        parts = []
        for x2 in range(nx):
            if rows is None:
                piece = abuf[origin, x2]
            else:
                piece = abuf[origin, x2, :, rows, :]
            parts.append(piece.reshape(-1, tokens))
        left = jnp.concatenate(parts, axis=1)
        return dot(left, cbuf[p, origin].reshape(nx * tokens, wide))

    diagonal = lax.broadcasted_iota(jnp.int32, (width, width), 0) == lax.broadcasted_iota(
        jnp.int32, (width, width), 1
    )

    def exchange(d, p):
        j = lax.rem(x + d, nx)
        return (
            remote(gsend.at[p, j], gq[p].at[x], ex_s.at[p, d - 1], ex_r.at[p, d - 1], x=j),
            remote(
                gsend_row.at[p, j], gq_row.at[p, x], exr_s.at[p, d - 1], exr_r.at[p, d - 1], x=j
            ),
        )

    def finish_columns(p):
        grad[...] = shard(z, p).reshape(grad.shape)

        def add(d, carry):
            origin = lax.rem(z + d + (d >= half).astype(jnp.int32), nz)
            grad[...] += shard(origin, p).reshape(grad.shape)
            return carry

        lax.fori_loop(1, nz - 1, add, 0)
        for k in range(nx):
            ring(0 if k < nx // 2 else 1, half - 1, k, p).wait_recv()
        far = lax.rem(z + half, nz)
        for d in [2, 1, nx - 1, 0]:
            j = lax.rem(x + d, nx)
            rows = pl.ds(pl.multiple_of(j * strip, strip), strip)
            value = grad[:, rows, :].reshape(width, wide) + shard(far, p, rows)
            top = jnp.maximum(jnp.max(jnp.abs(value), axis=1, keepdims=True), 1e-30)
            coded = jnp.round(value * (32767.0 / top)).astype(jnp.int32).astype(jnp.int16)
            row = jnp.sum(jnp.where(diagonal, top * (1.0 / 32767.0), 0.0), axis=0, keepdims=True)
            if d:
                gsend[p, j] = coded.reshape(rows_i, strip, wide)
                gsend_row[p, j] = row
                for copy in exchange(d, p):
                    copy.start()
            else:
                gq[p][x] = coded.reshape(rows_i, strip, wide)
                gq_row[p, x] = row

    def one_matrix(q, carry):
        p = (q >= 2).astype(jnp.int32)
        for u in range(6):
            t, tile = u // 2, u % 2
            n = 6 * q + u
            inner_n = n - 12 * p
            hop, place = inner_n // nx + 1, lax.rem(inner_n, nx)
            k = jnp.where(place == 2, nx - 1, jnp.where(place == 3, 2, place))
            ring(0, hop - 1, k, p).wait_recv()
            ring(1, hop - 1, k, p).wait_recv()
            inner = hop < half - 1

            @pl.when(jnp.logical_or(inner, place < nx // 2))
            def _():
                ring(0, hop, k, p).start()

            @pl.when(jnp.logical_or(inner, place >= nx // 2))
            def _():
                ring(1, hop, k, p).start()

            if u + 1 < nx:

                @pl.when(q == 0)
                def _():
                    a2(u + 1).wait_recv()
                    for d in range(1, ny):
                        over_y(u + 1, d).start()
                    sibling(u + 1, 0).start()

            item = n - 5
            if ny > 1:

                @pl.when(jnp.logical_and(item >= 0, item < items))
                def _():
                    k2, d2 = item // (ny - 1), lax.rem(item, ny - 1) + 1
                    over_y(k2, d2).wait_recv()
                    sibling(k2, d2).start()

            if u == 2:

                @pl.when(q == 3)
                def _():
                    for k3 in range(nx):
                        for d in range(ny):
                            sibling(k3, d).wait_recv()
                    finish_columns(0)

            each = -(-devices // 24)
            lax.fori_loop(n * each, jnp.minimum(n * each + each, devices), find_blocks, 0)
            each = -(-count // 24)
            lax.fori_loop(n * each, jnp.minimum(n * each + each, count), find_target, 0)

            if t == 0:
                if tile == 0:
                    stat = sbuf[q]
                    bound = jnp.max(
                        jnp.sum(jnp.abs(stat), axis=1, keepdims=True), axis=0, keepdims=True
                    )
                    value = stat * (1.0 / bound)
                    matrix[...] = value
                    m_h[...], m_l[...] = halves(value)

                def finish(rows, value):
                    m2[rows, :] = value
                    m2_h[rows, :], m2_l[rows, :] = halves(value)
                    w_h[rows, :], w_l[rows, :] = halves(
                        COEFFICIENTS[5] * matrix[rows, :] + COEFFICIENTS[6] * value
                    )

                half_product(tile, m_h, m_l, m_h, m_l, block, finish)
            elif t == 1:

                def finish(rows, value):
                    value += COEFFICIENTS[3] * matrix[rows, :] + COEFFICIENTS[4] * m2[rows, :]
                    m_h[rows, :], m_l[rows, :] = halves(value)

                half_product(tile, m2_h, m2_l, w_h, w_l, block, finish)
            else:

                def finish(rows, value):
                    value += COEFFICIENTS[1] * matrix[rows, :] + COEFFICIENTS[2] * m2[rows, :]
                    ids = lax.broadcasted_iota(jnp.int32, value.shape, 0) + rows.start
                    columns = lax.broadcasted_iota(jnp.int32, value.shape, 1)
                    value += jnp.where(ids == columns, COEFFICIENTS[0], 0.0)
                    root_h[q, rows, :], root_l[q, rows, :] = halves(value)

                half_product(tile, m2_h, m2_l, m_h, m_l, block, finish)

            each = -(-count // 24)
            for extra in range(each):
                b = n * each + extra

                @pl.when(b < count)
                def _():
                    rows = pl.ds(pl.multiple_of(b * strip, strip), strip)
                    for k in range(block // lane):
                        vt[k, rows, :] = vbuf[k, pl.ds(b, strip, stride=count), :]
        return carry

    lax.fori_loop(0, 4, one_matrix, 0)

    lanes = lax.broadcasted_iota(jnp.int32, (1, width), 1)

    def strips_of(j, p):
        row = gq_row[p, j]
        column = jnp.sum(jnp.where(diagonal, row, 0.0), axis=1, keepdims=True)
        chunks = range(p * wide // lane, (p + 1) * wide // lane)
        for i in range(rows_i):
            b = i * nx + j
            value = gq[p][j, i].astype(jnp.float32) * column[i * strip : (i + 1) * strip]
            square = value * value
            rows = pl.ds(pl.multiple_of(b * strip, strip), strip)
            old = jnp.concatenate([vt[k, rows, :] for k in chunks], axis=1)
            fresh = 0.9 * old + 0.1 * square
            for at, k in enumerate(chunks):
                vt[k, rows, :] = fresh[:, at * lane : (at + 1) * lane]
            total = jnp.sum(square / fresh, axis=0, keepdims=True)
            total = jnp.sum(total, axis=1, keepdims=True)
            inside = jnp.logical_and(lanes >= p * strip, lanes < (p + 1) * strip)
            moved = pltpu.roll(row, (p - i) * strip % width, 1)
            packed = jnp.where(inside, moved, 0.0) + jnp.where(lanes == width - 1, total, 0.0)
            if p:
                packed += scale_rows[pl.ds(b, 1), :]
            scale_rows[pl.ds(b, 1), :] = packed

    def strips_half(p):
        strips_of(x, p)
        for d in (1, nx - 1, 2):
            for copy in exchange(d, p):
                copy.wait_recv()
            strips_of(lax.rem(x - d + nx, nx), p)

    def wrapped(value, size):
        return jnp.where(value >= size, value - size, value)

    turns = [half] + [dz for step in range(1, half) for dz in (step, nz - step)]

    def others(body, sign):
        ends = {dz: wrapped(z + (dz if sign > 0 else nz - dz), nz) for dz in turns}

        def one(dx, carry):
            x2 = wrapped(x + (dx if sign > 0 else nx - dx), nx)
            for dz in turns:
                body(dx * nz + dz, x2, ends[dz])

            @pl.when(dx > 0)
            def _():
                body(dx * nz, x2, z)

            return carry

        lax.fori_loop(0, nx, one, 0)

    def go(slot, d, x2, z2):
        return remote(
            send_q.at[slot, x2 * nz + z2], rq.at[slot, me],
            go_s.at[slot, d - 1], go_r.at[slot, d - 1], x=x2, z=z2,
        )

    def go_both(d, x2, z2):
        return remote(
            send_both.at[x2 * nz + z2], rq_both.at[me],
            both_s.at[d - 1], both_r.at[d - 1], x=x2, z=z2,
        )

    def go_row(d, x2, z2):
        return remote(
            send_row.at[x2 * nz + z2], rq_row.at[me], gor_s.at[d - 1], gor_r.at[d - 1], x=x2, z=z2
        )

    def picked(slot, other, p):
        b = source[2 * other + slot]
        return gq[p][lax.rem(b, nx), b // nx]

    def picked_rows(other):
        return jnp.concatenate(
            [scale_rows[pl.ds(source[2 * other + slot], 1), :] for slot in range(2)], axis=0
        )

    strips_half(0)

    def send_first(d, x2, z2):
        other = x2 * nz + z2
        for slot in range(2):
            send_both[other, slot] = picked(slot, other, 0)
        go_both(d, x2, z2).start()

    others(send_first, 1)
    for slot in range(2):
        rq_both[me, slot] = picked(slot, me, 0)
    finish_columns(1)
    strips_half(1)
    for slot in range(2):

        def send(d, x2, z2):
            other = x2 * nz + z2
            send_q[slot, other] = picked(slot, other, 1)
            if slot == 0:
                send_row[other] = picked_rows(other)
                go_row(d, x2, z2).start()
            go(slot, d, x2, z2).start()

        others(send, 1)
        rq[slot, me] = picked(slot, me, 1)
        if slot == 0:
            rq_row[me] = picked_rows(me)

    def reorder(r, carry):
        rows = pl.ds(pl.multiple_of(r * count, count), count)
        for k in range(block // lane):
            vbuf[k, rows, :] = vt[k, pl.ds(r, count, stride=strip), :]
        return carry

    lax.fori_loop(0, strip, reorder, 0)
    outs = [
        pltpu.make_async_copy(
            vbuf.at[k], var_new.at[:, k * lane : (k + 1) * lane], var_sem.at[1, k]
        )
        for k in range(block // lane)
    ]
    for copy in outs:
        copy.start()

    def back(slot, d, x2, z2):
        rows = pl.ds(pl.multiple_of((x2 * nz + z2) * strip, strip), strip)
        return remote(
            finished.at[slot, rows, :], ret.at[2 * me + slot],
            back_s.at[slot, d - 1], back_r.at[slot, d - 1], x=x2, z=z2,
        )

    fits = [
        lax.broadcasted_iota(jnp.int32, (strip, width), 1)
        == lax.broadcasted_iota(jnp.int32, (strip, width), 0) + p * strip
        for p in range(2)
    ]
    for slot in range(2):
        keep = used[slot]

        def decode(other):
            values = []
            for p, data in enumerate((rq_both[other, slot], rq[slot, other])):
                row = rq_row[other, slot : slot + 1]
                column = jnp.sum(jnp.where(fits[p], row, 0.0), axis=1, keepdims=True) * keep
                values.append(data.astype(jnp.float32) * column)
            rows = pl.ds(pl.multiple_of(other * strip, strip), strip)
            value = jnp.concatenate(values, axis=1)
            owned_h[slot, rows, :], owned_l[slot, rows, :] = halves(value)

        def receive(d, x2, z2):
            if slot == 0:
                go_both(d, x2, z2).wait_recv()
                go_row(d, x2, z2).wait_recv()
            go(slot, d, x2, z2).wait_recv()
            decode(x2 * nz + z2)

        decode(me)
        others(receive, -1)
        total = jnp.sum(rq_row[:, slot : slot + 1, :], axis=0)
        total = jnp.where(lanes == width - 1, total, 0.0)

        def finish(rows, value):
            m_h[rows, :], m_l[rows, :] = halves(value)

        tiled_product(
            root_h.at[slot], root_l.at[slot], owned_h.at[slot], owned_l.at[slot], block, finish
        )

        def finish(rows, value):
            pre[rows, :] = value

        tiled_product(m_h, m_l, root_h.at[2 + slot], root_l.at[2 + slot], block, finish)
        value = pre[...]
        squares = jnp.sum(jnp.sum(value * value, axis=0, keepdims=True), axis=1, keepdims=True)
        mean_adam = jnp.sum(total, axis=1, keepdims=True) * (1.0 / (block * block))
        ratio = jnp.sqrt(mean_adam / (squares * (1.0 / (block * block)) + 1e-6))
        finished[slot] = (value * ratio).astype(jnp.bfloat16)

        others(lambda d, x2, z2: back(slot, d, x2, z2).start(), 1)
        rows = pl.ds(pl.multiple_of(me * strip, strip), strip)
        ret[2 * me + slot] = finished[slot, rows, :]

    tile = block // 2
    for slot in range(2):

        def outer(step, carry):
            rows = pl.ds(pl.multiple_of(step * tile, tile), tile)

            def pair(dims, left_high, left_low):
                def one(left, right):
                    return lax.dot_general(
                        left, right, (dims, ((), ())), preferred_element_type=jnp.float32
                    )

                total = one(left_high, owned_l[slot]) + one(left_low, owned_h[slot])
                return one(left_high, owned_h[slot]) + total

            left = pair(((1,), (1,)), owned_h[slot, rows, :], owned_l[slot, rows, :])
            sbuf[slot, rows, :] = 0.9 * sbuf[slot, rows, :] + 0.1 * left
            right = pair(((0,), (0,)), owned_h[slot, :, rows], owned_l[slot, :, rows])
            sbuf[2 + slot, rows, :] = 0.9 * sbuf[2 + slot, rows, :] + 0.1 * right
            return carry

        lax.fori_loop(0, 2, outer, 0)
        outs.append(pltpu.make_async_copy(sbuf.at[slot], left_new.at[slot], out_sem.at[slot]))
        outs.append(
            pltpu.make_async_copy(sbuf.at[2 + slot], right_new.at[slot], out_sem.at[2 + slot])
        )
        for copy in outs[-2:]:
            copy.start()

    for slot in range(2):
        others(lambda d, x2, z2: go(slot, d, x2, z2).wait_send(), 1)
    others(lambda d, x2, z2: go_row(d, x2, z2).wait_send(), 1)
    others(lambda d, x2, z2: go_both(d, x2, z2).wait_send(), 1)
    for p in range(2):
        for d in range(1, nx):
            for copy in exchange(d, p):
                copy.wait_send()
    for copy in sends:
        copy.wait_send()
    for p in range(2):
        for hop in range(1, half):
            for k in range(nx):
                for way in range(2):
                    if hop < half - 1 or (k < nx // 2) == (way == 0):
                        ring(way, hop, k, p).wait_send()
    for k in range(1, nx):
        for d in range(1, ny):
            over_y(k, d).wait_send()
    for k in range(nx):
        for d in range(ny):
            if (k, d) != (0, 0):
                sibling(k, d).wait_send()

    for slot in range(2):
        others(lambda d, x2, z2: back(slot, d, x2, z2).wait_recv(), -1)
        others(lambda d, x2, z2: back(slot, d, x2, z2).wait_send(), 1)

    def choose(b, carry):
        direction[b] = ret[targets[b]]
        return carry

    lax.fori_loop(0, count, choose, 0)

    for copy in outs:
        copy.wait()


def shampoo(act, cot, stats_left, stats_right, variance, owners):
    tokens = act.shape[0]
    nx, nz, ny = lax.axis_size("x"), lax.axis_size("z"), lax.axis_size("y")
    block = stats_left.shape[-1]
    strip = block // (nx * nz)
    rows_z = nx * strip
    rows_i = 2 * ny
    sizes = (nx, nz, ny, block, strip, tokens, rows_i)
    half = nz // 2
    count, devices, width = rows_i * nx, nx * nz, rows_i * strip
    lane = min(block // 2, 128)
    wide = block // 2
    bf16, f32, i16 = jnp.bfloat16, jnp.float32, jnp.int16
    sem, vmem = pltpu.SemaphoreType.DMA, pltpu.VMEM
    square = (block, block)
    anywhere = pl.BlockSpec(memory_space=pl.ANY)
    scalars = pl.BlockSpec(memory_space=pltpu.SMEM)
    return pl.pallas_call(
        functools.partial(step_kernel, sizes),
        out_shape=(
            jax.ShapeDtypeStruct((count, strip, block), bf16),
            jax.ShapeDtypeStruct(stats_left.shape, f32),
            jax.ShapeDtypeStruct(stats_right.shape, f32),
            jax.ShapeDtypeStruct(variance.shape, f32),
        ),
        in_specs=[anywhere] * 5 + [scalars],
        out_specs=(pl.BlockSpec(memory_space=pltpu.VMEM),) + (anywhere,) * 3,
        scratch_shapes=[
            vmem((tokens, block), bf16),
            vmem((nz, rows_z, tokens), bf16),
            pltpu.SMEM((2 * devices,), jnp.int32),
            pltpu.SMEM((count,), jnp.int32),
            pltpu.SMEM((2,), f32),
            vmem((2, nz, nx, tokens, wide), bf16),
            vmem((nz, nx, rows_i, rows_z, tokens), bf16),
            vmem((rows_i, rows_z, wide), f32),
            vmem((4, block, block), f32),
            vmem((block // lane, strip * count, lane), f32),
            vmem((block // lane, strip * count, lane), f32),
            vmem(square, f32),
            vmem(square, f32),
        ]
        + [vmem(square, bf16)] * 6
        + [
            vmem((4, block, block), bf16),
            vmem((4, block, block), bf16),
            vmem((2, nx, rows_i, strip, wide), i16),
            vmem((2, nx, 1, width), f32),
            vmem((nx, rows_i, strip, wide), i16),
            vmem((nx, rows_i, strip, wide), i16),
            vmem((2, nx, 1, width), f32),
            vmem((count, width), f32),
            vmem((2, devices, strip, wide), i16),
            vmem((devices, 2, strip, wide), i16),
            vmem((devices, 2, width), f32),
            vmem((2, devices, strip, wide), i16),
            vmem((devices, 2, strip, wide), i16),
            vmem((devices, 2, width), f32),
            vmem((2, block, block), bf16),
            vmem((2, block, block), bf16),
            vmem(square, f32),
            vmem((2, block, block), bf16),
            vmem((2 * devices, strip, block), bf16),
            sem((3,)), sem((4,)), sem((4,)), sem((2, block // lane)),
            sem((2, nx - 1)), sem((2, nx - 1)),
            sem((nz - 1,)), sem((nz - 1,)),
            sem((2, 2, half, nx)), sem((2, 2, half, nx)),
            sem((nx - 1,)), sem((nx - 1,)),
            sem((nx, max(1, ny - 1))), sem((nx, max(1, ny - 1))),
            sem((nx, ny)), sem((nx, ny)),
        ]
        + [sem((2, nx - 1))] * 4
        + [sem((2, devices - 1))] * 2
        + [sem((devices - 1,))] * 4
        + [sem((2, devices - 1))] * 2,
        compiler_params=pltpu.CompilerParams(
            collective_id=0, has_side_effects=True, vmem_limit_bytes=60 * 1024 * 1024
        ),
    )(act, cot, stats_left, stats_right, variance, owners)


def settle_kernel(
    left, right, variance, direction, left_out, right_out, variance_out, direction_out,
    held, held_rows, taken, spread, turned, in_sem, out_sem, way_sem,
):
    count, strip, block = direction.shape
    lane = spread.shape[2]
    pairs = [(left.at[k], held.at[k], left_out.at[k]) for k in range(2)]
    pairs += [(right.at[k], held.at[2 + k], right_out.at[k]) for k in range(2)]
    pairs += [(variance, held_rows, variance_out)]
    first = pltpu.make_async_copy(direction, taken, way_sem.at[0])
    last = pltpu.make_async_copy(turned, direction_out, way_sem.at[1])
    reads = [
        pltpu.make_async_copy(src, mid, in_sem.at[k]) for k, (src, mid, _) in enumerate(pairs)
    ]
    writes = [
        pltpu.make_async_copy(mid, dst, out_sem.at[k]) for k, (_, mid, dst) in enumerate(pairs)
    ]
    first.start()
    for copy in reads:
        copy.start()
    for read, write in zip(reads[:2], writes[:2]):
        read.wait()
        write.start()
    first.wait()
    value = taken[...].reshape(count * strip, block).astype(jnp.float32)
    for k in range(block // lane):
        spread[k] = value[:, k * lane : (k + 1) * lane]
    for r in range(strip):
        turned[r] = jnp.concatenate(
            [spread[k, pl.ds(r, count, stride=strip), :] for k in range(block // lane)], axis=1
        ).astype(turned.dtype)
    last.start()
    for read, write in zip(reads[2:], writes[2:]):
        read.wait()
        write.start()
    for copy in writes:
        copy.wait()
    last.wait()


def settle(left, right, variance, direction):
    count, strip, block = direction.shape
    lane = min(block, 128)
    anywhere = pl.BlockSpec(memory_space=pl.ANY)
    vmem, sem = pltpu.VMEM, pltpu.SemaphoreType.DMA
    return pl.pallas_call(
        settle_kernel,
        out_shape=tuple(jax.ShapeDtypeStruct(a.shape, a.dtype) for a in (left, right, variance))
        + (jax.ShapeDtypeStruct((strip, count, block), direction.dtype),),
        in_specs=[anywhere] * 4,
        out_specs=(anywhere,) * 4,
        scratch_shapes=[
            vmem((4, block, block), left.dtype),
            vmem(variance.shape, variance.dtype),
            vmem(direction.shape, direction.dtype),
            vmem((block // lane, count * strip, lane), jnp.float32),
            vmem((strip, count, block), direction.dtype),
            sem((5,)), sem((5,)), sem((2,)),
        ],
        compiler_params=pltpu.CompilerParams(vmem_limit_bytes=60 * 1024 * 1024),
    )(left, right, variance, direction)


def per_device(activations, cotangents, owners, stats_left, stats_right, variance):
    block = activations.shape[1]
    count = owners.shape[0]
    strip = variance.shape[1]
    direction, left_new, right_new, var_new = shampoo(
        activations, cotangents, stats_left[0, 0], stats_right[0, 0],
        variance.reshape(strip * count, block), owners[:, 0],
    )
    left_new, right_new, var_new, direction = settle(left_new, right_new, var_new, direction)
    return (direction[None], left_new[None, None], right_new[None, None], var_new.reshape(variance.shape))


def solution(mesh):
    fine = Mesh(mesh.devices.reshape(X, Z, Y, 2), ("x", "z", "y", "c"))
    dp, mp = ("x", "z"), ("y", "c")

    def whole(activations, cotangents, owners, stats_left, stats_right, variance):
        return per_device(activations, cotangents, owners, stats_left, stats_right, variance)

    return jax.shard_map(
        whole,
        mesh=fine,
        in_specs=(
            P(dp, mp),
            P(dp, mp),
            P(mp, None),
            P(mp, dp, None, None, None),
            P(mp, dp, None, None, None),
            P(mp, dp, None, None),
        ),
        out_specs=(
            P(mp, dp, None, None),
            P(mp, dp, None, None, None),
            P(mp, dp, None, None, None),
            P(mp, dp, None, None),
        ),
        check_vma=False,
    )
```
